32 devices in a mesh: dev: 32 (over z, y, x, core).
Axes of the slice: x: 2, y: 2, z: 4, core: 2. Of those that a mesh axis runs over, the one named last changes fastest.
Arguments:
- tile_lists: int32 [768, 512], P('dev'), may hold values from -1 to 2047, as said below
- send_rows: int32 [32, 2048], P('dev'), may hold values from -1 to 2047, as said below
- centres: float32 [2, 65536], P(None, 'dev'), may hold values from -12 to 12
- conic: float32 [2, 65536], P(None, 'dev'), may hold values from 0.015625 to 0.25
- rho: float32 [1, 65536], P(None, 'dev'), may hold values from -0.6 to 0.6
- opacity: float32 [1, 65536], P(None, 'dev'), may hold values from 0.002 to 0.03
- colors: float32 [3, 65536], P(None, 'dev'), may hold values from 0 to 1
- target: float32 [3, 512, 384], P(None, 'dev'), may hold values from 0 to 1
Outputs:
- rendered: float32 [3, 512, 384], P(None, 'dev')
- grads: float32 [9, 65536], P(None, 'dev')
The draws below stay inside these ranges and needn't reach their ends.
Inputs may be any that keep to these rules, and one draw needn't show every extreme that they name: `tile_lists`: row t belongs to strip t // 24. An entry is -1 only after all live entries of its row; a live entry s * 64 + m names a slot m that owner s fills for that strip. Some row has no -1. `send_rows`: entry [s, r * 64 + m] is the local index on owner s of the Gaussian in slot m for strip r, or -1 for an unused slot. The used slots of an owner and strip come first, are distinct, and number at least 32; some owner fills all 64 slots for some strip.
All inputs are finite; a program needn't handle non-finite values.
Results may differ from the reference program's by a relative error of at most 0.0003.
Values sent between devices are 32-bit elements; how exact they have to be, the bound alone decides.
No kernel may reach another device: no remote copies, remote signals or barrier semaphores. Data moves between devices by JAX's collectives and lax.ppermute only.
A program may use at most 256 MiB of HBM per device.

```python
import math
import jax
import jax.numpy as jnp
from jax import lax

TILE = 16
LIST = 512
TILES_DEV = 24
G_DEV = 2048
CAP = 64
TILES = 768
HEIGHT = 512
WIDTH = 384
GAUSSIANS = 65536
N_DEV = 32


def shared_tables(key):
    keys = jax.random.split(jax.random.fold_in(key, 7), 8)
    used = jax.random.randint(keys[0], (N_DEV, N_DEV), CAP // 2, CAP + 1)
    chosen = jax.random.randint(keys[1], (2,), 0, N_DEV)
    used = used.at[chosen[0], chosen[1]].set(CAP)
    offset = jax.random.randint(keys[2], (N_DEV, N_DEV), 0, G_DEV)
    position = jnp.arange(CAP)
    rows = jnp.where(position[None, None, :] < used[:, :, None], (offset[:, :, None] + position[None, None, :]) % G_DEV, -1)
    send_table = rows.reshape(N_DEV, N_DEV * CAP).astype(jnp.int32)
    levels = jnp.array([1, 2, 4, 8], jnp.int32)
    weight = levels[jax.random.randint(keys[3], (N_DEV,), 0, 4)]
    strip_of = jnp.arange(TILES) // TILES_DEV
    tile_weight = weight[strip_of]
    lowest = LIST * tile_weight // 16
    highest = LIST * tile_weight // 8 + 1
    length = jax.random.randint(keys[4], (TILES,), lowest, highest)
    longest = jax.random.randint(keys[5], (), 0, TILES)
    length = length.at[longest].set(LIST)
    source = jax.random.randint(keys[6], (TILES, LIST), 0, N_DEV)
    room = used[source, strip_of[:, None]]
    within = jax.random.randint(keys[7], (TILES, LIST), 0, room)
    place = jnp.arange(LIST)
    lists = jnp.where(place[None, :] < length[:, None], source * CAP + within, -1).astype(jnp.int32)
    return (lists, send_table)


def draw_tile_lists(key, part):
    return shared_tables(key)[0]


def draw_send_rows(key, part):
    return shared_tables(key)[1]


def shard_levels(own_key, shape, shards, low, high):
    def one(dim, parts):
        heights = jax.random.uniform(jax.random.fold_in(jax.random.fold_in(own_key, 6), dim), (parts,), jnp.float32, low / len(shards), high / len(shards))
        return jnp.repeat(jnp.exp(heights), shape[dim] // parts).reshape((-1,) + (1,) * (len(shape) - dim - 1))

    loudness = one(*shards[0])
    for cut in shards[1:]:
        loudness = loudness * one(*cut)
    return loudness


def setup_inputs(seed: int = 0) -> dict:
    arg_keys = jax.random.split(jax.random.key(seed), 9)
    tile_lists = draw_tile_lists(jax.random.fold_in(arg_keys[8], 71), 0)
    send_rows = draw_send_rows(jax.random.fold_in(arg_keys[8], 71), 0)
    centres = jnp.clip(jax.random.uniform(arg_keys[2], (2, GAUSSIANS), jnp.float32, -12.0, 12.0) * shard_levels(arg_keys[2], (2, GAUSSIANS), ((1, 32),), -0.4, 0.0), -12.0, 12.0)
    conic = jnp.clip(jnp.exp(math.log(0.25) - 2.7725887 * jax.random.uniform(arg_keys[3], (2, GAUSSIANS), jnp.float32) ** shard_levels(arg_keys[3], (2, GAUSSIANS), ((1, 32),), -0.2, 0.2)), 0.015625, 0.25)
    rho = jnp.clip(jax.random.uniform(arg_keys[4], (1, GAUSSIANS), jnp.float32, -0.6, 0.6) * shard_levels(arg_keys[4], (1, GAUSSIANS), ((1, 32),), -0.4, 0.0), -0.6, 0.6)
    opacity = jnp.clip(jnp.exp(math.log(0.03) - 2.70805 * jax.random.uniform(arg_keys[5], (1, GAUSSIANS), jnp.float32) ** shard_levels(arg_keys[5], (1, GAUSSIANS), ((1, 32),), -0.2, 0.2)), 0.002, 0.03)
    colors = jnp.clip(1.0 * jax.random.uniform(arg_keys[6], (3, GAUSSIANS), jnp.float32) ** shard_levels(arg_keys[6], (3, GAUSSIANS), ((1, 32),), -0.2, 0.2), 0.0, 1.0)
    target = jnp.clip(1.0 * jax.random.uniform(arg_keys[7], (3, HEIGHT, WIDTH), jnp.float32) ** shard_levels(arg_keys[7], (3, HEIGHT, WIDTH), ((1, 32),), -0.2, 0.2), 0.0, 1.0)
    return {"tile_lists": tile_lists, "send_rows": send_rows, "centres": centres, "conic": conic, "rho": rho, "opacity": opacity, "colors": colors, "target": target}


def filter_taps():
    offsets = jnp.arange(11).astype(jnp.float32) - 5.0
    taps = jnp.exp(-offsets * offsets / 4.5)
    return taps / jnp.sum(taps)

def blur_strip(values):
    taps = filter_taps()
    count = values.shape[1] - 10
    width = values.shape[2]
    rows_done = taps[0] * values[:, 0:count]
    for shift in range(1, 11):
        rows_done = rows_done + taps[shift] * values[:, shift:shift + count]
    padded = jnp.pad(rows_done, ((0, 0), (0, 0), (5, 5)))
    result = taps[0] * padded[:, :, 0:width]
    for shift in range(1, 11):
        result = result + taps[shift] * padded[:, :, shift:shift + width]
    return result

def local_loss(render_pad, target_pad):
    mean_r = blur_strip(render_pad)
    mean_t = blur_strip(target_pad)
    var_r = blur_strip(render_pad * render_pad) - mean_r * mean_r
    var_t = blur_strip(target_pad * target_pad) - mean_t * mean_t
    covar = blur_strip(render_pad * target_pad) - mean_r * mean_t
    ssim = (2.0 * mean_r * mean_t + 0.0001) * (2.0 * covar + 0.0009) / ((mean_r * mean_r + mean_t * mean_t + 0.0001) * (var_r + var_t + 0.0009))
    centre_r = render_pad[:, 5:-5]
    centre_t = target_pad[:, 5:-5]
    diff = centre_r - centre_t
    return jnp.sum(0.8 * diff * diff + 0.2 * (1.0 - ssim))

def composite(params, live, tile):
    count = tile * tile
    pixel = jnp.arange(count)
    vert = (pixel // tile).astype(jnp.float32) - (tile - 1) / 2.0
    horiz = (pixel % tile).astype(jnp.float32) - (tile - 1) / 2.0
    delta_x = horiz[None, :] - params[0][:, None]
    delta_y = vert[None, :] - params[1][:, None]
    cross = params[4] * jnp.sqrt(params[2] * params[3])
    quad = params[2][:, None] * delta_x * delta_x + 2.0 * cross[:, None] * delta_x * delta_y + params[3][:, None] * delta_y * delta_y
    alpha = jnp.where(live[:, None], params[5][:, None] * jnp.exp(-0.5 * quad), 0.0)
    logs = jnp.log1p(-alpha)
    before = jnp.cumsum(logs, axis=0) - logs
    weight = alpha * jnp.exp(before)
    return jnp.dot(params[6:9], weight, precision=lax.Precision.HIGHEST, preferred_element_type=jnp.float32)

def reference(tile_lists, send_rows, centres, conic, rho, opacity, colors, target):
    params = jnp.concatenate([centres, conic, rho, opacity, colors], axis=0)
    strip_of = (jnp.arange(TILES) // TILES_DEV).astype(jnp.int32)
    live = tile_lists >= 0
    entry = jnp.maximum(tile_lists, 0)
    source = (entry // CAP).astype(jnp.int32)
    column = (strip_of[:, None] * CAP + entry % CAP).astype(jnp.int32)
    global_id = source * G_DEV + send_rows[source, column]
    global_id = jnp.where(live, global_id, 0).astype(jnp.int32)

    def render_tile(args):
        ids, mask = args
        return composite(params[:, ids], mask, TILE)
    tiles = lax.map(render_tile, (global_id, live))
    rendered = tiles.reshape(N_DEV, TILES_DEV, 3, TILE, TILE).transpose(2, 0, 3, 1, 4).reshape(3, HEIGHT, WIDTH)
    target_pad = jnp.pad(target, ((0, 0), (5, 5), (0, 0)))

    def total(image):
        return local_loss(jnp.pad(image, ((0, 0), (5, 5), (0, 0))), target_pad)
    loss_value, pull = jax.vjp(total, rendered)
    cotangent = pull(jnp.ones_like(loss_value))[0]
    cot_tiles = cotangent.reshape(3, N_DEV, TILE, TILES_DEV, TILE).transpose(1, 3, 0, 2, 4).reshape(TILES, 3, TILE * TILE)

    def accumulate(carry, args):
        ids, mask, cot = args
        _, back = jax.vjp(lambda chosen: composite(chosen, mask, TILE), params[:, ids])
        entry_grad = back(cot)[0]
        carry = carry.at[:, ids].add(jnp.where(mask[None, :], entry_grad, 0.0))
        return (carry, None)
    grads, _ = lax.scan(accumulate, jnp.zeros_like(params), (global_id, live, cot_tiles))
    return (rendered, grads)
```

```python
import functools

import jax
import jax.numpy as jnp
import numpy as np
from jax import lax
from jax.experimental import pallas as pl
from jax.experimental.pallas import tpu as pltpu
from jax.sharding import PartitionSpec as P

LANES = 128
SUB = 8
RIM = 5
HALO = 2 * RIM
LOG2E = 1.4426950408889634
F32 = jnp.float32
BF16 = jnp.bfloat16
NT = (((1,), (1,)), ((), ()))
TN = (((0,), (0,)), ((), ()))


def dot(a, b, dims):
    return lax.dot_general(a, b, dims, preferred_element_type=F32)


def pieces(x, count):
    out = []
    for _ in range(count - 1):
        top = x.astype(BF16)
        out.append(top)
        x = x - top.astype(F32)
    out.append(x.astype(BF16))
    return out


def lanes_of(shape):
    return lax.broadcasted_iota(jnp.int32, shape, len(shape) - 1)


def rows_of(shape):
    return lax.broadcasted_iota(jnp.int32, shape, len(shape) - 2)


def pick(table, last, where):
    chunks = table.shape[0]
    lane = jnp.bitwise_and(where, LANES - 1)
    chunk = jnp.right_shift(where, 7)
    lane8 = jnp.broadcast_to(lane, (SUB, LANES))
    chunk8 = jnp.broadcast_to(chunk, (SUB, LANES))
    value = jnp.zeros((SUB, LANES), F32)
    for c in range(chunks):
        got = jnp.take_along_axis(table[c], lane8, axis=1, mode="promise_in_bounds")
        value = jnp.where(chunk8 == c, got, value)
    total = jnp.zeros((SUB, LANES), F32)
    for c in range(0, chunks, SUB):
        got = jnp.take_along_axis(last[c : c + SUB], lane8, axis=1, mode="promise_in_bounds")
        total = total + jnp.where(chunk8 == rows_of((SUB, LANES)) + c, got, 0.0)
    return value, jnp.sum(total, axis=0, keepdims=True)


def pack_kernel(rows_ref, centres, conic, rho, opacity, colors, out_ref, table, last):
    chunks = table.shape[0]
    s = -0.5 * LOG2E
    for c in range(chunks):
        at = slice(c * LANES, (c + 1) * LANES)
        x, y = centres[0:1, at], centres[1:2, at]
        a, d = conic[0:1, at], conic[1:2, at]
        b = rho[0:1, at] * jnp.sqrt(a * d)
        rows = [
            jnp.log(opacity[0:1, at]) * LOG2E + s * (a * x * x + 2.0 * b * x * y + d * y * y),
            -2.0 * s * (a * x + b * y),
            -2.0 * s * (d * y + b * x),
            s * a,
            2.0 * s * b,
            s * d,
            colors[0:1, at],
            colors[1:2, at],
        ]
        table[c] = jnp.concatenate(rows, axis=0)
        last[c : c + 1] = colors[2:3, at]
    half = LANES // 2
    left = lanes_of((SUB, LANES)) < half
    for g in range(rows_ref.shape[1] // LANES):
        where = jnp.maximum(rows_ref[0:1, g * LANES : (g + 1) * LANES], 0)
        value, ninth = pick(table, last, where)
        ninth = jnp.broadcast_to(ninth, (SUB, LANES))
        out_ref[2 * g * SUB : (2 * g + 1) * SUB] = jnp.where(left, value, pltpu.roll(ninth, half, 1))
        out_ref[(2 * g + 1) * SUB : (2 * g + 2) * SUB] = jnp.where(left, pltpu.roll(value, half, 1), ninth)


def shifted(x, by):
    return pltpu.roll(x, by % SUB, 0)


def forward_kernel(recv, idx_ref, basis, img_ref, x_ref, seg_ref, table, last):
    chunks = table.shape[0]
    tiles, pixels = img_ref.shape[0], img_ref.shape[2]
    groups = x_ref.shape[2] // LANES
    half = LANES // 2
    left = lanes_of((SUB, LANES)) < half
    for c in range(chunks):
        a = recv[2 * c * SUB : (2 * c + 1) * SUB]
        b = recv[(2 * c + 1) * SUB : (2 * c + 2) * SUB]
        table[c] = jnp.where(left, a, pltpu.roll(b, half, 1))
        last[c : c + 1] = jnp.where(left, pltpu.roll(a, half, 1), b)[0:1]
    first = rows_of((SUB, LANES)) == 0

    def fetch(t, carry):
        for q in range(groups):
            idx = idx_ref[pl.ds(t * groups + q, 1), :]
            live = idx >= 0
            value, ninth = pick(table, last, jnp.maximum(idx, 0))
            live8 = jnp.broadcast_to(live, (SUB, LANES))
            value = jnp.where(live8, value, jnp.where(first, -1000.0, 0.0))
            ninth = jnp.where(live8, jnp.broadcast_to(ninth, (SUB, LANES)), 0.0)
            p0, p1, p2 = [p.astype(F32) for p in pieces(value, 3)]
            n0, n1, n2 = [p.astype(F32) for p in pieces(ninth, 3)]
            r = rows_of((SUB, LANES))
            n = jnp.where(r == 0, n0, jnp.where(r == 1, n1, jnp.where(r == 2, n2, 0.0)))
            x_ref[t, :, q * LANES : (q + 1) * LANES] = jnp.concatenate([p0, p1, p2, n], axis=0).astype(BF16)
        return carry

    lax.fori_loop(0, tiles, fetch, 0)
    row = rows_of((SUB, pixels))

    def composite(t, carry):
        trans = jnp.ones((SUB, pixels), F32)
        acc = [jnp.zeros((SUB, pixels), F32) for _ in range(3)]
        for q in range(groups):
            out = dot(x_ref[t, :, q * LANES : (q + 1) * LANES], basis[...], TN)
            for i in range(LANES // SUB):
                at = slice(i * SUB, (i + 1) * SUB)
                alpha = jnp.exp2(out[at, :pixels])
                w = alpha * trans
                trans = trans * (1.0 - alpha)
                for ch in range(3):
                    tint = out[at, pixels + ch * LANES : pixels + (ch + 1) * LANES]
                    acc[ch] = acc[ch] + jnp.concatenate([tint] * (pixels // LANES), axis=1) * w
        before = jnp.where(row >= 1, shifted(trans, 1), 1.0)
        for by in (1, 2, 4):
            before = before * jnp.where(row >= by, shifted(before, by), 1.0)
        seg_ref[t, 0:SUB] = before
        seg_ref[t, SUB : 2 * SUB] = trans
        image = []
        for ch in range(3):
            seg_ref[t, (2 + ch) * SUB : (3 + ch) * SUB] = acc[ch]
            image.append(jnp.sum(acc[ch] * before, axis=0, keepdims=True))
        img_ref[t] = jnp.concatenate(image, axis=0)
        return carry

    lax.fori_loop(0, tiles, composite, 0)


def taps_of():
    m = np.arange(-RIM, RIM + 1)
    w = np.exp(-m * m / 4.5)
    return [float(v) for v in w / w.sum()]


def blur_rows(x, count):
    taps = taps_of()
    width = x.shape[1]
    out = taps[RIM] * x[RIM : RIM + count]
    for m in range(1, RIM + 1):
        out = out + taps[RIM + m] * (x[RIM - m : RIM - m + count] + x[RIM + m : RIM + m + count])
    lane = lanes_of(out.shape)
    res = taps[RIM] * out
    for m in range(1, RIM + 1):
        up = jnp.where(lane >= m, pltpu.roll(out, m, 1), 0.0)
        down = jnp.where(lane < width - m, pltpu.roll(out, width - m, 1), 0.0)
        res = res + taps[RIM + m] * (up + down)
    return res


def ssim_kernel(edge, ren, tar, ren_b, tar_b, ren_a, tar_a, cot_ref):
    rows = ren.shape[1]
    width = ren.shape[2]
    mid = rows + HALO
    r_at = rows_of((mid, width))
    inside = jnp.logical_and(r_at >= edge[0], r_at < edge[1])
    for ch in range(ren.shape[0]):
        r = jnp.concatenate([ren_b[ch], ren[ch], ren_a[ch]], axis=0)
        t = jnp.concatenate([tar_b[ch], tar[ch], tar_a[ch]], axis=0)
        mr, mt = blur_rows(r, mid), blur_rows(t, mid)
        er, et, ert = blur_rows(r * r, mid), blur_rows(t * t, mid), blur_rows(r * t, mid)
        a1 = 2.0 * mr * mt + 0.0001
        a2 = 2.0 * (ert - mr * mt) + 0.0009
        b1 = mr * mr + mt * mt + 0.0001
        b2 = (er - mr * mr) + (et - mt * mt) + 0.0009
        i1, i2 = 1.0 / b1, 1.0 / b2
        s = a1 * a2 * i1 * i2
        d_mr = 2.0 * mt * (a2 - a1) * i1 * i2 - 2.0 * mr * s * (i1 - i2)
        d_er = -s * i2
        d_ert = 2.0 * a1 * i1 * i2
        g0, g1, g2 = [blur_rows(jnp.where(inside, d, 0.0), rows) for d in (d_mr, d_er, d_ert)]
        rc, tc = ren[ch], tar[ch]
        cot_ref[ch] = 1.6 * (rc - tc) - 0.2 * (g0 + 2.0 * rc * g1 + tc * g2)


def spread(values, where, total):
    count = where.shape[1]
    wide = total.shape[1]
    p0, p1, p2 = [p.astype(F32) for p in pieces(values, 3)]
    rows = rows_of((SUB, count))
    tail = jnp.where(rows == 0, p0[SUB:], jnp.where(rows == 1, p1[SUB:], jnp.where(rows == 2, p2[SUB:], 0.0)))
    stacked = jnp.concatenate([p0[:SUB], p1[:SUB], p2[:SUB], tail], axis=0)
    low = jnp.bitwise_and(where, wide - 1)
    high = jnp.where(where < 0, -1, jnp.right_shift(where, wide.bit_length() - 1))
    hot = (jnp.broadcast_to(low, (wide, count)) == rows_of((wide, count))).astype(F32).astype(BF16)
    parts = []
    for c in range(total.shape[0] // 32):
        parts.append(jnp.where(jnp.broadcast_to(high == c, stacked.shape), stacked, 0.0).astype(BF16))
    total[...] += dot(jnp.concatenate(parts, axis=0), hot, NT)


def nine(total, c):
    got = total[c * 32 : (c + 1) * 32]
    return (
        got[0:SUB] + got[SUB : 2 * SUB] + got[2 * SUB : 3 * SUB],
        got[24:25] + got[25:26] + got[26:27],
    )


def backward_kernel(x_ref, idx_ref, seg_ref, cot_ref, basis, phi, out_ref, alphas, weights, grads, total):
    tiles, pixels = cot_ref.shape[0], cot_ref.shape[2]
    count = x_ref.shape[2]
    groups = count // LANES
    steps = LANES // SUB
    total[...] = jnp.zeros_like(total)
    row = rows_of((SUB, pixels))
    row32 = rows_of((32, pixels))

    def tile(t, carry):
        cot = [jnp.broadcast_to(cot_ref[t, ch : ch + 1], (SUB, pixels)) for ch in range(3)]
        hi = [c.astype(BF16).astype(F32) for c in cot]
        lo = [c - h for c, h in zip(cot, hi)]

        def place(v):
            body = jnp.where(row == 6, v[0], jnp.where(row == 7, v[1], 0.0))
            return [body, body, body, jnp.where(row < 3, v[2], 0.0)]

        rhs_g = jnp.concatenate(place(hi) + place(lo), axis=0).astype(BF16)
        lhs = jnp.where(row == 6, hi[0], jnp.where(row == 7, hi[1], 0.0)) + phi[0:SUB]
        lhs2 = jnp.where(row == 0, hi[2], jnp.where(row == 1, lo[0], jnp.where(row == 2, lo[1], jnp.where(row == 3, lo[2], 0.0))))
        lhs = jnp.concatenate([lhs, lhs2], axis=0).astype(BF16)

        seg = [seg_ref[t, s * SUB : (s + 1) * SUB] for s in range(5)]
        add = cot[0] * seg[2] + cot[1] * seg[3] + cot[2] * seg[4]
        mul = seg[1]
        for by in (1, 2, 4):
            more = row < SUB - by
            add_n = jnp.where(more, shifted(add, -by), 0.0)
            mul_n = jnp.where(more, shifted(mul, -by), 1.0)
            add, mul = add + mul * add_n, mul * mul_n
        behind = jnp.where(row < SUB - 1, shifted(add, -1), 0.0)

        trans = seg[0]
        for q in range(groups):
            out = dot(x_ref[t, :, q * LANES : (q + 1) * LANES], basis[:, :pixels], TN)
            for i in range(steps):
                at = slice(q * LANES + i * SUB, q * LANES + (i + 1) * SUB)
                alpha = jnp.exp2(out[i * SUB : (i + 1) * SUB])
                alphas[at] = alpha
                weights[at] = alpha * trans
                trans = trans * (1.0 - alpha)
        for q in reversed(range(groups)):
            x = x_ref[t, :, q * LANES : (q + 1) * LANES]
            g = dot(jnp.concatenate([x, x], axis=0), rhs_g, TN)
            hs = [None] * steps
            for i in reversed(range(steps)):
                at = slice(q * LANES + i * SUB, q * LANES + (i + 1) * SUB)
                d = g[i * SUB : (i + 1) * SUB] - behind
                hs[i] = weights[at] * d
                behind = behind + alphas[at] * d
            h = jnp.concatenate(hs, axis=0)
            h0, h1 = pieces(h, 2)
            w0, w1 = pieces(weights[q * LANES : (q + 1) * LANES], 2)
            gh = dot(lhs, h0, NT) + dot(lhs, h1, NT)
            gw = dot(lhs, w0, NT) + dot(lhs, w1, NT)
            r8 = rows_of((SUB, LANES))
            low = gw[SUB:]
            top = jnp.where(r8 < 6, gh[:SUB], gw[:SUB] + pltpu.roll(low, 5, 0))
            ninth = jnp.broadcast_to((low + pltpu.roll(low, 5, 0))[0:1], (SUB, LANES))
            grads[:, q * LANES : (q + 1) * LANES] = jnp.concatenate([top, ninth], axis=0)
        where = jnp.concatenate([idx_ref[pl.ds(t * groups + q, 1), :] for q in range(groups)], axis=1)
        spread(grads[...], where, total)
        return carry

    lax.fori_loop(0, tiles, tile, 0)
    half = LANES // 2
    left = lanes_of((SUB, LANES)) < half
    per = total.shape[1] // LANES
    for c in range(total.shape[0] // 32):
        eight, ninth = nine(total, c)
        for j in range(per):
            e = eight[:, j * LANES : (j + 1) * LANES]
            n = jnp.broadcast_to(ninth[:, j * LANES : (j + 1) * LANES], (SUB, LANES))
            at = (c * per + j) * 2 * SUB
            out_ref[at : at + SUB] = jnp.where(left, e, pltpu.roll(n, half, 1))
            out_ref[at + SUB : at + 2 * SUB] = jnp.where(left, pltpu.roll(e, half, 1), n)


def home_kernel(recv, rows_ref, centres, conic, rho, opacity, out_ref, total):
    half = LANES // 2
    left = lanes_of((SUB, LANES)) < half
    total[...] = jnp.zeros_like(total)
    step = 4
    for g in range(0, rows_ref.shape[1] // LANES, step):
        eights, ninths = [], []
        for k in range(g, g + step):
            a = recv[2 * k * SUB : (2 * k + 1) * SUB]
            b = recv[(2 * k + 1) * SUB : (2 * k + 2) * SUB]
            eights.append(jnp.where(left, a, pltpu.roll(b, half, 1)))
            n = jnp.where(left, pltpu.roll(a, half, 1), b)
            ninths.append(jnp.broadcast_to(n[0:1], (SUB, LANES)))
        values = jnp.concatenate([jnp.concatenate(eights, axis=1), jnp.concatenate(ninths, axis=1)], axis=0)
        spread(values, rows_ref[0:1, g * LANES : (g + step) * LANES], total)
    wide = total.shape[1]
    for c in range(total.shape[0] // 32):
        m, col2 = nine(total, c)
        at = slice(c * wide, (c + 1) * wide)
        x, y = centres[0:1, at], centres[1:2, at]
        a, d = conic[0:1, at], conic[1:2, at]
        root = jnp.sqrt(a * d)
        b = rho[0:1, at] * root
        m1, mu, mv, muu, muv, mvv = [m[i : i + 1] for i in range(6)]
        dx, dy = mu - x * m1, mv - y * m1
        dxx = muu - 2.0 * x * mu + x * x * m1
        dxy = muv - x * mv - y * mu + x * y * m1
        dyy = mvv - 2.0 * y * mv + y * y * m1
        rows = [
            a * dx + b * dy,
            b * dx + d * dy,
            -0.5 * (dxx + b / a * dxy),
            -0.5 * (dyy + b / d * dxy),
            -root * dxy,
            m1 / opacity[0:1, at],
            m[6:7],
            m[7:8],
            col2,
        ]
        for i, v in enumerate(rows):
            out_ref[i : i + 1, at] = v


def tables(tile):
    pixels = tile * tile
    p = np.arange(pixels)
    v = (p // tile) - (tile - 1) / 2.0
    u = (p % tile) - (tile - 1) / 2.0
    six = np.stack([np.ones(pixels), u, v, u * u, u * v, v * v])
    basis = np.zeros((32, pixels + 3 * LANES), np.float32)
    for k in range(3):
        basis[8 * k : 8 * k + 6, :pixels] = six
        basis[8 * k + 6, pixels : pixels + LANES] = 1.0
        basis[8 * k + 7, pixels + LANES : pixels + 2 * LANES] = 1.0
        basis[24 + k, pixels + 2 * LANES :] = 1.0
    phi = np.zeros((8, pixels), np.float32)
    phi[:6] = six
    return jnp.asarray(basis, BF16), jnp.asarray(phi)


def call(kernel, out_shape, scratch=(), smem=0):
    n_vmem = pl.BlockSpec()

    def run(*args):
        specs = [pl.BlockSpec(memory_space=pltpu.SMEM) if i < smem else n_vmem for i in range(len(args))]
        return pl.pallas_call(
            kernel,
            out_shape=out_shape,
            in_specs=specs,
            out_specs=jax.tree.map(lambda _: n_vmem, out_shape),
            scratch_shapes=list(scratch),
            compiler_params=pltpu.CompilerParams(vmem_limit_bytes=48 * 1024 * 1024),
        )(*args)

    return run


def swap_edges(value):
    size = lax.axis_size("dev")
    me = lax.axis_index("dev")
    first, last = value[:, :HALO], value[:, -HALO:]
    odd = (me % 2) == 1
    inner = [(i, i ^ 1) for i in range(size)]
    outer = [(i, i + 1) for i in range(1, size - 1, 2)]
    outer = outer + [(j, i) for i, j in outer]
    got_in = lax.ppermute(jnp.where(odd, first, last), "dev", inner)
    got_out = lax.ppermute(jnp.where(odd, last, first), "dev", outer)
    return jnp.where(odd, got_in, got_out), jnp.where(odd, got_out, got_in)


def shards(tile_lists, send_rows, centres, conic, rho, opacity, colors, target):
    slot_count = send_rows.shape[1]
    owned_count = centres.shape[1]
    channels, tile, width = target.shape
    strip_tiles, list_len = tile_lists.shape
    size = lax.axis_size("dev")
    me = lax.axis_index("dev")
    pixels = tile * tile
    chunks = slot_count // LANES
    wide = 2 * LANES
    basis, phi = tables(tile)
    sds = jax.ShapeDtypeStruct

    packed = call(
        pack_kernel,
        sds((size * SUB, LANES), F32),
        [pltpu.VMEM((owned_count // LANES, SUB, LANES), F32), pltpu.VMEM((owned_count // LANES, LANES), F32)],
    )(send_rows, centres, conic, rho, opacity, colors)
    received = lax.all_to_all(packed, "dev", split_axis=0, concat_axis=0, tiled=True)

    order = tile_lists.reshape(strip_tiles, SUB, list_len // SUB).transpose(0, 2, 1)
    order = order.reshape(strip_tiles * list_len // LANES, LANES)
    tar_b, tar_a = swap_edges(target)

    colour_tiles, coefs, segments = call(
        forward_kernel,
        (
            sds((strip_tiles, channels, pixels), F32),
            sds((strip_tiles, 32, list_len), BF16),
            sds((strip_tiles, 5 * SUB, pixels), F32),
        ),
        [pltpu.VMEM((chunks, SUB, LANES), F32), pltpu.VMEM((chunks, LANES), F32)],
    )(received, order, basis)
    image = (
        colour_tiles.reshape(strip_tiles, channels, tile, tile).transpose(1, 2, 0, 3).reshape(channels, tile, width)
    )
    ren_b, ren_a = swap_edges(image)
    edge = jnp.stack([jnp.where(me == 0, RIM, 0), jnp.where(me == size - 1, tile + RIM, tile + HALO)]).astype(jnp.int32)
    cot = call(ssim_kernel, sds((channels, tile, width), F32), smem=1)(
        edge, image, target, ren_b, tar_b, ren_a, tar_a
    )
    cot_tiles = (
        cot.reshape(channels, tile, strip_tiles, tile).transpose(2, 0, 1, 3).reshape(strip_tiles, channels, pixels)
    )
    slot_sums = call(
        backward_kernel,
        sds((size * SUB, LANES), F32),
        [
            pltpu.VMEM((list_len, pixels), F32),
            pltpu.VMEM((list_len, pixels), F32),
            pltpu.VMEM((2 * SUB, list_len), F32),
            pltpu.VMEM((slot_count // wide * 32, wide), F32),
        ],
    )(coefs, order, segments, cot_tiles, basis, phi)
    returned = lax.all_to_all(slot_sums, "dev", split_axis=0, concat_axis=0, tiled=True)
    grads = call(
        home_kernel,
        sds((9, owned_count), F32),
        [pltpu.VMEM((owned_count // wide * 32, wide), F32)],
    )(returned, send_rows, centres, conic, rho, opacity)
    return (image, grads)


def solution(mesh):
    return jax.shard_map(
        shards,
        mesh=mesh,
        in_specs=(
            P("dev", None),
            P("dev", None),
            P(None, "dev"),
            P(None, "dev"),
            P(None, "dev"),
            P(None, "dev"),
            P(None, "dev"),
            P(None, "dev", None),
        ),
        out_specs=(P(None, "dev", None), P(None, "dev")),
        check_vma=False,
    )
```

```python
import functools

import jax
import jax.numpy as jnp
import numpy as np
from jax import lax
from jax.experimental import pallas as pl
from jax.experimental.pallas import tpu as pltpu
from jax.sharding import PartitionSpec as P

LANES = 128
SUB = 8
RIM = 5
HALO = 2 * RIM
LOG2E = 1.4426950408889634
F32 = jnp.float32
BF16 = jnp.bfloat16
NN = (((1,), (0,)), ((), ()))
NT = (((1,), (1,)), ((), ()))
TN = (((0,), (0,)), ((), ()))


def dot(a, b, dims):
    return lax.dot_general(a, b, dims, preferred_element_type=F32)


def pieces(x, count):
    out = []
    for _ in range(count - 1):
        top = x.astype(BF16)
        out.append(top)
        x = x - top.astype(F32)
    out.append(x.astype(BF16))
    return out


def lanes_of(shape):
    return lax.broadcasted_iota(jnp.int32, shape, len(shape) - 1)


def rows_of(shape):
    return lax.broadcasted_iota(jnp.int32, shape, len(shape) - 2)


def pick(table, last, where):
    chunks = table.shape[0]
    lane = jnp.bitwise_and(where, LANES - 1)
    chunk = jnp.right_shift(where, 7)
    lane8 = jnp.broadcast_to(lane, (SUB, LANES))
    chunk8 = jnp.broadcast_to(chunk, (SUB, LANES))
    value = jnp.zeros((SUB, LANES), F32)
    for c in range(chunks):
        got = jnp.take_along_axis(table[c], lane8, axis=1, mode="promise_in_bounds")
        value = jnp.where(chunk8 == c, got, value)
    total = jnp.zeros((SUB, LANES), F32)
    for c in range(0, chunks, SUB):
        got = jnp.take_along_axis(last[c : c + SUB], lane8, axis=1, mode="promise_in_bounds")
        total = total + jnp.where(chunk8 == rows_of((SUB, LANES)) + c, got, 0.0)
    return value, jnp.sum(total, axis=0, keepdims=True)


def pack_kernel(rows_ref, centres, conic, rho, opacity, colors, out_ref, table, last):
    chunks = table.shape[0]
    s = -0.5 * LOG2E
    for c in range(chunks):
        at = slice(c * LANES, (c + 1) * LANES)
        x, y = centres[0:1, at], centres[1:2, at]
        a, d = conic[0:1, at], conic[1:2, at]
        b = rho[0:1, at] * jnp.sqrt(a * d)
        rows = [
            jnp.log(opacity[0:1, at]) * LOG2E + s * (a * x * x + 2.0 * b * x * y + d * y * y),
            -2.0 * s * (a * x + b * y),
            -2.0 * s * (d * y + b * x),
            s * a,
            2.0 * s * b,
            s * d,
            colors[0:1, at],
            colors[1:2, at],
        ]
        table[c] = jnp.concatenate(rows, axis=0)
        last[c : c + 1] = colors[2:3, at]
    half = LANES // 2
    left = lanes_of((SUB, LANES)) < half
    for g in range(rows_ref.shape[1] // LANES):
        where = jnp.maximum(rows_ref[0:1, g * LANES : (g + 1) * LANES], 0)
        value, ninth = pick(table, last, where)
        ninth = jnp.broadcast_to(ninth, (SUB, LANES))
        out_ref[2 * g * SUB : (2 * g + 1) * SUB] = jnp.where(left, value, pltpu.roll(ninth, half, 1))
        out_ref[(2 * g + 1) * SUB : (2 * g + 2) * SUB] = jnp.where(left, pltpu.roll(value, half, 1), ninth)


def shifted(x, by):
    return pltpu.roll(x, by % SUB, 0)


def forward_kernel(recv, idx_ref, basis, img_ref, x_ref, seg_ref, table, last):
    chunks = table.shape[0]
    tiles, pixels = img_ref.shape[0], img_ref.shape[2]
    groups = x_ref.shape[2] // LANES
    half = LANES // 2
    left = lanes_of((SUB, LANES)) < half
    for c in range(chunks):
        a = recv[2 * c * SUB : (2 * c + 1) * SUB]
        b = recv[(2 * c + 1) * SUB : (2 * c + 2) * SUB]
        table[c] = jnp.where(left, a, pltpu.roll(b, half, 1))
        last[c : c + 1] = jnp.where(left, pltpu.roll(a, half, 1), b)[0:1]
    first = rows_of((SUB, LANES)) == 0

    row = rows_of((SUB, pixels))

    def fetch(t, q):
        idx = idx_ref[pl.ds(t * groups + q, 1), :]
        live = idx >= 0
        value, ninth = pick(table, last, jnp.maximum(idx, 0))
        live8 = jnp.broadcast_to(live, (SUB, LANES))
        value = jnp.where(live8, value, jnp.where(first, -1000.0, 0.0))
        ninth = jnp.where(live8, jnp.broadcast_to(ninth, (SUB, LANES)), 0.0)
        p0, p1, p2 = [p.astype(F32) for p in pieces(value, 3)]
        n0, n1, n2 = [p.astype(F32) for p in pieces(ninth, 3)]
        r = rows_of((SUB, LANES))
        n = jnp.where(r == 0, n0, jnp.where(r == 1, n1, jnp.where(r == 2, n2, 0.0)))
        chunk = jnp.broadcast_to(jnp.where(live, jnp.right_shift(idx, 8), -1).astype(F32), (SUB, LANES))
        n = jnp.where(r == 3, chunk, jnp.where(r == 4, 1.0, n))
        return jnp.concatenate([p0, p1, p2, n], axis=0).astype(BF16)

    def composite(t):
        trans = jnp.ones((SUB, pixels), F32)
        acc = [jnp.zeros((SUB, pixels), F32) for _ in range(3)]
        for q in range(groups):
            x = fetch(t, q)
            x_ref[t, :, q * LANES : (q + 1) * LANES] = x
            out = dot(x, basis[...], TN)
            for i in range(LANES // SUB):
                at = slice(i * SUB, (i + 1) * SUB)
                alpha = jnp.exp2(out[at, :pixels])
                w = alpha * trans
                trans = trans * (1.0 - alpha)
                for ch in range(3):
                    tint = out[at, pixels + ch * LANES : pixels + (ch + 1) * LANES]
                    acc[ch] = acc[ch] + jnp.concatenate([tint] * (pixels // LANES), axis=1) * w
        before = jnp.where(row >= 1, shifted(trans, 1), 1.0)
        for by in (1, 2, 4):
            before = before * jnp.where(row >= by, shifted(before, by), 1.0)
        seg_ref[t, 0:SUB] = before
        seg_ref[t, SUB : 2 * SUB] = trans
        image = []
        for ch in range(3):
            seg_ref[t, (2 + ch) * SUB : (3 + ch) * SUB] = acc[ch]
            image.append(jnp.sum(acc[ch] * before, axis=0, keepdims=True))
        img_ref[t] = jnp.concatenate(image, axis=0)

    def body(i, carry):
        for k in range(par):
            composite(i * par + k)
        return carry

    par = 4
    lax.fori_loop(0, tiles // par, body, 0)


def taps_of():
    m = np.arange(-RIM, RIM + 1)
    w = np.exp(-m * m / 4.5)
    return [float(v) for v in w / w.sum()]


def blur_rows(x, count):
    taps = taps_of()
    width = x.shape[1]
    out = taps[RIM] * x[RIM : RIM + count]
    for m in range(1, RIM + 1):
        out = out + taps[RIM + m] * (x[RIM - m : RIM - m + count] + x[RIM + m : RIM + m + count])
    lane = lanes_of(out.shape)
    res = taps[RIM] * out
    for m in range(1, RIM + 1):
        up = jnp.where(lane >= m, pltpu.roll(out, m, 1), 0.0)
        down = jnp.where(lane < width - m, pltpu.roll(out, width - m, 1), 0.0)
        res = res + taps[RIM + m] * (up + down)
    return res


def ssim_kernel(edge, ren, tar, ren_b, tar_b, ren_a, tar_a, cot_ref):
    rows = ren.shape[1]
    width = ren.shape[2]
    mid = rows + HALO
    r_at = rows_of((mid, width))
    inside = jnp.logical_and(r_at >= edge[0], r_at < edge[1])
    for ch in range(ren.shape[0]):
        r = jnp.concatenate([ren_b[ch], ren[ch], ren_a[ch]], axis=0)
        t = jnp.concatenate([tar_b[ch], tar[ch], tar_a[ch]], axis=0)
        mr, mt = blur_rows(r, mid), blur_rows(t, mid)
        er, et, ert = blur_rows(r * r, mid), blur_rows(t * t, mid), blur_rows(r * t, mid)
        a1 = 2.0 * mr * mt + 0.0001
        a2 = 2.0 * (ert - mr * mt) + 0.0009
        b1 = mr * mr + mt * mt + 0.0001
        b2 = (er - mr * mr) + (et - mt * mt) + 0.0009
        i1, i2 = 1.0 / b1, 1.0 / b2
        s = a1 * a2 * i1 * i2
        d_mr = 2.0 * mt * (a2 - a1) * i1 * i2 - 2.0 * mr * s * (i1 - i2)
        d_er = -s * i2
        d_ert = 2.0 * a1 * i1 * i2
        g0, g1, g2 = [blur_rows(jnp.where(inside, d, 0.0), rows) for d in (d_mr, d_er, d_ert)]
        rc, tc = ren[ch], tar[ch]
        cot_ref[ch] = 1.6 * (rc - tc) - 0.2 * (g0 + 2.0 * rc * g1 + tc * g2)


def spread(values, where, total):
    count = where.shape[1]
    wide = total.shape[1]
    p0, p1, p2 = [p.astype(F32) for p in pieces(values, 3)]
    rows = rows_of((SUB, count))
    tail = jnp.where(rows == 0, p0[SUB:], jnp.where(rows == 1, p1[SUB:], jnp.where(rows == 2, p2[SUB:], 0.0)))
    stacked = jnp.concatenate([p0[:SUB], p1[:SUB], p2[:SUB], tail], axis=0)
    low = jnp.bitwise_and(where, wide - 1)
    high = jnp.where(where < 0, -1, jnp.right_shift(where, wide.bit_length() - 1))
    hot = (jnp.broadcast_to(low, (wide, count)) == rows_of((wide, count))).astype(F32).astype(BF16)
    parts = []
    for c in range(total.shape[0] // 32):
        parts.append(jnp.where(jnp.broadcast_to(high == c, stacked.shape), stacked, 0.0).astype(BF16))
    total[...] += dot(jnp.concatenate(parts, axis=0), hot, NT)


def nine(total, c):
    got = total[c * 32 : (c + 1) * 32]
    return (
        got[0:SUB] + got[SUB : 2 * SUB] + got[2 * SUB : 3 * SUB],
        got[24:25] + got[25:26] + got[26:27],
    )


BLOCK = 16


def backward_kernel(x_ref, idx_ref, seg_ref, cot_ref, basis, phi, out_ref, total, *buffers):
    tiles, pixels = cot_ref.shape[0], cot_ref.shape[2]
    count = x_ref.shape[2]
    groups = count // LANES
    steps = LANES // SUB
    wide = 2 * LANES
    total[...] = jnp.zeros_like(total)
    row = rows_of((SUB, pixels))
    each = 6
    par = len(buffers) // each
    columns = total.shape[1] // 2
    field_lane = jnp.bitwise_and(lanes_of((2 * SUB, LANES)), BLOCK - 1)
    select = (field_lane == rows_of((2 * SUB, LANES)) + 6).astype(F32).astype(BF16)

    def first_pass(t, alphas, weights, factors, rhs, offs, split):
        trans = seg_ref[t, 0:SUB]
        for q in range(groups):
            out = dot(x_ref[t, :, q * LANES : (q + 1) * LANES], basis[...], TN)
            offs[q * LANES : (q + 1) * LANES] = out[:, pixels:]
            for i in range(steps):
                at = slice(q * LANES + i * SUB, q * LANES + (i + 1) * SUB)
                alpha = jnp.exp2(out[i * SUB : (i + 1) * SUB, :pixels])
                alphas[at] = alpha
                weights[at] = alpha * trans
                trans = trans * (1.0 - alpha)

    def second_pass(t, alphas, weights, factors, rhs, offs, split):
        cot = [jnp.broadcast_to(cot_ref[t, ch : ch + 1], (SUB, pixels)) for ch in range(3)]
        hi = [c.astype(BF16).astype(F32) for c in cot]
        lo = [c - h for c, h in zip(cot, hi)]

        def place(v):
            body = jnp.where(row == 6, v[0], jnp.where(row == 7, v[1], 0.0))
            return [body, body, body, jnp.where(row < 3, v[2], 0.0)]

        rhs_g = jnp.concatenate(place(hi) + place(lo), axis=0).astype(BF16)
        six = jnp.zeros((SUB, pixels), F32)
        for k, v in enumerate(hi + lo):
            six = jnp.where(row == k, v, six)
        six = jnp.concatenate([six, jnp.zeros((SUB, pixels), F32)], axis=0).astype(BF16)
        six = dot(six, select, TN).astype(BF16)
        rhs[2 * pixels : 3 * pixels] = six
        rhs[3 * pixels :] = six

        seg = [seg_ref[t, s * SUB : (s + 1) * SUB] for s in range(5)]
        add = cot[0] * seg[2] + cot[1] * seg[3] + cot[2] * seg[4]
        mul = seg[1]
        for by in (1, 2, 4):
            more = row < SUB - by
            add_n = jnp.where(more, shifted(add, -by), 0.0)
            mul_n = jnp.where(more, shifted(mul, -by), 1.0)
            add, mul = add + mul * add_n, mul * mul_n
        behind = jnp.where(row < SUB - 1, shifted(add, -1), 0.0)
        for q in reversed(range(groups)):
            x = x_ref[t, :, q * LANES : (q + 1) * LANES]
            g = dot(jnp.concatenate([x, x], axis=0), rhs_g, TN)
            for i in reversed(range(0, steps, 2)):
                hs, ws = [], []
                for j in (i + 1, i):
                    at = slice(q * LANES + j * SUB, q * LANES + (j + 1) * SUB)
                    d = g[j * SUB : (j + 1) * SUB] - behind
                    w = weights[at]
                    hs.insert(0, w * d)
                    ws.insert(0, w)
                    behind = behind + alphas[at] * d
                at = slice(q * LANES + i * SUB, q * LANES + (i + 2) * SUB)
                parts = pieces(jnp.concatenate(hs, axis=0), 2) + pieces(jnp.concatenate(ws, axis=0), 2)
                for k, v in enumerate(parts):
                    factors[at, k * pixels : (k + 1) * pixels] = v

    def sums(t, alphas, weights, factors, rhs, offs, split):
        got = dot(factors[...], rhs[...], NN)
        where = jnp.concatenate([idx_ref[pl.ds(t * groups + q, 1), :] for q in range(groups)], axis=1)
        low = jnp.bitwise_and(where, wide - 1)
        hot = (jnp.broadcast_to(low, (wide, count)) == rows_of((wide, count))).astype(F32).astype(BF16)
        for base in range(0, columns, LANES):
            kept = jnp.where(offs[:, base : base + LANES] == 0.0, got, 0.0)
            top, rest = pieces(kept, 2)
            split[:, base : base + LANES] = top
            split[:, columns + base : columns + base + LANES] = rest
        total[...] += dot(hot, split[...], NN)

    def body(i, carry):
        for stage in (first_pass, second_pass, sums):
            for k in range(par):
                stage(i * par + k, *buffers[each * k : each * (k + 1)])
        return carry

    for k in range(par):
        buffers[each * k + 3][: 2 * pixels] = phi[...]
    lax.fori_loop(0, tiles // par, body, 0)
    half = LANES // 2
    left = lanes_of((SUB, LANES)) < half
    for c in range(columns // BLOCK):
        if c % SUB == 0:
            at = c // SUB * LANES
            both = total[:, at : at + LANES] + total[:, columns + at : columns + at + LANES]
            turned = jnp.concatenate([jnp.transpose(both[:LANES]), jnp.transpose(both[LANES:])], axis=1)
        got = turned[c % SUB * BLOCK : (c % SUB + 1) * BLOCK]
        eight = jnp.concatenate([got[:6], got[6:8] + got[9:11]], axis=0)
        ninth = got[8:9] + got[11:12]
        for j in range(2):
            e = eight[:, j * LANES : (j + 1) * LANES]
            n = jnp.broadcast_to(ninth[:, j * LANES : (j + 1) * LANES], (SUB, LANES))
            at = (c * 2 + j) * 2 * SUB
            out_ref[at : at + SUB] = jnp.where(left, e, pltpu.roll(n, half, 1))
            out_ref[at + SUB : at + 2 * SUB] = jnp.where(left, pltpu.roll(e, half, 1), n)


def home_kernel(recv, rows_ref, centres, conic, rho, opacity, out_ref, total):
    half = LANES // 2
    left = lanes_of((SUB, LANES)) < half
    total[...] = jnp.zeros_like(total)
    step = 4
    for g in range(0, rows_ref.shape[1] // LANES, step):
        eights, ninths = [], []
        for k in range(g, g + step):
            a = recv[2 * k * SUB : (2 * k + 1) * SUB]
            b = recv[(2 * k + 1) * SUB : (2 * k + 2) * SUB]
            eights.append(jnp.where(left, a, pltpu.roll(b, half, 1)))
            n = jnp.where(left, pltpu.roll(a, half, 1), b)
            ninths.append(jnp.broadcast_to(n[0:1], (SUB, LANES)))
        values = jnp.concatenate([jnp.concatenate(eights, axis=1), jnp.concatenate(ninths, axis=1)], axis=0)
        spread(values, rows_ref[0:1, g * LANES : (g + step) * LANES], total)
    wide = total.shape[1]
    for c in range(total.shape[0] // 32):
        m, col2 = nine(total, c)
        at = slice(c * wide, (c + 1) * wide)
        x, y = centres[0:1, at], centres[1:2, at]
        a, d = conic[0:1, at], conic[1:2, at]
        root = jnp.sqrt(a * d)
        b = rho[0:1, at] * root
        m1, mu, mv, muu, muv, mvv = [m[i : i + 1] for i in range(6)]
        dx, dy = mu - x * m1, mv - y * m1
        dxx = muu - 2.0 * x * mu + x * x * m1
        dxy = muv - x * mv - y * mu + x * y * m1
        dyy = mvv - 2.0 * y * mv + y * y * m1
        rows = [
            a * dx + b * dy,
            b * dx + d * dy,
            -0.5 * (dxx + b / a * dxy),
            -0.5 * (dyy + b / d * dxy),
            -root * dxy,
            m1 / opacity[0:1, at],
            m[6:7],
            m[7:8],
            col2,
        ]
        for i, v in enumerate(rows):
            out_ref[i : i + 1, at] = v


def tables(tile, slots):
    pixels = tile * tile
    wide = 2 * LANES
    p = np.arange(pixels)
    v = (p // tile) - (tile - 1) / 2.0
    u = (p % tile) - (tile - 1) / 2.0
    six = np.stack([np.ones(pixels), u, v, u * u, u * v, v * v])
    columns = slots // wide * BLOCK
    ahead = np.zeros((32, pixels + 3 * LANES), np.float32)
    back = np.zeros((32, pixels + columns), np.float32)
    for k in range(3):
        ahead[8 * k : 8 * k + 6, :pixels] = six
        back[8 * k : 8 * k + 6, :pixels] = six
        ahead[8 * k + 6, pixels : pixels + LANES] = 1.0
        ahead[8 * k + 7, pixels + LANES : pixels + 2 * LANES] = 1.0
        ahead[24 + k, pixels + 2 * LANES :] = 1.0
    back[27, pixels:] = 1.0
    back[28, pixels:] = -(np.arange(columns) // BLOCK)
    phi = np.zeros((2 * pixels, LANES), np.float32)
    for lane in range(LANES):
        field = lane % BLOCK
        if field < 6:
            phi[:pixels, lane] = six[field]
            phi[pixels:, lane] = six[field]
    return jnp.asarray(ahead, BF16), jnp.asarray(back, BF16), jnp.asarray(phi, BF16)


def back_scratch(list_len, pixels, slots, par=4):
    columns = slots // (2 * LANES) * BLOCK
    one = [
        pltpu.VMEM((list_len, pixels), F32),
        pltpu.VMEM((list_len, pixels), F32),
        pltpu.VMEM((list_len, 4 * pixels), BF16),
        pltpu.VMEM((4 * pixels, LANES), BF16),
        pltpu.VMEM((list_len, columns), F32),
        pltpu.VMEM((list_len, 2 * columns), BF16),
    ]
    return [pltpu.VMEM((2 * LANES, 2 * columns), F32)] + one * par


def call(kernel, out_shape, scratch=(), smem=0, mib=48):
    n_vmem = pl.BlockSpec()

    def run(*args):
        specs = [pl.BlockSpec(memory_space=pltpu.SMEM) if i < smem else n_vmem for i in range(len(args))]
        return pl.pallas_call(
            kernel,
            out_shape=out_shape,
            in_specs=specs,
            out_specs=jax.tree.map(lambda _: n_vmem, out_shape),
            scratch_shapes=list(scratch),
            compiler_params=pltpu.CompilerParams(vmem_limit_bytes=mib * 1024 * 1024),
        )(*args)

    return run


def swap_edges(value):
    size = lax.axis_size("dev")
    me = lax.axis_index("dev")
    first, last = value[:, :HALO], value[:, -HALO:]
    odd = (me % 2) == 1
    inner = [(i, i ^ 1) for i in range(size)]
    outer = [(i, i + 1) for i in range(1, size - 1, 2)]
    outer = outer + [(j, i) for i, j in outer]
    got_in = lax.ppermute(jnp.where(odd, first, last), "dev", inner)
    got_out = lax.ppermute(jnp.where(odd, last, first), "dev", outer)
    return jnp.where(odd, got_in, got_out), jnp.where(odd, got_out, got_in)


def shards(tile_lists, send_rows, centres, conic, rho, opacity, colors, target):
    slot_count = send_rows.shape[1]
    owned_count = centres.shape[1]
    channels, tile, width = target.shape
    strip_tiles, list_len = tile_lists.shape
    size = lax.axis_size("dev")
    me = lax.axis_index("dev")
    pixels = tile * tile
    chunks = slot_count // LANES
    wide = 2 * LANES
    basis, basis_back, phi = tables(tile, slot_count)
    sds = jax.ShapeDtypeStruct

    packed = call(
        pack_kernel,
        sds((size * SUB, LANES), F32),
        [pltpu.VMEM((owned_count // LANES, SUB, LANES), F32), pltpu.VMEM((owned_count // LANES, LANES), F32)],
        mib=63,
    )(send_rows, centres, conic, rho, opacity, colors)
    received = lax.all_to_all(packed, "dev", split_axis=0, concat_axis=0, tiled=True)

    order = tile_lists.reshape(strip_tiles, SUB, list_len // SUB).transpose(0, 2, 1)
    order = order.reshape(strip_tiles * list_len // LANES, LANES)
    tar_b, tar_a = swap_edges(target)

    colour_tiles, coefs, segments = call(
        forward_kernel,
        (
            sds((strip_tiles, channels, pixels), F32),
            sds((strip_tiles, 32, list_len), BF16),
            sds((strip_tiles, 5 * SUB, pixels), F32),
        ),
        [pltpu.VMEM((chunks, SUB, LANES), F32), pltpu.VMEM((chunks, LANES), F32)],
    )(received, order, basis)
    image = (
        colour_tiles.reshape(strip_tiles, channels, tile, tile).transpose(1, 2, 0, 3).reshape(channels, tile, width)
    )
    ren_b, ren_a = swap_edges(image)
    edge = jnp.stack([jnp.where(me == 0, RIM, 0), jnp.where(me == size - 1, tile + RIM, tile + HALO)]).astype(jnp.int32)
    cot = call(ssim_kernel, sds((channels, tile, width), F32), smem=1)(
        edge, image, target, ren_b, tar_b, ren_a, tar_a
    )
    cot_tiles = (
        cot.reshape(channels, tile, strip_tiles, tile).transpose(2, 0, 1, 3).reshape(strip_tiles, channels, pixels)
    )
    slot_sums = call(
        backward_kernel,
        sds((size * SUB, LANES), F32),
        back_scratch(list_len, pixels, slot_count),
    )(coefs, order, segments, cot_tiles, basis_back, phi)
    returned = lax.all_to_all(slot_sums, "dev", split_axis=0, concat_axis=0, tiled=True)
    grads = call(
        home_kernel,
        sds((9, owned_count), F32),
        [pltpu.VMEM((owned_count // wide * 32, wide), F32)],
    )(returned, send_rows, centres, conic, rho, opacity)
    return (image, grads)


def solution(mesh):
    return jax.shard_map(
        shards,
        mesh=mesh,
        in_specs=(
            P("dev", None),
            P("dev", None),
            P(None, "dev"),
            P(None, "dev"),
            P(None, "dev"),
            P(None, "dev"),
            P(None, "dev"),
            P(None, "dev", None),
        ),
        out_specs=(P(None, "dev", None), P(None, "dev")),
        check_vma=False,
    )
```

```python
import functools

import jax
import jax.numpy as jnp
import numpy as np
from jax import lax
from jax.experimental import pallas as pl
from jax.experimental.pallas import tpu as pltpu
from jax.sharding import PartitionSpec as P

LANES = 128
SUB = 8
RIM = 5
HALO = 2 * RIM
LOG2E = 1.4426950408889634
F32 = jnp.float32
BF16 = jnp.bfloat16
NN = (((1,), (0,)), ((), ()))
NT = (((1,), (1,)), ((), ()))
TN = (((0,), (0,)), ((), ()))


def dot(a, b, dims):
    return lax.dot_general(a, b, dims, preferred_element_type=F32)


def pieces(x, count):
    out = []
    for _ in range(count - 1):
        top = x.astype(BF16)
        out.append(top)
        x = x - top.astype(F32)
    out.append(x.astype(BF16))
    return out


def lanes_of(shape):
    return lax.broadcasted_iota(jnp.int32, shape, len(shape) - 1)


def rows_of(shape):
    return lax.broadcasted_iota(jnp.int32, shape, len(shape) - 2)


def pick(table, last, where):
    chunks = table.shape[0]
    lane = jnp.bitwise_and(where, LANES - 1)
    chunk = jnp.right_shift(where, 7)
    lane8 = jnp.broadcast_to(lane, (SUB, LANES))
    chunk8 = jnp.broadcast_to(chunk, (SUB, LANES))
    value = jnp.zeros((SUB, LANES), F32)
    for c in range(chunks):
        got = jnp.take_along_axis(table[c], lane8, axis=1, mode="promise_in_bounds")
        value = jnp.where(chunk8 == c, got, value)
    total = jnp.zeros((SUB, LANES), F32)
    for c in range(0, chunks, SUB):
        got = jnp.take_along_axis(last[c : c + SUB], lane8, axis=1, mode="promise_in_bounds")
        total = total + jnp.where(chunk8 == rows_of((SUB, LANES)) + c, got, 0.0)
    return value, jnp.sum(total, axis=0, keepdims=True)


def pack_kernel(rows_ref, centres, conic, rho, opacity, colors, out_ref, table, last):
    chunks = table.shape[0]
    s = -0.5 * LOG2E
    for c in range(chunks):
        at = slice(c * LANES, (c + 1) * LANES)
        x, y = centres[0:1, at], centres[1:2, at]
        a, d = conic[0:1, at], conic[1:2, at]
        b = rho[0:1, at] * jnp.sqrt(a * d)
        rows = [
            jnp.log(opacity[0:1, at]) * LOG2E + s * (a * x * x + 2.0 * b * x * y + d * y * y),
            -2.0 * s * (a * x + b * y),
            -2.0 * s * (d * y + b * x),
            s * a,
            2.0 * s * b,
            s * d,
            colors[0:1, at],
            colors[1:2, at],
        ]
        table[c] = jnp.concatenate(rows, axis=0)
        last[c : c + 1] = colors[2:3, at]
    half = LANES // 2
    left = lanes_of((SUB, LANES)) < half
    for g in range(rows_ref.shape[1] // LANES):
        where = jnp.maximum(rows_ref[0:1, g * LANES : (g + 1) * LANES], 0)
        value, ninth = pick(table, last, where)
        ninth = jnp.broadcast_to(ninth, (SUB, LANES))
        out_ref[2 * g * SUB : (2 * g + 1) * SUB] = jnp.where(left, value, pltpu.roll(ninth, half, 1))
        out_ref[(2 * g + 1) * SUB : (2 * g + 2) * SUB] = jnp.where(left, pltpu.roll(value, half, 1), ninth)


def part_of(count, most):
    return max(d for d in range(1, most + 1) if count % d == 0)


def shifted(x, by):
    return pltpu.roll(x, by % SUB, 0)


def forward_kernel(recv, idx_ref, basis, img_ref, x_ref, seg_ref, table, last):
    chunks = table.shape[0]
    tiles, pixels = img_ref.shape[0], img_ref.shape[2]
    groups = x_ref.shape[2] // LANES
    half = LANES // 2
    left = lanes_of((SUB, LANES)) < half
    for c in range(chunks):
        a = recv[2 * c * SUB : (2 * c + 1) * SUB]
        b = recv[(2 * c + 1) * SUB : (2 * c + 2) * SUB]
        table[c] = jnp.where(left, a, pltpu.roll(b, half, 1))
        last[c : c + 1] = jnp.where(left, pltpu.roll(a, half, 1), b)[0:1]
    first = rows_of((SUB, LANES)) == 0

    row = rows_of((SUB, pixels))

    def fetch(t, q):
        idx = idx_ref[pl.ds(t * groups + q, 1), :]
        live = idx >= 0
        value, ninth = pick(table, last, jnp.maximum(idx, 0))
        live8 = jnp.broadcast_to(live, (SUB, LANES))
        value = jnp.where(live8, value, jnp.where(first, -1000.0, 0.0))
        ninth = jnp.where(live8, jnp.broadcast_to(ninth, (SUB, LANES)), 0.0)
        p0, p1, p2 = [p.astype(F32) for p in pieces(value, 3)]
        n0, n1, n2 = [p.astype(F32) for p in pieces(ninth, 3)]
        r = rows_of((SUB, LANES))
        n = jnp.where(r == 0, n0, jnp.where(r == 1, n1, jnp.where(r == 2, n2, 0.0)))
        return jnp.concatenate([p0, p1, p2, n], axis=0).astype(BF16)

    def composite(t):
        trans = jnp.ones((SUB, pixels), F32)
        acc = [jnp.zeros((SUB, pixels), F32) for _ in range(3)]
        for q in range(groups):
            x = fetch(t, q)
            x_ref[t, :, q * LANES : (q + 1) * LANES] = x
            out = dot(x, basis[...], TN)
            for i in range(LANES // SUB):
                at = slice(i * SUB, (i + 1) * SUB)
                alpha = jnp.exp2(out[at, :pixels])
                w = alpha * trans
                trans = trans * (1.0 - alpha)
                for ch in range(3):
                    tint = out[at, pixels + ch * LANES : pixels + (ch + 1) * LANES]
                    acc[ch] = acc[ch] + jnp.concatenate([tint] * (pixels // LANES), axis=1) * w
        before = jnp.where(row >= 1, shifted(trans, 1), 1.0)
        for by in (1, 2, 4):
            before = before * jnp.where(row >= by, shifted(before, by), 1.0)
        seg_ref[t, 0:SUB] = before
        seg_ref[t, SUB : 2 * SUB] = trans
        image = []
        for ch in range(3):
            seg_ref[t, (2 + ch) * SUB : (3 + ch) * SUB] = acc[ch]
            image.append(jnp.sum(acc[ch] * before, axis=0, keepdims=True))
        img_ref[t] = jnp.concatenate(image, axis=0)

    def body(i, carry):
        for k in range(par):
            composite(i * par + k)
        return carry

    par = part_of(tiles, 4)
    lax.fori_loop(0, tiles // par, body, 0)


def taps_of():
    m = np.arange(-RIM, RIM + 1)
    w = np.exp(-m * m / 4.5)
    return [float(v) for v in w / w.sum()]


def blur_rows(x, count):
    taps = taps_of()
    width = x.shape[1]
    out = taps[RIM] * x[RIM : RIM + count]
    for m in range(1, RIM + 1):
        out = out + taps[RIM + m] * (x[RIM - m : RIM - m + count] + x[RIM + m : RIM + m + count])
    lane = lanes_of(out.shape)
    res = taps[RIM] * out
    for m in range(1, RIM + 1):
        up = jnp.where(lane >= m, pltpu.roll(out, m, 1), 0.0)
        down = jnp.where(lane < width - m, pltpu.roll(out, width - m, 1), 0.0)
        res = res + taps[RIM + m] * (up + down)
    return res


def ssim_kernel(edge, ren, tar, ren_b, tar_b, ren_a, tar_a, cot_ref):
    rows = ren.shape[1]
    width = ren.shape[2]
    mid = rows + HALO
    r_at = rows_of((mid, width))
    inside = jnp.logical_and(r_at >= edge[0], r_at < edge[1])
    for ch in range(ren.shape[0]):
        r = jnp.concatenate([ren_b[ch], ren[ch], ren_a[ch]], axis=0)
        t = jnp.concatenate([tar_b[ch], tar[ch], tar_a[ch]], axis=0)
        mr, mt = blur_rows(r, mid), blur_rows(t, mid)
        er, et, ert = blur_rows(r * r, mid), blur_rows(t * t, mid), blur_rows(r * t, mid)
        a1 = 2.0 * mr * mt + 0.0001
        a2 = 2.0 * (ert - mr * mt) + 0.0009
        b1 = mr * mr + mt * mt + 0.0001
        b2 = (er - mr * mr) + (et - mt * mt) + 0.0009
        i1, i2 = 1.0 / b1, 1.0 / b2
        s = a1 * a2 * i1 * i2
        d_mr = 2.0 * mt * (a2 - a1) * i1 * i2 - 2.0 * mr * s * (i1 - i2)
        d_er = -s * i2
        d_ert = 2.0 * a1 * i1 * i2
        g0, g1, g2 = [blur_rows(jnp.where(inside, d, 0.0), rows) for d in (d_mr, d_er, d_ert)]
        rc, tc = ren[ch], tar[ch]
        cot_ref[ch] = 1.6 * (rc - tc) - 0.2 * (g0 + 2.0 * rc * g1 + tc * g2)


def spread(values, where, total):
    count = where.shape[1]
    wide = total.shape[1]
    p0, p1, p2 = [p.astype(F32) for p in pieces(values, 3)]
    rows = rows_of((SUB, count))
    tail = jnp.where(rows == 0, p0[SUB:], jnp.where(rows == 1, p1[SUB:], jnp.where(rows == 2, p2[SUB:], 0.0)))
    stacked = jnp.concatenate([p0[:SUB], p1[:SUB], p2[:SUB], tail], axis=0)
    low = jnp.bitwise_and(where, wide - 1)
    high = jnp.where(where < 0, -1, jnp.right_shift(where, wide.bit_length() - 1))
    hot = (jnp.broadcast_to(low, (wide, count)) == rows_of((wide, count))).astype(F32).astype(BF16)
    parts = []
    for c in range(total.shape[0] // 32):
        parts.append(jnp.where(jnp.broadcast_to(high == c, stacked.shape), stacked, 0.0).astype(BF16))
    total[...] += dot(jnp.concatenate(parts, axis=0), hot, NT)


def nine(total, c):
    got = total[c * 32 : (c + 1) * 32]
    return (
        got[0:SUB] + got[SUB : 2 * SUB] + got[2 * SUB : 3 * SUB],
        got[24:25] + got[25:26] + got[26:27],
    )


BLOCK = 16


def backward_kernel(x_ref, idx_ref, seg_ref, cot_ref, basis, phi, out_ref, total, *buffers):
    tiles, pixels = cot_ref.shape[0], cot_ref.shape[2]
    count = x_ref.shape[2]
    groups = count // LANES
    steps = LANES // SUB
    wide = 2 * LANES
    total[...] = jnp.zeros_like(total)
    row = rows_of((SUB, pixels))
    each = 3
    columns = total.shape[1] // 2
    field = jnp.bitwise_and(lanes_of((SUB, LANES)), BLOCK - 1)
    moment = jnp.bitwise_and(lanes_of((count, LANES)), BLOCK - 1) < 6
    block = jnp.right_shift(lanes_of((LANES, LANES)), BLOCK.bit_length() - 1)

    def sweep(t, factors, tints_ref, split):
        cot = [jnp.broadcast_to(cot_ref[t, ch : ch + 1], (SUB, pixels)) for ch in range(3)]
        hi = [c.astype(BF16).astype(F32) for c in cot]
        lo = [c - h for c, h in zip(cot, hi)]

        def place(v):
            body = jnp.where(row == 6, v[0], jnp.where(row == 7, v[1], 0.0))
            return [body, body, body, jnp.where(row < 3, v[2], 0.0)]

        rhs = jnp.concatenate(place(hi) + place(lo), axis=0).astype(BF16)
        rhs = jnp.concatenate([basis[...], rhs], axis=1)
        trans = seg_ref[t, 0:SUB]
        rest = trans * (cot[0] * seg_ref[t, 2 * SUB : 3 * SUB] + cot[1] * seg_ref[t, 3 * SUB : 4 * SUB] + cot[2] * seg_ref[t, 4 * SUB : 5 * SUB])
        for by in (1, 2, 4):
            rest = rest + jnp.where(row < SUB - by, shifted(rest, -by), 0.0)
        for q in range(groups):
            x = x_ref[t, :, q * LANES : (q + 1) * LANES]
            out = dot(jnp.concatenate([x, x], axis=0), rhs, TN)
            for i in range(0, steps, 2):
                hs = []
                for j in (i, i + 1):
                    at = slice(q * LANES + j * SUB, q * LANES + (j + 1) * SUB)
                    alpha = jnp.exp2(out[j * SUB : (j + 1) * SUB, :pixels])
                    w = alpha * trans
                    clear = 1.0 - alpha
                    trans = trans * clear
                    wg = w * out[j * SUB : (j + 1) * SUB, pixels:]
                    rest = rest - wg
                    hs.append(wg - alpha * pl.reciprocal(clear, approx=True) * rest)
                    tints = [jnp.sum(w * c, axis=1, keepdims=True) for c in cot]
                    tints_ref[at] = jnp.where(field == 6, tints[0], jnp.where(field == 7, tints[1], tints[2]))
                at = slice(q * LANES + i * SUB, q * LANES + (i + 2) * SUB)
                for p, v in enumerate(pieces(jnp.concatenate(hs, axis=0), 2)):
                    factors[at, p * pixels : (p + 1) * pixels] = v

    def sums(t, factors, tints_ref, split):
        got = jnp.where(moment, dot(factors[...], phi[...], NN), tints_ref[...])
        where = [idx_ref[pl.ds(t * groups + q, 1), :] for q in range(groups)]
        where = jnp.concatenate(where + [where[0]] * (SUB - groups), axis=0)
        chunk = jnp.transpose(jnp.where(where < 0, -1, jnp.right_shift(where, 8)))
        for q in range(groups):
            at = slice(q * LANES, (q + 1) * LANES)
            mine = jnp.broadcast_to(chunk[:, q : q + 1], (LANES, LANES))
            for base in range(0, columns, LANES):
                kept = jnp.where(mine == block + base // BLOCK, got[at], 0.0)
                top, rest = pieces(kept, 2)
                split[at, base : base + LANES] = top
                split[at, columns + base : columns + base + LANES] = rest

    def scatter(t, factors, tints_ref, split):
        where = jnp.concatenate([idx_ref[pl.ds(t * groups + q, 1), :] for q in range(groups)], axis=1)
        low = jnp.bitwise_and(where, wide - 1)
        hot = (jnp.broadcast_to(low, (wide, count)) == rows_of((wide, count))).astype(F32).astype(BF16)
        total[...] += dot(hot, split[...], NN)

    par = len(buffers) // each

    def body(i, carry):
        for k in range(par):
            now = buffers[each * k : each * (k + 1)]
            last = buffers[each * ((k - 1) % par) :][:each]
            t = i * par + k
            sums(jnp.maximum(t - 1, 0), *last)
            sweep(t, *now)
            scatter(jnp.maximum(t - 1, 0), *last)
        return carry

    buffers[each * (par - 1)][...] = jnp.zeros((count, 2 * pixels), BF16)
    buffers[each * (par - 1) + 1][...] = jnp.zeros((count, LANES), F32)
    lax.fori_loop(0, tiles // par, body, 0)
    sums(tiles - 1, *buffers[each * (par - 1) :])
    scatter(tiles - 1, *buffers[each * (par - 1) :])
    half = LANES // 2
    left = lanes_of((SUB, LANES)) < half
    for c in range(columns // BLOCK):
        if c % SUB == 0:
            at = c // SUB * LANES
            both = total[:, at : at + LANES] + total[:, columns + at : columns + at + LANES]
            turned = jnp.concatenate([jnp.transpose(both[:LANES]), jnp.transpose(both[LANES:])], axis=1)
        got = turned[c % SUB * BLOCK : (c % SUB + 1) * BLOCK]
        eight, ninth = got[:SUB], got[SUB : SUB + 1]
        for j in range(2):
            e = eight[:, j * LANES : (j + 1) * LANES]
            n = jnp.broadcast_to(ninth[:, j * LANES : (j + 1) * LANES], (SUB, LANES))
            at = (c * 2 + j) * 2 * SUB
            out_ref[at : at + SUB] = jnp.where(left, e, pltpu.roll(n, half, 1))
            out_ref[at + SUB : at + 2 * SUB] = jnp.where(left, pltpu.roll(e, half, 1), n)


def home_kernel(recv, rows_ref, centres, conic, rho, opacity, out_ref, total):
    half = LANES // 2
    left = lanes_of((SUB, LANES)) < half
    total[...] = jnp.zeros_like(total)
    step = 4
    for g in range(0, rows_ref.shape[1] // LANES, step):
        eights, ninths = [], []
        for k in range(g, g + step):
            a = recv[2 * k * SUB : (2 * k + 1) * SUB]
            b = recv[(2 * k + 1) * SUB : (2 * k + 2) * SUB]
            eights.append(jnp.where(left, a, pltpu.roll(b, half, 1)))
            n = jnp.where(left, pltpu.roll(a, half, 1), b)
            ninths.append(jnp.broadcast_to(n[0:1], (SUB, LANES)))
        values = jnp.concatenate([jnp.concatenate(eights, axis=1), jnp.concatenate(ninths, axis=1)], axis=0)
        spread(values, rows_ref[0:1, g * LANES : (g + step) * LANES], total)
    wide = total.shape[1]
    for c in range(total.shape[0] // 32):
        m, col2 = nine(total, c)
        at = slice(c * wide, (c + 1) * wide)
        x, y = centres[0:1, at], centres[1:2, at]
        a, d = conic[0:1, at], conic[1:2, at]
        root = jnp.sqrt(a * d)
        b = rho[0:1, at] * root
        m1, mu, mv, muu, muv, mvv = [m[i : i + 1] for i in range(6)]
        dx, dy = mu - x * m1, mv - y * m1
        dxx = muu - 2.0 * x * mu + x * x * m1
        dxy = muv - x * mv - y * mu + x * y * m1
        dyy = mvv - 2.0 * y * mv + y * y * m1
        rows = [
            a * dx + b * dy,
            b * dx + d * dy,
            -0.5 * (dxx + b / a * dxy),
            -0.5 * (dyy + b / d * dxy),
            -root * dxy,
            m1 / opacity[0:1, at],
            m[6:7],
            m[7:8],
            col2,
        ]
        for i, v in enumerate(rows):
            out_ref[i : i + 1, at] = v


def tables(tile, slots):
    pixels = tile * tile
    wide = 2 * LANES
    p = np.arange(pixels)
    v = (p // tile) - (tile - 1) / 2.0
    u = (p % tile) - (tile - 1) / 2.0
    six = np.stack([np.ones(pixels), u, v, u * u, u * v, v * v])
    ahead = np.zeros((32, pixels + 3 * LANES), np.float32)
    back = np.zeros((64, pixels), np.float32)
    for k in range(3):
        ahead[8 * k : 8 * k + 6, :pixels] = six
        back[8 * k : 8 * k + 6, :pixels] = six
        ahead[8 * k + 6, pixels : pixels + LANES] = 1.0
        ahead[8 * k + 7, pixels + LANES : pixels + 2 * LANES] = 1.0
        ahead[24 + k, pixels + 2 * LANES :] = 1.0
    phi = np.zeros((2 * pixels, LANES), np.float32)
    for lane in range(LANES):
        field = lane % BLOCK
        if field < 6:
            phi[:pixels, lane] = six[field]
            phi[pixels:, lane] = six[field]
    return jnp.asarray(ahead, BF16), jnp.asarray(back, BF16), jnp.asarray(phi, BF16)


def back_scratch(list_len, pixels, slots, par):
    columns = slots // (2 * LANES) * BLOCK
    one = [
        pltpu.VMEM((list_len, 2 * pixels), BF16),
        pltpu.VMEM((list_len, LANES), F32),
        pltpu.VMEM((list_len, 2 * columns), BF16),
    ]
    return [pltpu.VMEM((2 * LANES, 2 * columns), F32)] + one * par


def call(kernel, out_shape, scratch=(), smem=0, mib=48):
    n_vmem = pl.BlockSpec()

    def run(*args):
        specs = [pl.BlockSpec(memory_space=pltpu.SMEM) if i < smem else n_vmem for i in range(len(args))]
        return pl.pallas_call(
            kernel,
            out_shape=out_shape,
            in_specs=specs,
            out_specs=jax.tree.map(lambda _: n_vmem, out_shape),
            scratch_shapes=list(scratch),
            compiler_params=pltpu.CompilerParams(vmem_limit_bytes=mib * 1024 * 1024),
        )(*args)

    return run


def swap_edges(value):
    size = lax.axis_size("dev")
    me = lax.axis_index("dev")
    first, last = value[:, :HALO], value[:, -HALO:]
    odd = (me % 2) == 1
    inner = [(i, i ^ 1) for i in range(size)]
    outer = [(i, i + 1) for i in range(1, size - 1, 2)]
    outer = outer + [(j, i) for i, j in outer]
    got_in = lax.ppermute(jnp.where(odd, first, last), "dev", inner)
    got_out = lax.ppermute(jnp.where(odd, last, first), "dev", outer)
    return jnp.where(odd, got_in, got_out), jnp.where(odd, got_out, got_in)


def shards(tile_lists, send_rows, centres, conic, rho, opacity, colors, target):
    slot_count = send_rows.shape[1]
    owned_count = centres.shape[1]
    channels, tile, width = target.shape
    strip_tiles, list_len = tile_lists.shape
    size = lax.axis_size("dev")
    me = lax.axis_index("dev")
    pixels = tile * tile
    chunks = slot_count // LANES
    wide = 2 * LANES
    basis, basis_back, phi = tables(tile, slot_count)
    sds = jax.ShapeDtypeStruct

    packed = call(
        pack_kernel,
        sds((size * SUB, LANES), F32),
        [pltpu.VMEM((owned_count // LANES, SUB, LANES), F32), pltpu.VMEM((owned_count // LANES, LANES), F32)],
        mib=63,
    )(send_rows, centres, conic, rho, opacity, colors)
    received = lax.all_to_all(packed, "dev", split_axis=0, concat_axis=0, tiled=True)

    order = tile_lists.reshape(strip_tiles, SUB, list_len // SUB).transpose(0, 2, 1)
    order = order.reshape(strip_tiles * list_len // LANES, LANES)
    tar_b, tar_a = swap_edges(target)

    colour_tiles, coefs, segments = call(
        forward_kernel,
        (
            sds((strip_tiles, channels, pixels), F32),
            sds((strip_tiles, 32, list_len), BF16),
            sds((strip_tiles, 5 * SUB, pixels), F32),
        ),
        [pltpu.VMEM((chunks, SUB, LANES), F32), pltpu.VMEM((chunks, LANES), F32)],
    )(received, order, basis)
    image = (
        colour_tiles.reshape(strip_tiles, channels, tile, tile).transpose(1, 2, 0, 3).reshape(channels, tile, width)
    )
    ren_b, ren_a = swap_edges(image)
    edge = jnp.stack([jnp.where(me == 0, RIM, 0), jnp.where(me == size - 1, tile + RIM, tile + HALO)]).astype(jnp.int32)
    cot = call(ssim_kernel, sds((channels, tile, width), F32), smem=1)(
        edge, image, target, ren_b, tar_b, ren_a, tar_a
    )
    cot_tiles = (
        cot.reshape(channels, tile, strip_tiles, tile).transpose(2, 0, 1, 3).reshape(strip_tiles, channels, pixels)
    )
    slot_sums = call(
        backward_kernel,
        sds((size * SUB, LANES), F32),
        back_scratch(list_len, pixels, slot_count, part_of(strip_tiles, 6)),
    )(coefs, order, segments, cot_tiles, basis_back, phi)
    returned = lax.all_to_all(slot_sums, "dev", split_axis=0, concat_axis=0, tiled=True)
    grads = call(
        home_kernel,
        sds((9, owned_count), F32),
        [pltpu.VMEM((owned_count // wide * 32, wide), F32)],
    )(returned, send_rows, centres, conic, rho, opacity)
    return (image, grads)


def solution(mesh):
    return jax.shard_map(
        shards,
        mesh=mesh,
        in_specs=(
            P("dev", None),
            P("dev", None),
            P(None, "dev"),
            P(None, "dev"),
            P(None, "dev"),
            P(None, "dev"),
            P(None, "dev"),
            P(None, "dev", None),
        ),
        out_specs=(P(None, "dev", None), P(None, "dev")),
        check_vma=False,
    )
```

```python
import functools

import jax
import jax.numpy as jnp
import numpy as np
from jax import lax
from jax.experimental import pallas as pl
from jax.experimental.pallas import tpu as pltpu
from jax.sharding import PartitionSpec as P

LANES = 128
SUB = 8
RIM = 5
HALO = 2 * RIM
BLOCK = 16
LOG2E = 1.4426950408889634
F32 = jnp.float32
BF16 = jnp.bfloat16
NN = (((1,), (0,)), ((), ()))
NT = (((1,), (1,)), ((), ()))
TN = (((0,), (0,)), ((), ()))


def dot(a, b, dims):
    return lax.dot_general(a, b, dims, preferred_element_type=F32)


def pieces(x, count):
    out = []
    for _ in range(count - 1):
        top = x.astype(BF16)
        out.append(top)
        x = x - top.astype(F32)
    out.append(x.astype(BF16))
    return out


def lanes_of(shape):
    return lax.broadcasted_iota(jnp.int32, shape, len(shape) - 1)


def rows_of(shape):
    return lax.broadcasted_iota(jnp.int32, shape, len(shape) - 2)


def pick(table, last, where):
    chunks = table.shape[0]
    lane = jnp.bitwise_and(where, LANES - 1)
    chunk = jnp.right_shift(where, 7)
    lane8 = jnp.broadcast_to(lane, (SUB, LANES))
    chunk8 = jnp.broadcast_to(chunk, (SUB, LANES))
    value = jnp.zeros((SUB, LANES), F32)
    for c in range(chunks):
        got = jnp.take_along_axis(table[c], lane8, axis=1, mode="promise_in_bounds")
        value = jnp.where(chunk8 == c, got, value)
    total = jnp.zeros((SUB, LANES), F32)
    for c in range(0, chunks, SUB):
        got = jnp.take_along_axis(last[c : c + SUB], lane8, axis=1, mode="promise_in_bounds")
        total = total + jnp.where(chunk8 == rows_of((SUB, LANES)) + c, got, 0.0)
    return value, jnp.sum(total, axis=0, keepdims=True)


def pack_kernel(rows_ref, centres, conic, rho, opacity, colors, out_ref, table, last):
    chunks = table.shape[0]
    s = -0.5 * LOG2E
    for c in range(chunks):
        at = slice(c * LANES, (c + 1) * LANES)
        x, y = centres[0:1, at], centres[1:2, at]
        a, d = conic[0:1, at], conic[1:2, at]
        b = rho[0:1, at] * jnp.sqrt(a * d)
        rows = [
            jnp.log(opacity[0:1, at]) * LOG2E + s * (a * x * x + 2.0 * b * x * y + d * y * y),
            -2.0 * s * (a * x + b * y),
            -2.0 * s * (d * y + b * x),
            s * a,
            2.0 * s * b,
            s * d,
            colors[0:1, at],
            colors[1:2, at],
        ]
        table[c] = jnp.concatenate(rows, axis=0)
        last[c : c + 1] = colors[2:3, at]
    half = LANES // 2
    left = lanes_of((SUB, LANES)) < half
    for g in range(rows_ref.shape[1] // LANES):
        where = jnp.maximum(rows_ref[0:1, g * LANES : (g + 1) * LANES], 0)
        value, ninth = pick(table, last, where)
        ninth = jnp.broadcast_to(ninth, (SUB, LANES))
        out_ref[2 * g * SUB : (2 * g + 1) * SUB] = jnp.where(left, value, pltpu.roll(ninth, half, 1))
        out_ref[(2 * g + 1) * SUB : (2 * g + 2) * SUB] = jnp.where(left, pltpu.roll(value, half, 1), ninth)


def part_of(count, most):
    return max(d for d in range(1, most + 1) if count % d == 0)


def shifted(x, by):
    return pltpu.roll(x, by % SUB, 0)


def forward_kernel(recv, idx_ref, basis, img_ref, x_ref, seg_ref, table):
    tiles, pixels = img_ref.shape[0], img_ref.shape[2]
    groups = x_ref.shape[2] // LANES
    wide = table.shape[1]
    half = LANES // 2
    left = lanes_of((SUB, LANES)) < half
    r = rows_of((SUB, wide))
    for c in range(table.shape[0] // 32):
        eights, ninths = [], []
        for j in range(wide // LANES):
            at = (c * (wide // LANES) + j) * 2 * SUB
            a, b = recv[at : at + SUB], recv[at + SUB : at + 2 * SUB]
            eights.append(jnp.where(left, a, pltpu.roll(b, half, 1)))
            n = jnp.where(left, pltpu.roll(a, half, 1), b)
            ninths.append(jnp.broadcast_to(n[0:1], (SUB, LANES)))
        p = [v.astype(F32) for v in pieces(jnp.concatenate(eights, axis=1), 3)]
        n = [v.astype(F32) for v in pieces(jnp.concatenate(ninths, axis=1), 3)]
        tail = jnp.where(r == 0, n[0], jnp.where(r == 1, n[1], jnp.where(r == 2, n[2], 0.0)))
        table[c * 32 : (c + 1) * 32] = jnp.concatenate(p + [tail], axis=0).astype(BF16)
    row = rows_of((SUB, pixels))

    def fetch(t):
        per = wide // LANES
        for q in range(0, groups, per):
            idx = jnp.concatenate([idx_ref[pl.ds(t * groups + q + j, 1), :] for j in range(per)], axis=1)
            low = jnp.broadcast_to(jnp.bitwise_and(idx, wide - 1), (wide, wide))
            hot = (low == rows_of((wide, wide))).astype(F32).astype(BF16)
            got = dot(table[...], hot, NN)
            chunk = jnp.where(idx < 0, -1, jnp.right_shift(idx, wide.bit_length() - 1))
            chunk = jnp.broadcast_to(chunk, (32, wide))
            x = jnp.where(jnp.logical_and(chunk < 0, rows_of((32, wide)) == 0), -1000.0, 0.0)
            for c in range(table.shape[0] // 32):
                x = jnp.where(chunk == c, got[c * 32 : (c + 1) * 32], x)
            x_ref[t, :, q * LANES : (q + per) * LANES] = x.astype(BF16)

    def composite(t):
        trans = jnp.ones((SUB, pixels), F32)
        acc = [jnp.zeros((SUB, pixels), F32) for _ in range(3)]
        for q in range(groups):
            out = dot(x_ref[t, :, q * LANES : (q + 1) * LANES], basis[...], TN)
            for i in range(LANES // SUB):
                at = slice(i * SUB, (i + 1) * SUB)
                alpha = jnp.exp2(out[at, :pixels])
                w = alpha * trans
                trans = trans * (1.0 - alpha)
                for ch in range(3):
                    tint = out[at, pixels + ch * LANES : pixels + (ch + 1) * LANES]
                    acc[ch] = acc[ch] + jnp.concatenate([tint] * (pixels // LANES), axis=1) * w
        before = jnp.where(row >= 1, shifted(trans, 1), 1.0)
        for by in (1, 2, 4):
            before = before * jnp.where(row >= by, shifted(before, by), 1.0)
        seg_ref[t, 0:SUB] = before
        seg_ref[t, SUB : 2 * SUB] = trans
        image = []
        for ch in range(3):
            seg_ref[t, (2 + ch) * SUB : (3 + ch) * SUB] = acc[ch]
            image.append(jnp.sum(acc[ch] * before, axis=0, keepdims=True))
        img_ref[t] = jnp.concatenate(image, axis=0)

    def body(i, carry):
        for k in range(par):
            fetch(i * par + k)
        for k in range(par):
            composite(i * par + k)
        return carry

    par = part_of(tiles, 4)
    lax.fori_loop(0, tiles // par, body, 0)


def exact(a, b):
    return sum(dot(a[i], b[j], NN) for i in range(3) for j in range(3 - i))


def blur(images, rows, cols):
    height = rows.shape[0] // 3
    done = []
    for x in images:
        got = dot(rows[...], jnp.concatenate(pieces(x, 3), axis=0), NN)
        done.append(got[:height] + got[height : 2 * height] + got[2 * height :])
    stacked = jnp.concatenate(done, axis=0)
    out = exact(pieces(stacked, 3), [cols[k] for k in range(3)])
    return [out[i * height : (i + 1) * height] for i in range(len(images))]


def padded(own, before, after, ch):
    fill = jnp.zeros((-HALO % SUB, own.shape[2]), F32)
    return jnp.concatenate([own[ch], before[ch], fill, after[ch], fill], axis=0)


def target_kernel(tar, tar_b, tar_a, rows, cols, out_ref):
    channels = tar.shape[0]
    images = [padded(tar, tar_b, tar_a, ch) for ch in range(channels)]
    for i, v in enumerate(blur(images + [x * x for x in images], rows, cols)):
        out_ref[i] = v


def ssim_kernel(edge, ren, tar, ren_b, tar_b, ren_a, tar_a, known, rows, back, cols, cot_ref):
    channels, height, width = ren.shape
    r_at = rows_of((rows.shape[0] // 3, width))
    inside = jnp.logical_and(r_at >= edge[0], r_at < edge[1])
    ren_s = [padded(ren, ren_b, ren_a, ch) for ch in range(channels)]
    tar_s = [padded(tar, tar_b, tar_a, ch) for ch in range(channels)]
    found = blur(ren_s + [x * x for x in ren_s] + [x * y for x, y in zip(ren_s, tar_s)], rows, cols)
    fields = []
    for ch in range(channels):
        mr, er, ert = found[ch], found[channels + ch], found[2 * channels + ch]
        mt, et = known[ch], known[channels + ch]
        a1 = 2.0 * mr * mt + 0.0001
        a2 = 2.0 * (ert - mr * mt) + 0.0009
        b1 = mr * mr + mt * mt + 0.0001
        b2 = (er - mr * mr) + (et - mt * mt) + 0.0009
        i1, i2 = 1.0 / b1, 1.0 / b2
        s = a1 * a2 * i1 * i2
        d_mr = 2.0 * mt * (a2 - a1) * i1 * i2 - 2.0 * mr * s * (i1 - i2)
        d_er = -s * i2
        d_ert = 2.0 * a1 * i1 * i2
        fields += [jnp.where(inside, d, 0.0) for d in (d_mr, d_er, d_ert)]
    pulled = blur(fields, back, cols)
    for ch in range(channels):
        g0, g1, g2 = pulled[3 * ch : 3 * ch + 3]
        rc, tc = ren[ch], tar[ch]
        cot_ref[ch] = 1.6 * (rc - tc) - 0.2 * (g0 + 2.0 * rc * g1 + tc * g2)


def parts_of(matrix):
    out = []
    rest = matrix.astype(np.float32)
    for _ in range(3):
        top = rest.astype(jnp.bfloat16)
        out.append(top)
        rest = rest - top.astype(np.float32)
    return jnp.asarray(np.stack(out))


def blur_tables(height, width):
    m = np.arange(-RIM, RIM + 1)
    taps = np.exp(-m * m / 4.5)
    taps = taps / taps.sum()
    side = HALO + (-HALO % SUB)
    place = [height + i for i in range(HALO)] + list(range(height)) + [height + side + i for i in range(HALO)]
    mid = height + HALO
    tall = mid + (-mid % SUB)
    rows = np.zeros((tall, height + 2 * side))
    back = np.zeros((height, tall))
    cols = np.zeros((width, width))
    for k, tap in enumerate(taps):
        for i in range(mid):
            rows[i, place[i + k]] = tap
        for i in range(height):
            back[i, i + k] = tap
        for i in range(width):
            if 0 <= i + k - RIM < width:
                cols[i + k - RIM, i] = tap

    def stack(matrix):
        p = parts_of(matrix)
        none = jnp.zeros_like(p[0])
        sides = [[p[i] if i + j < 3 else none for j in range(3)] for i in range(3)]
        return jnp.concatenate([jnp.concatenate(side, axis=1) for side in sides], axis=0)

    return stack(rows), stack(back), parts_of(cols)


def spread(values, where, total):
    count = where.shape[1]
    wide = total.shape[1]
    p0, p1, p2 = [p.astype(F32) for p in pieces(values, 3)]
    rows = rows_of((SUB, count))
    tail = jnp.where(rows == 0, p0[SUB:], jnp.where(rows == 1, p1[SUB:], jnp.where(rows == 2, p2[SUB:], 0.0)))
    stacked = jnp.concatenate([p0[:SUB], p1[:SUB], p2[:SUB], tail], axis=0)
    low = jnp.bitwise_and(where, wide - 1)
    high = jnp.where(where < 0, -1, jnp.right_shift(where, wide.bit_length() - 1))
    hot = (jnp.broadcast_to(low, (wide, count)) == rows_of((wide, count))).astype(F32).astype(BF16)
    parts = []
    for c in range(total.shape[0] // 32):
        parts.append(jnp.where(jnp.broadcast_to(high == c, stacked.shape), stacked, 0.0).astype(BF16))
    total[...] += dot(jnp.concatenate(parts, axis=0), hot, NT)


def nine(total, c):
    got = total[c * 32 : (c + 1) * 32]
    return (
        got[0:SUB] + got[SUB : 2 * SUB] + got[2 * SUB : 3 * SUB],
        got[24:25] + got[25:26] + got[26:27],
    )


def backward_kernel(x_ref, idx_ref, seg_ref, cot_ref, basis, phi, out_ref, total, *buffers):
    tiles, pixels = cot_ref.shape[0], cot_ref.shape[2]
    count = x_ref.shape[2]
    groups = count // LANES
    steps = LANES // SUB
    wide = 2 * LANES
    total[...] = jnp.zeros_like(total)
    row = rows_of((SUB, pixels))
    each = 3
    columns = total.shape[1] // 2
    field = jnp.bitwise_and(lanes_of((SUB, LANES)), BLOCK - 1)
    moment = jnp.bitwise_and(lanes_of((count, LANES)), BLOCK - 1) < 6
    block = jnp.right_shift(lanes_of((LANES, LANES)), BLOCK.bit_length() - 1)

    def sweep(t, factors, tints_ref, split):
        cot = [jnp.broadcast_to(cot_ref[t, ch : ch + 1], (SUB, pixels)) for ch in range(3)]
        hi = [c.astype(BF16).astype(F32) for c in cot]
        lo = [c - h for c, h in zip(cot, hi)]

        def place(v):
            body = jnp.where(row == 6, v[0], jnp.where(row == 7, v[1], 0.0))
            return [body, body, body, jnp.where(row < 3, v[2], 0.0)]

        rhs = jnp.concatenate(place(hi) + place(lo), axis=0).astype(BF16)
        rhs = jnp.concatenate([basis[...], rhs], axis=1)
        trans = seg_ref[t, 0:SUB]
        rest = trans * (cot[0] * seg_ref[t, 2 * SUB : 3 * SUB] + cot[1] * seg_ref[t, 3 * SUB : 4 * SUB] + cot[2] * seg_ref[t, 4 * SUB : 5 * SUB])
        for by in (1, 2, 4):
            rest = rest + jnp.where(row < SUB - by, shifted(rest, -by), 0.0)
        for q in range(groups):
            x = x_ref[t, :, q * LANES : (q + 1) * LANES]
            out = dot(jnp.concatenate([x, x], axis=0), rhs, TN)
            for i in range(0, steps, 2):
                hs = []
                for j in (i, i + 1):
                    at = slice(q * LANES + j * SUB, q * LANES + (j + 1) * SUB)
                    alpha = jnp.exp2(out[j * SUB : (j + 1) * SUB, :pixels])
                    w = alpha * trans
                    clear = 1.0 - alpha
                    trans = trans * clear
                    wg = w * out[j * SUB : (j + 1) * SUB, pixels:]
                    rest = rest - wg
                    hs.append(wg - alpha * pl.reciprocal(clear, approx=True) * rest)
                    tints = [jnp.sum(w * c, axis=1, keepdims=True) for c in cot]
                    tints_ref[at] = jnp.where(field == 6, tints[0], jnp.where(field == 7, tints[1], tints[2]))
                at = slice(q * LANES + i * SUB, q * LANES + (i + 2) * SUB)
                for p, v in enumerate(pieces(jnp.concatenate(hs, axis=0), 2)):
                    factors[at, p * pixels : (p + 1) * pixels] = v

    def sums(t, factors, tints_ref, split):
        got = jnp.where(moment, dot(factors[...], phi[...], NN), tints_ref[...])
        where = [idx_ref[pl.ds(t * groups + q, 1), :] for q in range(groups)]
        where = jnp.concatenate(where + [where[0]] * (SUB - groups), axis=0)
        chunk = jnp.transpose(jnp.where(where < 0, -1, jnp.right_shift(where, 8)))
        for q in range(groups):
            at = slice(q * LANES, (q + 1) * LANES)
            mine = jnp.broadcast_to(chunk[:, q : q + 1], (LANES, LANES))
            for base in range(0, columns, LANES):
                kept = jnp.where(mine == block + base // BLOCK, got[at], 0.0)
                top, rest = pieces(kept, 2)
                split[at, base : base + LANES] = top
                split[at, columns + base : columns + base + LANES] = rest

    def scatter(t, factors, tints_ref, split):
        where = jnp.concatenate([idx_ref[pl.ds(t * groups + q, 1), :] for q in range(groups)], axis=1)
        low = jnp.bitwise_and(where, wide - 1)
        hot = (jnp.broadcast_to(low, (wide, count)) == rows_of((wide, count))).astype(F32).astype(BF16)
        total[...] += dot(hot, split[...], NN)

    par = len(buffers) // each

    def body(i, carry):
        for k in range(par):
            now = buffers[each * k : each * (k + 1)]
            last = buffers[each * ((k - 1) % par) :][:each]
            t = i * par + k
            sums(jnp.maximum(t - 1, 0), *last)
            sweep(t, *now)
            scatter(jnp.maximum(t - 1, 0), *last)
        return carry

    buffers[each * (par - 1)][...] = jnp.zeros((count, 2 * pixels), BF16)
    buffers[each * (par - 1) + 1][...] = jnp.zeros((count, LANES), F32)
    lax.fori_loop(0, tiles // par, body, 0)
    sums(tiles - 1, *buffers[each * (par - 1) :])
    scatter(tiles - 1, *buffers[each * (par - 1) :])
    half = LANES // 2
    left = lanes_of((SUB, LANES)) < half
    for c in range(columns // BLOCK):
        if c % SUB == 0:
            at = c // SUB * LANES
            both = total[:, at : at + LANES] + total[:, columns + at : columns + at + LANES]
            turned = jnp.concatenate([jnp.transpose(both[:LANES]), jnp.transpose(both[LANES:])], axis=1)
        got = turned[c % SUB * BLOCK : (c % SUB + 1) * BLOCK]
        eight, ninth = got[:SUB], got[SUB : SUB + 1]
        for j in range(2):
            e = eight[:, j * LANES : (j + 1) * LANES]
            n = jnp.broadcast_to(ninth[:, j * LANES : (j + 1) * LANES], (SUB, LANES))
            at = (c * 2 + j) * 2 * SUB
            out_ref[at : at + SUB] = jnp.where(left, e, pltpu.roll(n, half, 1))
            out_ref[at + SUB : at + 2 * SUB] = jnp.where(left, pltpu.roll(e, half, 1), n)


def home_kernel(recv, rows_ref, centres, conic, rho, opacity, out_ref, total):
    half = LANES // 2
    left = lanes_of((SUB, LANES)) < half
    total[...] = jnp.zeros_like(total)
    step = 4
    for g in range(0, rows_ref.shape[1] // LANES, step):
        eights, ninths = [], []
        for k in range(g, g + step):
            a = recv[2 * k * SUB : (2 * k + 1) * SUB]
            b = recv[(2 * k + 1) * SUB : (2 * k + 2) * SUB]
            eights.append(jnp.where(left, a, pltpu.roll(b, half, 1)))
            n = jnp.where(left, pltpu.roll(a, half, 1), b)
            ninths.append(jnp.broadcast_to(n[0:1], (SUB, LANES)))
        values = jnp.concatenate([jnp.concatenate(eights, axis=1), jnp.concatenate(ninths, axis=1)], axis=0)
        spread(values, rows_ref[0:1, g * LANES : (g + step) * LANES], total)
    wide = total.shape[1]
    for c in range(total.shape[0] // 32):
        m, col2 = nine(total, c)
        at = slice(c * wide, (c + 1) * wide)
        x, y = centres[0:1, at], centres[1:2, at]
        a, d = conic[0:1, at], conic[1:2, at]
        root = jnp.sqrt(a * d)
        b = rho[0:1, at] * root
        m1, mu, mv, muu, muv, mvv = [m[i : i + 1] for i in range(6)]
        dx, dy = mu - x * m1, mv - y * m1
        dxx = muu - 2.0 * x * mu + x * x * m1
        dxy = muv - x * mv - y * mu + x * y * m1
        dyy = mvv - 2.0 * y * mv + y * y * m1
        rows = [
            a * dx + b * dy,
            b * dx + d * dy,
            -0.5 * (dxx + b / a * dxy),
            -0.5 * (dyy + b / d * dxy),
            -root * dxy,
            m1 / opacity[0:1, at],
            m[6:7],
            m[7:8],
            col2,
        ]
        for i, v in enumerate(rows):
            out_ref[i : i + 1, at] = v


def tables(tile, slots):
    pixels = tile * tile
    wide = 2 * LANES
    p = np.arange(pixels)
    v = (p // tile) - (tile - 1) / 2.0
    u = (p % tile) - (tile - 1) / 2.0
    six = np.stack([np.ones(pixels), u, v, u * u, u * v, v * v])
    ahead = np.zeros((32, pixels + 3 * LANES), np.float32)
    back = np.zeros((64, pixels), np.float32)
    for k in range(3):
        ahead[8 * k : 8 * k + 6, :pixels] = six
        back[8 * k : 8 * k + 6, :pixels] = six
        ahead[8 * k + 6, pixels : pixels + LANES] = 1.0
        ahead[8 * k + 7, pixels + LANES : pixels + 2 * LANES] = 1.0
        ahead[24 + k, pixels + 2 * LANES :] = 1.0
    phi = np.zeros((2 * pixels, LANES), np.float32)
    for lane in range(LANES):
        field = lane % BLOCK
        if field < 6:
            phi[:pixels, lane] = six[field]
            phi[pixels:, lane] = six[field]
    return jnp.asarray(ahead, BF16), jnp.asarray(back, BF16), jnp.asarray(phi, BF16)


def back_scratch(list_len, pixels, slots, par):
    columns = slots // (2 * LANES) * BLOCK
    one = [
        pltpu.VMEM((list_len, 2 * pixels), BF16),
        pltpu.VMEM((list_len, LANES), F32),
        pltpu.VMEM((list_len, 2 * columns), BF16),
    ]
    return [pltpu.VMEM((2 * LANES, 2 * columns), F32)] + one * par


def call(kernel, out_shape, scratch=(), smem=0, mib=48):
    n_vmem = pl.BlockSpec()

    def run(*args):
        specs = [pl.BlockSpec(memory_space=pltpu.SMEM) if i < smem else n_vmem for i in range(len(args))]
        return pl.pallas_call(
            kernel,
            out_shape=out_shape,
            in_specs=specs,
            out_specs=jax.tree.map(lambda _: n_vmem, out_shape),
            scratch_shapes=list(scratch),
            compiler_params=pltpu.CompilerParams(vmem_limit_bytes=mib * 1024 * 1024),
        )(*args)

    return run


def swap_edges(value):
    size = lax.axis_size("dev")
    me = lax.axis_index("dev")
    first, last = value[:, :HALO], value[:, -HALO:]
    odd = (me % 2) == 1
    inner = [(i, i ^ 1) for i in range(size)]
    outer = [(i, i + 1) for i in range(1, size - 1, 2)]
    outer = outer + [(j, i) for i, j in outer]
    got_in = lax.ppermute(jnp.where(odd, first, last), "dev", inner)
    got_out = lax.ppermute(jnp.where(odd, last, first), "dev", outer)
    return jnp.where(odd, got_in, got_out), jnp.where(odd, got_out, got_in)


def shards(tile_lists, send_rows, centres, conic, rho, opacity, colors, target):
    slot_count = send_rows.shape[1]
    owned_count = centres.shape[1]
    channels, tile, width = target.shape
    strip_tiles, list_len = tile_lists.shape
    size = lax.axis_size("dev")
    me = lax.axis_index("dev")
    pixels = tile * tile
    wide = 2 * LANES
    basis, basis_back, phi = tables(tile, slot_count)
    sds = jax.ShapeDtypeStruct

    packed = call(
        pack_kernel,
        sds((size * SUB, LANES), F32),
        [pltpu.VMEM((owned_count // LANES, SUB, LANES), F32), pltpu.VMEM((owned_count // LANES, LANES), F32)],
        mib=63,
    )(send_rows, centres, conic, rho, opacity, colors)
    received = lax.all_to_all(packed, "dev", split_axis=0, concat_axis=0, tiled=True)

    order = tile_lists.reshape(strip_tiles, SUB, list_len // SUB).transpose(0, 2, 1)
    order = order.reshape(strip_tiles * list_len // LANES, LANES)
    tar_b, tar_a = swap_edges(target)
    rows, back, cols = blur_tables(tile, width)
    known = call(target_kernel, sds((2 * channels, rows.shape[0] // 3, width), F32))(target, tar_b, tar_a, rows, cols)

    colour_tiles, coefs, segments = call(
        forward_kernel,
        (
            sds((strip_tiles, channels, pixels), F32),
            sds((strip_tiles, 32, list_len), BF16),
            sds((strip_tiles, 5 * SUB, pixels), F32),
        ),
        [pltpu.VMEM((slot_count // wide * 32, wide), BF16)],
    )(received, order, basis)
    image = (
        colour_tiles.reshape(strip_tiles, channels, tile, tile).transpose(1, 2, 0, 3).reshape(channels, tile, width)
    )
    ren_b, ren_a = swap_edges(image)
    edge = jnp.stack([jnp.where(me == 0, RIM, 0), jnp.where(me == size - 1, tile + RIM, tile + HALO)]).astype(jnp.int32)
    cot = call(ssim_kernel, sds((channels, tile, width), F32), smem=1)(
        edge, image, target, ren_b, tar_b, ren_a, tar_a, known, rows, back, cols
    )
    cot_tiles = (
        cot.reshape(channels, tile, strip_tiles, tile).transpose(2, 0, 1, 3).reshape(strip_tiles, channels, pixels)
    )
    slot_sums = call(
        backward_kernel,
        sds((size * SUB, LANES), F32),
        back_scratch(list_len, pixels, slot_count, part_of(strip_tiles, 6)),
    )(coefs, order, segments, cot_tiles, basis_back, phi)
    returned = lax.all_to_all(slot_sums, "dev", split_axis=0, concat_axis=0, tiled=True)
    grads = call(
        home_kernel,
        sds((9, owned_count), F32),
        [pltpu.VMEM((owned_count // wide * 32, wide), F32)],
    )(returned, send_rows, centres, conic, rho, opacity)
    return (image, grads)


def solution(mesh):
    return jax.shard_map(
        shards,
        mesh=mesh,
        in_specs=(
            P("dev", None),
            P("dev", None),
            P(None, "dev"),
            P(None, "dev"),
            P(None, "dev"),
            P(None, "dev"),
            P(None, "dev"),
            P(None, "dev", None),
        ),
        out_specs=(P(None, "dev", None), P(None, "dev")),
        check_vma=False,
    )
```

```python
import functools

import jax
import jax.numpy as jnp
import numpy as np
from jax import lax
from jax.experimental import pallas as pl
from jax.experimental.pallas import tpu as pltpu
from jax.sharding import PartitionSpec as P

LANES = 128
SUB = 8
RIM = 5
HALO = 2 * RIM
BLOCK = 16
LOG2E = 1.4426950408889634
F32 = jnp.float32
BF16 = jnp.bfloat16
NN = (((1,), (0,)), ((), ()))
NT = (((1,), (1,)), ((), ()))
TN = (((0,), (0,)), ((), ()))


def dot(a, b, dims):
    return lax.dot_general(a, b, dims, preferred_element_type=F32)


def pieces(x, count):
    out = []
    for _ in range(count - 1):
        top = x.astype(BF16)
        out.append(top)
        x = x - top.astype(F32)
    out.append(x.astype(BF16))
    return out


def lanes_of(shape):
    return lax.broadcasted_iota(jnp.int32, shape, len(shape) - 1)


def rows_of(shape):
    return lax.broadcasted_iota(jnp.int32, shape, len(shape) - 2)


def fill(table, c, eight, ninth):
    p = [v.astype(F32) for v in pieces(eight, 3)]
    n = [v.astype(F32) for v in pieces(jnp.broadcast_to(ninth, eight.shape), 3)]
    r = rows_of(eight.shape)
    tail = jnp.where(r == 0, n[0], jnp.where(r == 1, n[1], jnp.where(r == 2, n[2], 0.0)))
    table[c * 32 : (c + 1) * 32] = jnp.concatenate(p + [tail], axis=0).astype(BF16)


def choose(table, idx, none):
    wide = table.shape[1]
    low = jnp.broadcast_to(jnp.bitwise_and(idx, wide - 1), (wide, wide))
    hot = (low == rows_of((wide, wide))).astype(F32).astype(BF16)
    got = dot(table[...], hot, NN)
    chunk = jnp.where(idx < 0, -1, jnp.right_shift(idx, wide.bit_length() - 1))
    chunk = jnp.broadcast_to(chunk, (32, wide))
    x = none
    for c in range(table.shape[0] // 32):
        x = jnp.where(chunk == c, got[c * 32 : (c + 1) * 32], x)
    return x


def pack_kernel(rows_ref, centres, conic, rho, opacity, colors, out_ref, table):
    wide = table.shape[1]
    s = -0.5 * LOG2E
    for c in range(table.shape[0] // 32):
        at = slice(c * wide, (c + 1) * wide)
        x, y = centres[0:1, at], centres[1:2, at]
        a, d = conic[0:1, at], conic[1:2, at]
        b = rho[0:1, at] * jnp.sqrt(a * d)
        rows = [
            jnp.log(opacity[0:1, at]) * LOG2E + s * (a * x * x + 2.0 * b * x * y + d * y * y),
            -2.0 * s * (a * x + b * y),
            -2.0 * s * (d * y + b * x),
            s * a,
            2.0 * s * b,
            s * d,
            colors[0:1, at],
            colors[1:2, at],
        ]
        fill(table, c, jnp.concatenate(rows, axis=0), colors[2:3, at])
    half = LANES // 2
    left = lanes_of((SUB, LANES)) < half
    none = jnp.zeros((32, wide), F32)
    for g in range(rows_ref.shape[1] // wide):
        x = choose(table, rows_ref[0:1, g * wide : (g + 1) * wide], none)
        eight = x[0:SUB] + x[SUB : 2 * SUB] + x[2 * SUB : 3 * SUB]
        ninth = jnp.broadcast_to(x[24:25] + x[25:26] + x[26:27], (SUB, wide))
        for j in range(wide // LANES):
            e, n = [v[:, j * LANES : (j + 1) * LANES] for v in (eight, ninth)]
            at = (g * (wide // LANES) + j) * 2 * SUB
            out_ref[at : at + SUB] = jnp.where(left, e, pltpu.roll(n, half, 1))
            out_ref[at + SUB : at + 2 * SUB] = jnp.where(left, pltpu.roll(e, half, 1), n)


def part_of(count, most):
    return max(d for d in range(1, most + 1) if count % d == 0)


def shifted(x, by):
    return pltpu.roll(x, by % SUB, 0)


def forward_kernel(recv, idx_ref, basis, img_ref, x_ref, seg_ref, table):
    tiles, pixels = img_ref.shape[0], img_ref.shape[2]
    groups = x_ref.shape[2] // LANES
    wide = table.shape[1]
    half = LANES // 2
    left = lanes_of((SUB, LANES)) < half
    for c in range(table.shape[0] // 32):
        eights, ninths = [], []
        for j in range(wide // LANES):
            at = (c * (wide // LANES) + j) * 2 * SUB
            a, b = recv[at : at + SUB], recv[at + SUB : at + 2 * SUB]
            eights.append(jnp.where(left, a, pltpu.roll(b, half, 1)))
            n = jnp.where(left, pltpu.roll(a, half, 1), b)
            ninths.append(n[0:1])
        fill(table, c, jnp.concatenate(eights, axis=1), jnp.concatenate(ninths, axis=1))
    none = jnp.where(rows_of((32, wide)) == 0, -1000.0, 0.0)
    row = rows_of((SUB, pixels))

    def fetch(t):
        per = wide // LANES
        for q in range(0, groups, per):
            idx = jnp.concatenate([idx_ref[pl.ds(t * groups + q + j, 1), :] for j in range(per)], axis=1)
            x = choose(table, idx, none)
            x_ref[t, :, q * LANES : (q + per) * LANES] = x.astype(BF16)

    def composite(t):
        trans = jnp.ones((SUB, pixels), F32)
        acc = [jnp.zeros((SUB, pixels), F32) for _ in range(3)]
        for q in range(groups):
            out = dot(x_ref[t, :, q * LANES : (q + 1) * LANES], basis[...], TN)
            for i in range(LANES // SUB):
                at = slice(i * SUB, (i + 1) * SUB)
                alpha = jnp.exp2(out[at, :pixels])
                w = alpha * trans
                trans = trans * (1.0 - alpha)
                for ch in range(3):
                    tint = out[at, pixels + ch * LANES : pixels + (ch + 1) * LANES]
                    acc[ch] = acc[ch] + jnp.concatenate([tint] * (pixels // LANES), axis=1) * w
        before = jnp.where(row >= 1, shifted(trans, 1), 1.0)
        for by in (1, 2, 4):
            before = before * jnp.where(row >= by, shifted(before, by), 1.0)
        seg_ref[t, 0:SUB] = before
        seg_ref[t, SUB : 2 * SUB] = trans
        image = []
        for ch in range(3):
            seg_ref[t, (2 + ch) * SUB : (3 + ch) * SUB] = acc[ch]
            image.append(jnp.sum(acc[ch] * before, axis=0, keepdims=True))
        img_ref[t] = jnp.concatenate(image, axis=0)

    def body(i, carry):
        for k in range(par):
            fetch(i * par + k)
        for k in range(par):
            composite(i * par + k)
        return carry

    par = part_of(tiles, 4)
    lax.fori_loop(0, tiles // par, body, 0)


def exact(a, b):
    return sum(dot(a[i], b[j], NN) for i in range(3) for j in range(3 - i))


def blur(images, rows, cols):
    height = rows.shape[0] // 3
    done = []
    for x in images:
        got = dot(rows, jnp.concatenate(pieces(x, 3), axis=0), NN)
        done.append(got[:height] + got[height : 2 * height] + got[2 * height :])
    stacked = jnp.concatenate(done, axis=0)
    out = exact(pieces(stacked, 3), [cols[k] for k in range(3)])
    return [out[i * height : (i + 1) * height] for i in range(len(images))]


def padded(own, before, after, ch):
    fill = jnp.zeros((-HALO % SUB, own.shape[2]), F32)
    return jnp.concatenate([own[ch], before[ch], fill, after[ch], fill], axis=0)


def target_kernel(tar, tar_b, tar_a, rows_back, cols, out_ref):
    rows = rows_back[: 3 * out_ref.shape[1]]
    channels = tar.shape[0]
    images = [padded(tar, tar_b, tar_a, ch) for ch in range(channels)]
    for i, v in enumerate(blur(images + [x * x for x in images], rows, cols)):
        out_ref[i] = v


def ssim_kernel(edge, ren, tar, ren_b, tar_b, ren_a, tar_a, known, rows_back, cols, cot_ref):
    channels, height, width = ren.shape
    tall = known.shape[1]
    rows = rows_back[: 3 * tall]
    back = rows_back[3 * tall :, : 3 * tall]
    r_at = rows_of((tall, width))
    inside = jnp.logical_and(r_at >= edge[0], r_at < edge[1])
    ren_s = [padded(ren, ren_b, ren_a, ch) for ch in range(channels)]
    tar_s = [padded(tar, tar_b, tar_a, ch) for ch in range(channels)]
    found = blur(ren_s + [x * x for x in ren_s] + [x * y for x, y in zip(ren_s, tar_s)], rows, cols)
    fields = []
    for ch in range(channels):
        mr, er, ert = found[ch], found[channels + ch], found[2 * channels + ch]
        mt, et = known[ch], known[channels + ch]
        a1 = 2.0 * mr * mt + 0.0001
        a2 = 2.0 * (ert - mr * mt) + 0.0009
        b1 = mr * mr + mt * mt + 0.0001
        b2 = (er - mr * mr) + (et - mt * mt) + 0.0009
        i1, i2 = 1.0 / b1, 1.0 / b2
        s = a1 * a2 * i1 * i2
        d_mr = 2.0 * mt * (a2 - a1) * i1 * i2 - 2.0 * mr * s * (i1 - i2)
        d_er = -s * i2
        d_ert = 2.0 * a1 * i1 * i2
        fields += [jnp.where(inside, d, 0.0) for d in (d_mr, d_er, d_ert)]
    pulled = blur(fields, back, cols)
    for ch in range(channels):
        g0, g1, g2 = pulled[3 * ch : 3 * ch + 3]
        rc, tc = ren[ch], tar[ch]
        cot_ref[ch] = 1.6 * (rc - tc) - 0.2 * (g0 + 2.0 * rc * g1 + tc * g2)


def parts_of(matrix):
    out = []
    rest = matrix.astype(np.float32)
    for _ in range(3):
        top = rest.astype(jnp.bfloat16)
        out.append(top)
        rest = rest - top.astype(np.float32)
    return jnp.asarray(np.stack(out))


def blur_tables(height, width):
    m = np.arange(-RIM, RIM + 1)
    taps = np.exp(-m * m / 4.5)
    taps = taps / taps.sum()
    side = HALO + (-HALO % SUB)
    place = [height + i for i in range(HALO)] + list(range(height)) + [height + side + i for i in range(HALO)]
    mid = height + HALO
    tall = mid + (-mid % SUB)
    rows = np.zeros((tall, height + 2 * side))
    back = np.zeros((height, tall))
    cols = np.zeros((width, width))
    for k, tap in enumerate(taps):
        for i in range(mid):
            rows[i, place[i + k]] = tap
        for i in range(height):
            back[i, i + k] = tap
        for i in range(width):
            if 0 <= i + k - RIM < width:
                cols[i + k - RIM, i] = tap

    def stack(matrix):
        p = parts_of(matrix)
        none = jnp.zeros_like(p[0])
        sides = [[p[i] if i + j < 3 else none for j in range(3)] for i in range(3)]
        return jnp.concatenate([jnp.concatenate(side, axis=1) for side in sides], axis=0)

    down, up = stack(rows), stack(back)
    up = jnp.pad(up, ((0, 0), (0, down.shape[1] - up.shape[1])))
    return jnp.concatenate([down, up], axis=0), parts_of(cols)


def spread(values, where, total):
    count = where.shape[1]
    wide = total.shape[1]
    p0, p1, p2 = [p.astype(F32) for p in pieces(values, 3)]
    rows = rows_of((SUB, count))
    tail = jnp.where(rows == 0, p0[SUB:], jnp.where(rows == 1, p1[SUB:], jnp.where(rows == 2, p2[SUB:], 0.0)))
    stacked = jnp.concatenate([p0[:SUB], p1[:SUB], p2[:SUB], tail], axis=0)
    low = jnp.bitwise_and(where, wide - 1)
    high = jnp.where(where < 0, -1, jnp.right_shift(where, wide.bit_length() - 1))
    hot = (jnp.broadcast_to(low, (wide, count)) == rows_of((wide, count))).astype(F32).astype(BF16)
    parts = []
    for c in range(total.shape[0] // 32):
        parts.append(jnp.where(jnp.broadcast_to(high == c, stacked.shape), stacked, 0.0).astype(BF16))
    total[...] += dot(jnp.concatenate(parts, axis=0), hot, NT)


def nine(total, c):
    got = total[c * 32 : (c + 1) * 32]
    return (
        got[0:SUB] + got[SUB : 2 * SUB] + got[2 * SUB : 3 * SUB],
        got[24:25] + got[25:26] + got[26:27],
    )


def backward_kernel(x_ref, idx_ref, seg_ref, cot_ref, ahead, out_ref, total, phi, *buffers):
    tiles, pixels = cot_ref.shape[0], cot_ref.shape[2]
    count = x_ref.shape[2]
    groups = count // LANES
    steps = LANES // SUB
    wide = 2 * LANES
    total[...] = jnp.zeros_like(total)
    row = rows_of((SUB, pixels))
    each = 3
    columns = total.shape[1] // 2
    field = jnp.bitwise_and(lanes_of((SUB, LANES)), BLOCK - 1)
    basis = jnp.concatenate([ahead[:, :pixels], jnp.zeros((32, pixels), BF16)], axis=0)
    side = int(pixels**0.5)
    kind = jnp.bitwise_and(lanes_of((pixels, LANES)), BLOCK - 1)
    spot = rows_of((pixels, LANES))
    down = jnp.right_shift(spot, side.bit_length() - 1)
    u = (spot - down * side).astype(F32) - (side - 1) / 2.0
    v = down.astype(F32) - (side - 1) / 2.0
    six = jnp.zeros((pixels, LANES), F32)
    for i, f in enumerate((jnp.ones_like(u), u, v, u * u, u * v, v * v)):
        six = jnp.where(kind == i, f, six)
    phi[:pixels] = six.astype(BF16)
    phi[pixels:] = six.astype(BF16)
    moment = jnp.bitwise_and(lanes_of((count, LANES)), BLOCK - 1) < 6
    block = jnp.right_shift(lanes_of((LANES, LANES)), BLOCK.bit_length() - 1)

    def sweep(t, factors, tints_ref, split):
        cot = [jnp.broadcast_to(cot_ref[t, ch : ch + 1], (SUB, pixels)) for ch in range(3)]
        hi = [c.astype(BF16).astype(F32) for c in cot]
        lo = [c - h for c, h in zip(cot, hi)]

        def place(v):
            body = jnp.where(row == 6, v[0], jnp.where(row == 7, v[1], 0.0))
            return [body, body, body, jnp.where(row < 3, v[2], 0.0)]

        rhs = jnp.concatenate(place(hi) + place(lo), axis=0).astype(BF16)
        rhs = jnp.concatenate([basis, rhs], axis=1)
        trans = seg_ref[t, 0:SUB]
        rest = trans * (cot[0] * seg_ref[t, 2 * SUB : 3 * SUB] + cot[1] * seg_ref[t, 3 * SUB : 4 * SUB] + cot[2] * seg_ref[t, 4 * SUB : 5 * SUB])
        for by in (1, 2, 4):
            rest = rest + jnp.where(row < SUB - by, shifted(rest, -by), 0.0)
        for q in range(groups):
            x = x_ref[t, :, q * LANES : (q + 1) * LANES]
            out = dot(jnp.concatenate([x, x], axis=0), rhs, TN)
            for i in range(0, steps, 2):
                hs = []
                for j in (i, i + 1):
                    at = slice(q * LANES + j * SUB, q * LANES + (j + 1) * SUB)
                    alpha = jnp.exp2(out[j * SUB : (j + 1) * SUB, :pixels])
                    w = alpha * trans
                    clear = 1.0 - alpha
                    trans = trans * clear
                    wg = w * out[j * SUB : (j + 1) * SUB, pixels:]
                    rest = rest - wg
                    hs.append(wg - alpha * pl.reciprocal(clear, approx=True) * rest)
                    tints = [jnp.sum(w * c, axis=1, keepdims=True) for c in cot]
                    tints_ref[at] = jnp.where(field == 6, tints[0], jnp.where(field == 7, tints[1], tints[2]))
                at = slice(q * LANES + i * SUB, q * LANES + (i + 2) * SUB)
                for p, v in enumerate(pieces(jnp.concatenate(hs, axis=0), 2)):
                    factors[at, p * pixels : (p + 1) * pixels] = v

    def sums(t, factors, tints_ref, split):
        got = jnp.where(moment, dot(factors[...], phi[...], NN), tints_ref[...])
        where = [idx_ref[pl.ds(t * groups + q, 1), :] for q in range(groups)]
        where = jnp.concatenate(where + [where[0]] * (SUB - groups), axis=0)
        chunk = jnp.transpose(jnp.where(where < 0, -1, jnp.right_shift(where, 8)))
        for q in range(groups):
            at = slice(q * LANES, (q + 1) * LANES)
            mine = jnp.broadcast_to(chunk[:, q : q + 1], (LANES, LANES))
            for base in range(0, columns, LANES):
                kept = jnp.where(mine == block + base // BLOCK, got[at], 0.0)
                top, rest = pieces(kept, 2)
                split[at, base : base + LANES] = top
                split[at, columns + base : columns + base + LANES] = rest

    def scatter(t, factors, tints_ref, split):
        where = jnp.concatenate([idx_ref[pl.ds(t * groups + q, 1), :] for q in range(groups)], axis=1)
        low = jnp.bitwise_and(where, wide - 1)
        hot = (jnp.broadcast_to(low, (wide, count)) == rows_of((wide, count))).astype(F32).astype(BF16)
        total[...] += dot(hot, split[...], NN)

    par = len(buffers) // each

    def body(i, carry):
        for k in range(par):
            now = buffers[each * k : each * (k + 1)]
            last = buffers[each * ((k - 1) % par) :][:each]
            t = i * par + k
            sums(jnp.maximum(t - 1, 0), *last)
            sweep(t, *now)
            scatter(jnp.maximum(t - 1, 0), *last)
        return carry

    buffers[each * (par - 1)][...] = jnp.zeros((count, 2 * pixels), BF16)
    buffers[each * (par - 1) + 1][...] = jnp.zeros((count, LANES), F32)
    lax.fori_loop(0, tiles // par, body, 0)
    sums(tiles - 1, *buffers[each * (par - 1) :])
    scatter(tiles - 1, *buffers[each * (par - 1) :])
    half = LANES // 2
    left = lanes_of((SUB, LANES)) < half
    for c in range(columns // BLOCK):
        if c % SUB == 0:
            at = c // SUB * LANES
            both = total[:, at : at + LANES] + total[:, columns + at : columns + at + LANES]
            turned = jnp.concatenate([jnp.transpose(both[:LANES]), jnp.transpose(both[LANES:])], axis=1)
        got = turned[c % SUB * BLOCK : (c % SUB + 1) * BLOCK]
        eight, ninth = got[:SUB], got[SUB : SUB + 1]
        for j in range(2):
            e = eight[:, j * LANES : (j + 1) * LANES]
            n = jnp.broadcast_to(ninth[:, j * LANES : (j + 1) * LANES], (SUB, LANES))
            at = (c * 2 + j) * 2 * SUB
            out_ref[at : at + SUB] = jnp.where(left, e, pltpu.roll(n, half, 1))
            out_ref[at + SUB : at + 2 * SUB] = jnp.where(left, pltpu.roll(e, half, 1), n)


def home_kernel(recv, rows_ref, centres, conic, rho, opacity, out_ref, total):
    half = LANES // 2
    left = lanes_of((SUB, LANES)) < half
    total[...] = jnp.zeros_like(total)
    step = 4
    for g in range(0, rows_ref.shape[1] // LANES, step):
        eights, ninths = [], []
        for k in range(g, g + step):
            a = recv[2 * k * SUB : (2 * k + 1) * SUB]
            b = recv[(2 * k + 1) * SUB : (2 * k + 2) * SUB]
            eights.append(jnp.where(left, a, pltpu.roll(b, half, 1)))
            n = jnp.where(left, pltpu.roll(a, half, 1), b)
            ninths.append(jnp.broadcast_to(n[0:1], (SUB, LANES)))
        values = jnp.concatenate([jnp.concatenate(eights, axis=1), jnp.concatenate(ninths, axis=1)], axis=0)
        spread(values, rows_ref[0:1, g * LANES : (g + step) * LANES], total)
    wide = total.shape[1]
    for c in range(total.shape[0] // 32):
        m, col2 = nine(total, c)
        at = slice(c * wide, (c + 1) * wide)
        x, y = centres[0:1, at], centres[1:2, at]
        a, d = conic[0:1, at], conic[1:2, at]
        root = jnp.sqrt(a * d)
        b = rho[0:1, at] * root
        m1, mu, mv, muu, muv, mvv = [m[i : i + 1] for i in range(6)]
        dx, dy = mu - x * m1, mv - y * m1
        dxx = muu - 2.0 * x * mu + x * x * m1
        dxy = muv - x * mv - y * mu + x * y * m1
        dyy = mvv - 2.0 * y * mv + y * y * m1
        rows = [
            a * dx + b * dy,
            b * dx + d * dy,
            -0.5 * (dxx + b / a * dxy),
            -0.5 * (dyy + b / d * dxy),
            -root * dxy,
            m1 / opacity[0:1, at],
            m[6:7],
            m[7:8],
            col2,
        ]
        for i, v in enumerate(rows):
            out_ref[i : i + 1, at] = v


def tables(tile):
    pixels = tile * tile
    p = np.arange(pixels)
    v = (p // tile) - (tile - 1) / 2.0
    u = (p % tile) - (tile - 1) / 2.0
    six = np.stack([np.ones(pixels), u, v, u * u, u * v, v * v])
    ahead = np.zeros((32, pixels + 3 * LANES), np.float32)
    for k in range(3):
        ahead[8 * k : 8 * k + 6, :pixels] = six
        ahead[8 * k + 6, pixels : pixels + LANES] = 1.0
        ahead[8 * k + 7, pixels + LANES : pixels + 2 * LANES] = 1.0
        ahead[24 + k, pixels + 2 * LANES :] = 1.0
    return jnp.asarray(ahead, BF16)


def back_scratch(list_len, pixels, slots, par):
    columns = slots // (2 * LANES) * BLOCK
    one = [
        pltpu.VMEM((list_len, 2 * pixels), BF16),
        pltpu.VMEM((list_len, LANES), F32),
        pltpu.VMEM((list_len, 2 * columns), BF16),
    ]
    return [pltpu.VMEM((2 * LANES, 2 * columns), F32), pltpu.VMEM((2 * pixels, LANES), BF16)] + one * par


def call(kernel, out_shape, scratch=(), smem=0, mib=48):
    n_vmem = pl.BlockSpec()

    def run(*args):
        specs = [pl.BlockSpec(memory_space=pltpu.SMEM) if i < smem else n_vmem for i in range(len(args))]
        return pl.pallas_call(
            kernel,
            out_shape=out_shape,
            in_specs=specs,
            out_specs=jax.tree.map(lambda _: n_vmem, out_shape),
            scratch_shapes=list(scratch),
            compiler_params=pltpu.CompilerParams(vmem_limit_bytes=mib * 1024 * 1024),
        )(*args)

    return run


def swap_edges(value):
    size = lax.axis_size("dev")
    me = lax.axis_index("dev")
    first, last = value[:, :HALO], value[:, -HALO:]
    odd = (me % 2) == 1
    inner = [(i, i ^ 1) for i in range(size)]
    outer = [(i, i + 1) for i in range(1, size - 1, 2)]
    outer = outer + [(j, i) for i, j in outer]
    got_in = lax.ppermute(jnp.where(odd, first, last), "dev", inner)
    got_out = lax.ppermute(jnp.where(odd, last, first), "dev", outer)
    return jnp.where(odd, got_in, got_out), jnp.where(odd, got_out, got_in)


def shards(tile_lists, send_rows, centres, conic, rho, opacity, colors, target):
    slot_count = send_rows.shape[1]
    owned_count = centres.shape[1]
    channels, tile, width = target.shape
    strip_tiles, list_len = tile_lists.shape
    size = lax.axis_size("dev")
    me = lax.axis_index("dev")
    pixels = tile * tile
    wide = 2 * LANES
    basis = tables(tile)
    sds = jax.ShapeDtypeStruct

    packed = call(
        pack_kernel,
        sds((size * SUB, LANES), F32),
        [pltpu.VMEM((owned_count // wide * 32, wide), BF16)],
        mib=63,
    )(send_rows, centres, conic, rho, opacity, colors)
    received = lax.all_to_all(packed, "dev", split_axis=0, concat_axis=0, tiled=True)

    order = tile_lists.reshape(strip_tiles, SUB, list_len // SUB).transpose(0, 2, 1)
    order = order.reshape(strip_tiles * list_len // LANES, LANES)
    tar_b, tar_a = swap_edges(target)
    rows_back, cols = blur_tables(tile, width)
    tall = rows_back.shape[0] // 3 - tile
    known = call(target_kernel, sds((2 * channels, tall, width), F32))(target, tar_b, tar_a, rows_back, cols)

    colour_tiles, coefs, segments = call(
        forward_kernel,
        (
            sds((strip_tiles, channels, pixels), F32),
            sds((strip_tiles, 32, list_len), BF16),
            sds((strip_tiles, 5 * SUB, pixels), F32),
        ),
        [pltpu.VMEM((slot_count // wide * 32, wide), BF16)],
    )(received, order, basis)
    image = (
        colour_tiles.reshape(strip_tiles, channels, tile, tile).transpose(1, 2, 0, 3).reshape(channels, tile, width)
    )
    ren_b, ren_a = swap_edges(image)
    edge = jnp.stack([jnp.where(me == 0, RIM, 0), jnp.where(me == size - 1, tile + RIM, tile + HALO)]).astype(jnp.int32)
    cot = call(ssim_kernel, sds((channels, tile, width), F32), smem=1)(
        edge, image, target, ren_b, tar_b, ren_a, tar_a, known, rows_back, cols
    )
    cot_tiles = (
        cot.reshape(channels, tile, strip_tiles, tile).transpose(2, 0, 1, 3).reshape(strip_tiles, channels, pixels)
    )
    slot_sums = call(
        backward_kernel,
        sds((size * SUB, LANES), F32),
        back_scratch(list_len, pixels, slot_count, part_of(strip_tiles, 6)),
    )(coefs, order, segments, cot_tiles, basis)
    returned = lax.all_to_all(slot_sums, "dev", split_axis=0, concat_axis=0, tiled=True)
    grads = call(
        home_kernel,
        sds((9, owned_count), F32),
        [pltpu.VMEM((owned_count // wide * 32, wide), F32)],
    )(returned, send_rows, centres, conic, rho, opacity)
    return (image, grads)


def solution(mesh):
    return jax.shard_map(
        shards,
        mesh=mesh,
        in_specs=(
            P("dev", None),
            P("dev", None),
            P(None, "dev"),
            P(None, "dev"),
            P(None, "dev"),
            P(None, "dev"),
            P(None, "dev"),
            P(None, "dev", None),
        ),
        out_specs=(P(None, "dev", None), P(None, "dev")),
        check_vma=False,
    )
```

```python
import functools

import jax
import jax.numpy as jnp
import numpy as np
from jax import lax
from jax.experimental import pallas as pl
from jax.experimental.pallas import tpu as pltpu
from jax.sharding import PartitionSpec as P

LANES = 128
SUB = 8
RIM = 5
HALO = 2 * RIM
BLOCK = 16
LOG2E = 1.4426950408889634
F32 = jnp.float32
BF16 = jnp.bfloat16
NN = (((1,), (0,)), ((), ()))
NT = (((1,), (1,)), ((), ()))
TN = (((0,), (0,)), ((), ()))


def dot(a, b, dims):
    return lax.dot_general(a, b, dims, preferred_element_type=F32)


def pieces(x, count):
    out = []
    for _ in range(count - 1):
        top = x.astype(BF16)
        out.append(top)
        x = x - top.astype(F32)
    out.append(x.astype(BF16))
    return out


def lanes_of(shape):
    return lax.broadcasted_iota(jnp.int32, shape, len(shape) - 1)


def rows_of(shape):
    return lax.broadcasted_iota(jnp.int32, shape, len(shape) - 2)


def fill(table, c, eight, ninth):
    p = [v.astype(F32) for v in pieces(eight, 3)]
    n = [v.astype(F32) for v in pieces(jnp.broadcast_to(ninth, eight.shape), 3)]
    r = rows_of(eight.shape)
    tail = jnp.where(r == 0, n[0], jnp.where(r == 1, n[1], jnp.where(r == 2, n[2], 0.0)))
    table[c * 32 : (c + 1) * 32] = jnp.concatenate(p + [tail], axis=0).astype(BF16)


def choose(table, idx, none):
    wide = table.shape[1]
    low = jnp.broadcast_to(jnp.bitwise_and(idx, wide - 1), (wide, wide))
    hot = (low == rows_of((wide, wide))).astype(F32).astype(BF16)
    got = dot(table[...], hot, NN)
    chunk = jnp.where(idx < 0, -1, jnp.right_shift(idx, wide.bit_length() - 1))
    chunk = jnp.broadcast_to(chunk, (32, wide))
    x = none
    for c in range(table.shape[0] // 32):
        x = jnp.where(chunk == c, got[c * 32 : (c + 1) * 32], x)
    return x


def pack_kernel(rows_ref, centres, conic, rho, opacity, colors, out_ref, table):
    wide = table.shape[1]
    s = -0.5 * LOG2E
    for c in range(table.shape[0] // 32):
        at = slice(c * wide, (c + 1) * wide)
        x, y = centres[0:1, at], centres[1:2, at]
        a, d = conic[0:1, at], conic[1:2, at]
        b = rho[0:1, at] * jnp.sqrt(a * d)
        rows = [
            jnp.log(opacity[0:1, at]) * LOG2E + s * (a * x * x + 2.0 * b * x * y + d * y * y),
            -2.0 * s * (a * x + b * y),
            -2.0 * s * (d * y + b * x),
            s * a,
            2.0 * s * b,
            s * d,
            colors[0:1, at],
            colors[1:2, at],
        ]
        fill(table, c, jnp.concatenate(rows, axis=0), colors[2:3, at])
    half = LANES // 2
    left = lanes_of((SUB, LANES)) < half
    none = jnp.zeros((32, wide), F32)
    for g in range(rows_ref.shape[1] // wide):
        x = choose(table, rows_ref[0:1, g * wide : (g + 1) * wide], none)
        eight = x[0:SUB] + x[SUB : 2 * SUB] + x[2 * SUB : 3 * SUB]
        ninth = jnp.broadcast_to(x[24:25] + x[25:26] + x[26:27], (SUB, wide))
        for j in range(wide // LANES):
            e, n = [v[:, j * LANES : (j + 1) * LANES] for v in (eight, ninth)]
            at = (g * (wide // LANES) + j) * 2 * SUB
            out_ref[at : at + SUB] = jnp.where(left, e, pltpu.roll(n, half, 1))
            out_ref[at + SUB : at + 2 * SUB] = jnp.where(left, pltpu.roll(e, half, 1), n)


def part_of(count, most):
    return max(d for d in range(1, most + 1) if count % d == 0)


def shifted(x, by):
    return pltpu.roll(x, by % SUB, 0)


def forward_kernel(recv, idx_ref, basis, img_ref, x_ref, seg_ref, table):
    tiles, pixels = img_ref.shape[0], img_ref.shape[2]
    groups = x_ref.shape[2] // LANES
    wide = table.shape[1]
    half = LANES // 2
    left = lanes_of((SUB, LANES)) < half
    for c in range(table.shape[0] // 32):
        eights, ninths = [], []
        for j in range(wide // LANES):
            at = (c * (wide // LANES) + j) * 2 * SUB
            a, b = recv[at : at + SUB], recv[at + SUB : at + 2 * SUB]
            eights.append(jnp.where(left, a, pltpu.roll(b, half, 1)))
            n = jnp.where(left, pltpu.roll(a, half, 1), b)
            ninths.append(n[0:1])
        fill(table, c, jnp.concatenate(eights, axis=1), jnp.concatenate(ninths, axis=1))
    none = jnp.where(rows_of((32, wide)) == 0, -1000.0, 0.0)
    row = rows_of((SUB, pixels))

    def fetch(t):
        per = wide // LANES
        for q in range(0, groups, per):
            idx = jnp.concatenate([idx_ref[pl.ds(t * groups + q + j, 1), :] for j in range(per)], axis=1)
            x = choose(table, idx, none)
            x_ref[t, :, q * LANES : (q + per) * LANES] = x.astype(BF16)

    def composite(t):
        trans = jnp.ones((SUB, pixels), F32)
        acc = [jnp.zeros((SUB, pixels), F32) for _ in range(3)]
        for q in range(groups):
            out = dot(x_ref[t, :, q * LANES : (q + 1) * LANES], basis[...], TN)
            for i in range(LANES // SUB):
                at = slice(i * SUB, (i + 1) * SUB)
                alpha = jnp.exp2(out[at, :pixels])
                w = alpha * trans
                trans = trans * (1.0 - alpha)
                for ch in range(3):
                    tint = out[at, pixels + ch * LANES : pixels + (ch + 1) * LANES]
                    acc[ch] = acc[ch] + jnp.concatenate([tint] * (pixels // LANES), axis=1) * w
        before = jnp.where(row >= 1, shifted(trans, 1), 1.0)
        for by in (1, 2, 4):
            before = before * jnp.where(row >= by, shifted(before, by), 1.0)
        seg_ref[t, 0:SUB] = before
        seg_ref[t, SUB : 2 * SUB] = trans
        image = []
        for ch in range(3):
            seg_ref[t, (2 + ch) * SUB : (3 + ch) * SUB] = acc[ch]
            image.append(jnp.sum(acc[ch] * before, axis=0, keepdims=True))
        img_ref[t] = jnp.concatenate(image, axis=0)

    def body(i, carry):
        for k in range(par):
            fetch(i * par + k)
        for k in range(par):
            composite(i * par + k)
        return carry

    par = part_of(tiles, 6)
    lax.fori_loop(0, tiles // par, body, 0)


def exact(a, b):
    return sum(dot(a[i], b[j], NN) for i in range(3) for j in range(3 - i))


def blur(images, rows, cols):
    height = rows.shape[0] // 3
    done = []
    for x in images:
        got = dot(rows, jnp.concatenate(pieces(x, 3), axis=0), NN)
        done.append(got[:height] + got[height : 2 * height] + got[2 * height :])
    stacked = jnp.concatenate(done, axis=0)
    parts = pieces(stacked, 3)
    width = stacked.shape[1]
    out = []
    for low in range(0, width, 2 * LANES):
        high = min(low + 2 * LANES, width)
        first = max(low - RIM, 0) // LANES * LANES
        end = min(-(-(high + RIM) // LANES) * LANES, width)
        out.append(exact([p[:, first:end] for p in parts], [cols[k, first:end, low:high] for k in range(3)]))
    out = jnp.concatenate(out, axis=1)
    return [out[i * height : (i + 1) * height] for i in range(len(images))]


def padded(own, before, after, ch):
    fill = jnp.zeros((-HALO % SUB, own.shape[2]), F32)
    return jnp.concatenate([own[ch], before[ch], fill, after[ch], fill], axis=0)


def target_kernel(tar, tar_b, tar_a, rows_back, cols, out_ref):
    rows = rows_back[: 3 * out_ref.shape[1]]
    channels = tar.shape[0]
    images = [padded(tar, tar_b, tar_a, ch) for ch in range(channels)]
    for i, v in enumerate(blur(images + [x * x for x in images], rows, cols)):
        out_ref[i] = v


def ssim_kernel(edge, ren, tar, ren_b, tar_b, ren_a, tar_a, known, rows_back, cols, cot_ref):
    channels, height, width = ren.shape
    tall = known.shape[1]
    rows = rows_back[: 3 * tall]
    back = rows_back[3 * tall :, : 3 * tall]
    r_at = rows_of((tall, width))
    inside = jnp.logical_and(r_at >= edge[0], r_at < edge[1])
    ren_s = [padded(ren, ren_b, ren_a, ch) for ch in range(channels)]
    tar_s = [padded(tar, tar_b, tar_a, ch) for ch in range(channels)]
    found = blur(ren_s + [x * x for x in ren_s] + [x * y for x, y in zip(ren_s, tar_s)], rows, cols)
    fields = []
    for ch in range(channels):
        mr, er, ert = found[ch], found[channels + ch], found[2 * channels + ch]
        mt, et = known[ch], known[channels + ch]
        a1 = 2.0 * mr * mt + 0.0001
        a2 = 2.0 * (ert - mr * mt) + 0.0009
        b1 = mr * mr + mt * mt + 0.0001
        b2 = (er - mr * mr) + (et - mt * mt) + 0.0009
        i1, i2 = 1.0 / b1, 1.0 / b2
        s = a1 * a2 * i1 * i2
        d_mr = 2.0 * mt * (a2 - a1) * i1 * i2 - 2.0 * mr * s * (i1 - i2)
        d_er = -s * i2
        d_ert = 2.0 * a1 * i1 * i2
        fields += [jnp.where(inside, d, 0.0) for d in (d_mr, d_er, d_ert)]
    pulled = blur(fields, back, cols)
    for ch in range(channels):
        g0, g1, g2 = pulled[3 * ch : 3 * ch + 3]
        rc, tc = ren[ch], tar[ch]
        cot_ref[ch] = 1.6 * (rc - tc) - 0.2 * (g0 + 2.0 * rc * g1 + tc * g2)


def parts_of(matrix):
    out = []
    rest = matrix.astype(np.float32)
    for _ in range(3):
        top = rest.astype(jnp.bfloat16)
        out.append(top)
        rest = rest - top.astype(np.float32)
    return jnp.asarray(np.stack(out))


def blur_tables(height, width):
    m = np.arange(-RIM, RIM + 1)
    taps = np.exp(-m * m / 4.5)
    taps = taps / taps.sum()
    side = HALO + (-HALO % SUB)
    place = [height + i for i in range(HALO)] + list(range(height)) + [height + side + i for i in range(HALO)]
    mid = height + HALO
    tall = mid + (-mid % SUB)
    rows = np.zeros((tall, height + 2 * side))
    back = np.zeros((height, tall))
    cols = np.zeros((width, width))
    for k, tap in enumerate(taps):
        for i in range(mid):
            rows[i, place[i + k]] = tap
        for i in range(height):
            back[i, i + k] = tap
        for i in range(width):
            if 0 <= i + k - RIM < width:
                cols[i + k - RIM, i] = tap

    def stack(matrix):
        p = parts_of(matrix)
        none = jnp.zeros_like(p[0])
        sides = [[p[i] if i + j < 3 else none for j in range(3)] for i in range(3)]
        return jnp.concatenate([jnp.concatenate(side, axis=1) for side in sides], axis=0)

    down, up = stack(rows), stack(back)
    up = jnp.pad(up, ((0, 0), (0, down.shape[1] - up.shape[1])))
    return jnp.concatenate([down, up], axis=0), parts_of(cols)


def spread(values, where, total):
    count = where.shape[1]
    wide = total.shape[1]
    p0, p1, p2 = [p.astype(F32) for p in pieces(values, 3)]
    rows = rows_of((SUB, count))
    tail = jnp.where(rows == 0, p0[SUB:], jnp.where(rows == 1, p1[SUB:], jnp.where(rows == 2, p2[SUB:], 0.0)))
    stacked = jnp.concatenate([p0[:SUB], p1[:SUB], p2[:SUB], tail], axis=0)
    low = jnp.bitwise_and(where, wide - 1)
    high = jnp.where(where < 0, -1, jnp.right_shift(where, wide.bit_length() - 1))
    hot = (jnp.broadcast_to(low, (wide, count)) == rows_of((wide, count))).astype(F32).astype(BF16)
    parts = []
    for c in range(total.shape[0] // 32):
        parts.append(jnp.where(jnp.broadcast_to(high == c, stacked.shape), stacked, 0.0).astype(BF16))
    total[...] += dot(jnp.concatenate(parts, axis=0), hot, NT)


def nine(total, c):
    got = total[c * 32 : (c + 1) * 32]
    return (
        got[0:SUB] + got[SUB : 2 * SUB] + got[2 * SUB : 3 * SUB],
        got[24:25] + got[25:26] + got[26:27],
    )


def backward_kernel(x_ref, idx_ref, seg_ref, cot_ref, ahead, out_ref, total, phi, *buffers):
    tiles, pixels = cot_ref.shape[0], cot_ref.shape[2]
    count = x_ref.shape[2]
    groups = count // LANES
    steps = LANES // SUB
    wide = 2 * LANES
    total[...] = jnp.zeros_like(total)
    row = rows_of((SUB, pixels))
    each = 3
    columns = total.shape[1] // 2
    field = jnp.bitwise_and(lanes_of((SUB, LANES)), BLOCK - 1)
    basis = jnp.concatenate([ahead[:, :pixels], jnp.zeros((32, pixels), BF16)], axis=0)
    side = int(pixels**0.5)
    kind = jnp.bitwise_and(lanes_of((pixels, LANES)), BLOCK - 1)
    spot = rows_of((pixels, LANES))
    down = jnp.right_shift(spot, side.bit_length() - 1)
    u = (spot - down * side).astype(F32) - (side - 1) / 2.0
    v = down.astype(F32) - (side - 1) / 2.0
    six = jnp.zeros((pixels, LANES), F32)
    for i, f in enumerate((jnp.ones_like(u), u, v, u * u, u * v, v * v)):
        six = jnp.where(kind == i, f, six)
    phi[:pixels] = six.astype(BF16)
    phi[pixels:] = six.astype(BF16)
    moment = jnp.bitwise_and(lanes_of((count, LANES)), BLOCK - 1) < 6
    block = jnp.right_shift(lanes_of((LANES, LANES)), BLOCK.bit_length() - 1)

    def sweep(t, factors, tints_ref, split):
        cot = [jnp.broadcast_to(cot_ref[t, ch : ch + 1], (SUB, pixels)) for ch in range(3)]
        hi = [c.astype(BF16).astype(F32) for c in cot]
        lo = [c - h for c, h in zip(cot, hi)]

        def place(v):
            body = jnp.where(row == 6, v[0], jnp.where(row == 7, v[1], 0.0))
            return [body, body, body, jnp.where(row < 3, v[2], 0.0)]

        rhs = jnp.concatenate(place(hi) + place(lo), axis=0).astype(BF16)
        rhs = jnp.concatenate([basis, rhs], axis=1)
        trans = seg_ref[t, 0:SUB]
        rest = trans * (cot[0] * seg_ref[t, 2 * SUB : 3 * SUB] + cot[1] * seg_ref[t, 3 * SUB : 4 * SUB] + cot[2] * seg_ref[t, 4 * SUB : 5 * SUB])
        for by in (1, 2, 4):
            rest = rest + jnp.where(row < SUB - by, shifted(rest, -by), 0.0)
        for q in range(groups):
            x = x_ref[t, :, q * LANES : (q + 1) * LANES]
            out = dot(jnp.concatenate([x, x], axis=0), rhs, TN)
            for i in range(0, steps, 2):
                hs = []
                for j in (i, i + 1):
                    at = slice(q * LANES + j * SUB, q * LANES + (j + 1) * SUB)
                    alpha = jnp.exp2(out[j * SUB : (j + 1) * SUB, :pixels])
                    w = alpha * trans
                    clear = 1.0 - alpha
                    trans = trans * clear
                    wg = w * out[j * SUB : (j + 1) * SUB, pixels:]
                    rest = rest - wg
                    hs.append(wg - alpha * pl.reciprocal(clear, approx=True) * rest)
                    tints = [jnp.sum(w * c, axis=1, keepdims=True) for c in cot]
                    tints_ref[at] = jnp.where(field == 6, tints[0], jnp.where(field == 7, tints[1], tints[2]))
                at = slice(q * LANES + i * SUB, q * LANES + (i + 2) * SUB)
                for p, v in enumerate(pieces(jnp.concatenate(hs, axis=0), 2)):
                    factors[at, p * pixels : (p + 1) * pixels] = v

    def sums(t, factors, tints_ref, split):
        got = jnp.where(moment, dot(factors[...], phi[...], NN), tints_ref[...])
        where = [idx_ref[pl.ds(t * groups + q, 1), :] for q in range(groups)]
        words = []
        for q, idx in enumerate(where):
            if q % 4 == 0:
                words.append(jnp.zeros((1, LANES), jnp.int32))
            words[-1] = words[-1] | jnp.left_shift(jnp.where(idx < 0, 255, jnp.right_shift(idx, 8)), 8 * (q % 4))
        words = jnp.transpose(jnp.concatenate(words + [words[0]] * (SUB - len(words)), axis=0))
        for q in range(groups):
            at = slice(q * LANES, (q + 1) * LANES)
            if q % 4 == 0:
                word = jnp.broadcast_to(words[:, q // 4 : q // 4 + 1], (LANES, LANES))
            mine = word & jnp.left_shift(jnp.full((LANES, LANES), 255, jnp.int32), 8 * (q % 4))
            for base in range(0, columns, LANES):
                kept = jnp.where(mine == jnp.left_shift(block + base // BLOCK, 8 * (q % 4)), got[at], 0.0)
                top, rest = pieces(kept, 2)
                split[at, base : base + LANES] = top
                split[at, columns + base : columns + base + LANES] = rest

    def scatter(t, factors, tints_ref, split):
        where = jnp.concatenate([idx_ref[pl.ds(t * groups + q, 1), :] for q in range(groups)], axis=1)
        low = jnp.bitwise_and(where, wide - 1)
        hot = (jnp.broadcast_to(low, (wide, count)) == rows_of((wide, count))).astype(F32).astype(BF16)
        total[...] += dot(hot, split[...], NN)

    par = len(buffers) // each

    def body(i, carry):
        for k in range(par):
            now = buffers[each * k : each * (k + 1)]
            last = buffers[each * ((k - 1) % par) :][:each]
            t = i * par + k
            sums(jnp.maximum(t - 1, 0), *last)
            sweep(t, *now)
            scatter(jnp.maximum(t - 1, 0), *last)
        return carry

    buffers[each * (par - 1)][...] = jnp.zeros((count, 2 * pixels), BF16)
    buffers[each * (par - 1) + 1][...] = jnp.zeros((count, LANES), F32)
    lax.fori_loop(0, tiles // par, body, 0)
    sums(tiles - 1, *buffers[each * (par - 1) :])
    scatter(tiles - 1, *buffers[each * (par - 1) :])
    half = LANES // 2
    left = lanes_of((SUB, LANES)) < half
    for c in range(columns // BLOCK):
        if c % SUB == 0:
            at = c // SUB * LANES
            both = total[:, at : at + LANES] + total[:, columns + at : columns + at + LANES]
            turned = jnp.concatenate([jnp.transpose(both[:LANES]), jnp.transpose(both[LANES:])], axis=1)
        got = turned[c % SUB * BLOCK : (c % SUB + 1) * BLOCK]
        eight, ninth = got[:SUB], got[SUB : SUB + 1]
        for j in range(2):
            e = eight[:, j * LANES : (j + 1) * LANES]
            n = jnp.broadcast_to(ninth[:, j * LANES : (j + 1) * LANES], (SUB, LANES))
            at = (c * 2 + j) * 2 * SUB
            out_ref[at : at + SUB] = jnp.where(left, e, pltpu.roll(n, half, 1))
            out_ref[at + SUB : at + 2 * SUB] = jnp.where(left, pltpu.roll(e, half, 1), n)


def home_kernel(recv, rows_ref, centres, conic, rho, opacity, out_ref, total):
    half = LANES // 2
    left = lanes_of((SUB, LANES)) < half
    total[...] = jnp.zeros_like(total)
    step = 4
    for g in range(0, rows_ref.shape[1] // LANES, step):
        eights, ninths = [], []
        for k in range(g, g + step):
            a = recv[2 * k * SUB : (2 * k + 1) * SUB]
            b = recv[(2 * k + 1) * SUB : (2 * k + 2) * SUB]
            eights.append(jnp.where(left, a, pltpu.roll(b, half, 1)))
            n = jnp.where(left, pltpu.roll(a, half, 1), b)
            ninths.append(jnp.broadcast_to(n[0:1], (SUB, LANES)))
        values = jnp.concatenate([jnp.concatenate(eights, axis=1), jnp.concatenate(ninths, axis=1)], axis=0)
        spread(values, rows_ref[0:1, g * LANES : (g + step) * LANES], total)
    wide = total.shape[1]
    for c in range(total.shape[0] // 32):
        m, col2 = nine(total, c)
        at = slice(c * wide, (c + 1) * wide)
        x, y = centres[0:1, at], centres[1:2, at]
        a, d = conic[0:1, at], conic[1:2, at]
        root = jnp.sqrt(a * d)
        b = rho[0:1, at] * root
        m1, mu, mv, muu, muv, mvv = [m[i : i + 1] for i in range(6)]
        dx, dy = mu - x * m1, mv - y * m1
        dxx = muu - 2.0 * x * mu + x * x * m1
        dxy = muv - x * mv - y * mu + x * y * m1
        dyy = mvv - 2.0 * y * mv + y * y * m1
        rows = [
            a * dx + b * dy,
            b * dx + d * dy,
            -0.5 * (dxx + b / a * dxy),
            -0.5 * (dyy + b / d * dxy),
            -root * dxy,
            m1 / opacity[0:1, at],
            m[6:7],
            m[7:8],
            col2,
        ]
        for i, v in enumerate(rows):
            out_ref[i : i + 1, at] = v


def tables(tile):
    pixels = tile * tile
    p = np.arange(pixels)
    v = (p // tile) - (tile - 1) / 2.0
    u = (p % tile) - (tile - 1) / 2.0
    six = np.stack([np.ones(pixels), u, v, u * u, u * v, v * v])
    ahead = np.zeros((32, pixels + 3 * LANES), np.float32)
    for k in range(3):
        ahead[8 * k : 8 * k + 6, :pixels] = six
        ahead[8 * k + 6, pixels : pixels + LANES] = 1.0
        ahead[8 * k + 7, pixels + LANES : pixels + 2 * LANES] = 1.0
        ahead[24 + k, pixels + 2 * LANES :] = 1.0
    return jnp.asarray(ahead, BF16)


def back_scratch(list_len, pixels, slots, par):
    columns = slots // (2 * LANES) * BLOCK
    one = [
        pltpu.VMEM((list_len, 2 * pixels), BF16),
        pltpu.VMEM((list_len, LANES), F32),
        pltpu.VMEM((list_len, 2 * columns), BF16),
    ]
    return [pltpu.VMEM((2 * LANES, 2 * columns), F32), pltpu.VMEM((2 * pixels, LANES), BF16)] + one * par


def call(kernel, out_shape, scratch=(), smem=0, mib=48):
    n_vmem = pl.BlockSpec()

    def run(*args):
        specs = [pl.BlockSpec(memory_space=pltpu.SMEM) if i < smem else n_vmem for i in range(len(args))]
        return pl.pallas_call(
            kernel,
            out_shape=out_shape,
            in_specs=specs,
            out_specs=jax.tree.map(lambda _: n_vmem, out_shape),
            scratch_shapes=list(scratch),
            compiler_params=pltpu.CompilerParams(vmem_limit_bytes=mib * 1024 * 1024),
        )(*args)

    return run


def swap_edges(value):
    size = lax.axis_size("dev")
    me = lax.axis_index("dev")
    first, last = value[:, :HALO], value[:, -HALO:]
    odd = (me % 2) == 1
    inner = [(i, i ^ 1) for i in range(size)]
    outer = [(i, i + 1) for i in range(1, size - 1, 2)]
    outer = outer + [(j, i) for i, j in outer]
    got_in = lax.ppermute(jnp.where(odd, first, last), "dev", inner)
    got_out = lax.ppermute(jnp.where(odd, last, first), "dev", outer)
    return jnp.where(odd, got_in, got_out), jnp.where(odd, got_out, got_in)


def shards(tile_lists, send_rows, centres, conic, rho, opacity, colors, target):
    slot_count = send_rows.shape[1]
    owned_count = centres.shape[1]
    channels, tile, width = target.shape
    strip_tiles, list_len = tile_lists.shape
    size = lax.axis_size("dev")
    me = lax.axis_index("dev")
    pixels = tile * tile
    wide = 2 * LANES
    basis = tables(tile)
    sds = jax.ShapeDtypeStruct

    packed = call(
        pack_kernel,
        sds((size * SUB, LANES), F32),
        [pltpu.VMEM((owned_count // wide * 32, wide), BF16)],
        mib=63,
    )(send_rows, centres, conic, rho, opacity, colors)
    received = lax.all_to_all(packed, "dev", split_axis=0, concat_axis=0, tiled=True)

    order = tile_lists.reshape(strip_tiles, SUB, list_len // SUB).transpose(0, 2, 1)
    order = order.reshape(strip_tiles * list_len // LANES, LANES)
    tar_b, tar_a = swap_edges(target)
    rows_back, cols = blur_tables(tile, width)
    tall = rows_back.shape[0] // 3 - tile
    known = call(target_kernel, sds((2 * channels, tall, width), F32))(target, tar_b, tar_a, rows_back, cols)

    colour_tiles, coefs, segments = call(
        forward_kernel,
        (
            sds((strip_tiles, channels, pixels), F32),
            sds((strip_tiles, 32, list_len), BF16),
            sds((strip_tiles, 5 * SUB, pixels), F32),
        ),
        [pltpu.VMEM((slot_count // wide * 32, wide), BF16)],
    )(received, order, basis)
    image = (
        colour_tiles.reshape(strip_tiles, channels, tile, tile).transpose(1, 2, 0, 3).reshape(channels, tile, width)
    )
    ren_b, ren_a = swap_edges(image)
    edge = jnp.stack([jnp.where(me == 0, RIM, 0), jnp.where(me == size - 1, tile + RIM, tile + HALO)]).astype(jnp.int32)
    cot = call(ssim_kernel, sds((channels, tile, width), F32), smem=1)(
        edge, image, target, ren_b, tar_b, ren_a, tar_a, known, rows_back, cols
    )
    cot_tiles = (
        cot.reshape(channels, tile, strip_tiles, tile).transpose(2, 0, 1, 3).reshape(strip_tiles, channels, pixels)
    )
    slot_sums = call(
        backward_kernel,
        sds((size * SUB, LANES), F32),
        back_scratch(list_len, pixels, slot_count, part_of(strip_tiles, 6)),
    )(coefs, order, segments, cot_tiles, basis)
    returned = lax.all_to_all(slot_sums, "dev", split_axis=0, concat_axis=0, tiled=True)
    grads = call(
        home_kernel,
        sds((9, owned_count), F32),
        [pltpu.VMEM((owned_count // wide * 32, wide), F32)],
    )(returned, send_rows, centres, conic, rho, opacity)
    return (image, grads)


def solution(mesh):
    return jax.shard_map(
        shards,
        mesh=mesh,
        in_specs=(
            P("dev", None),
            P("dev", None),
            P(None, "dev"),
            P(None, "dev"),
            P(None, "dev"),
            P(None, "dev"),
            P(None, "dev"),
            P(None, "dev", None),
        ),
        out_specs=(P(None, "dev", None), P(None, "dev")),
        check_vma=False,
    )
```

```python
import functools

import jax
import jax.numpy as jnp
import numpy as np
from jax import lax
from jax.experimental import pallas as pl
from jax.experimental.pallas import tpu as pltpu
from jax.sharding import PartitionSpec as P

LANES = 128
SUB = 8
RIM = 5
HALO = 2 * RIM
BLOCK = 16
LOG2E = 1.4426950408889634
F32 = jnp.float32
BF16 = jnp.bfloat16
NN = (((1,), (0,)), ((), ()))
NT = (((1,), (1,)), ((), ()))
TN = (((0,), (0,)), ((), ()))


def dot(a, b, dims):
    return lax.dot_general(a, b, dims, preferred_element_type=F32)


def pieces(x, count):
    out = []
    for _ in range(count - 1):
        top = x.astype(BF16)
        out.append(top)
        x = x - top.astype(F32)
    out.append(x.astype(BF16))
    return out


def lanes_of(shape):
    return lax.broadcasted_iota(jnp.int32, shape, len(shape) - 1)


def rows_of(shape):
    return lax.broadcasted_iota(jnp.int32, shape, len(shape) - 2)


def fill(table, c, eight, ninth):
    p = [v.astype(F32) for v in pieces(eight, 3)]
    n = [v.astype(F32) for v in pieces(jnp.broadcast_to(ninth, eight.shape), 3)]
    r = rows_of(eight.shape)
    tail = jnp.where(r == 0, n[0], jnp.where(r == 1, n[1], jnp.where(r == 2, n[2], 0.0)))
    table[c * 32 : (c + 1) * 32] = jnp.concatenate(p + [tail], axis=0).astype(BF16)


def choose(table, idx, none):
    wide = table.shape[1]
    low = jnp.broadcast_to(jnp.bitwise_and(idx, wide - 1), (wide, wide))
    hot = (low == rows_of((wide, wide))).astype(F32).astype(BF16)
    got = dot(table[...], hot, NN)
    chunk = jnp.where(idx < 0, -1, jnp.right_shift(idx, wide.bit_length() - 1))
    chunk = jnp.broadcast_to(chunk, (32, wide))
    x = none
    for c in range(table.shape[0] // 32):
        x = jnp.where(chunk == c, got[c * 32 : (c + 1) * 32], x)
    return x


def pack_kernel(rows_ref, centres, conic, rho, opacity, colors, out_ref, table):
    wide = table.shape[1]
    s = -0.5 * LOG2E
    for c in range(table.shape[0] // 32):
        at = slice(c * wide, (c + 1) * wide)
        x, y = centres[0:1, at], centres[1:2, at]
        a, d = conic[0:1, at], conic[1:2, at]
        b = rho[0:1, at] * jnp.sqrt(a * d)
        rows = [
            jnp.log(opacity[0:1, at]) * LOG2E + s * (a * x * x + 2.0 * b * x * y + d * y * y),
            -2.0 * s * (a * x + b * y),
            -2.0 * s * (d * y + b * x),
            s * a,
            2.0 * s * b,
            s * d,
            colors[0:1, at],
            colors[1:2, at],
        ]
        fill(table, c, jnp.concatenate(rows, axis=0), colors[2:3, at])
    half = LANES // 2
    left = lanes_of((SUB, LANES)) < half
    none = jnp.zeros((32, wide), F32)
    for g in range(rows_ref.shape[1] // wide):
        x = choose(table, rows_ref[0:1, g * wide : (g + 1) * wide], none)
        eight = x[0:SUB] + x[SUB : 2 * SUB] + x[2 * SUB : 3 * SUB]
        ninth = jnp.broadcast_to(x[24:25] + x[25:26] + x[26:27], (SUB, wide))
        for j in range(wide // LANES):
            e, n = [v[:, j * LANES : (j + 1) * LANES] for v in (eight, ninth)]
            at = (g * (wide // LANES) + j) * 2 * SUB
            out_ref[at : at + SUB] = jnp.where(left, e, pltpu.roll(n, half, 1))
            out_ref[at + SUB : at + 2 * SUB] = jnp.where(left, pltpu.roll(e, half, 1), n)


def part_of(count, most):
    return max(d for d in range(1, most + 1) if count % d == 0)


def shifted(x, by):
    return pltpu.roll(x, by % SUB, 0)


def six_of(kind, spot, side):
    down = jnp.right_shift(spot, side.bit_length() - 1)
    u = (spot - down * side).astype(F32) - (side - 1) / 2.0
    v = down.astype(F32) - (side - 1) / 2.0
    six = jnp.zeros(kind.shape, F32)
    for i, f in enumerate((jnp.ones_like(u), u, v, u * u, u * v, v * v)):
        six = jnp.where(kind == i, f, six)
    return six


def terms(pixels):
    r = rows_of((32, pixels))
    kind = jnp.where(r < 24, jnp.bitwise_and(r, SUB - 1), SUB)
    return six_of(kind, lanes_of((32, pixels)), int(pixels**0.5))


def forward_kernel(recv, idx_ref, img_ref, x_ref, seg_ref, table, basis):
    tiles, pixels = img_ref.shape[0], img_ref.shape[2]
    groups = x_ref.shape[2] // LANES
    wide = table.shape[1]
    half = LANES // 2
    left = lanes_of((SUB, LANES)) < half
    for c in range(table.shape[0] // 32):
        eights, ninths = [], []
        for j in range(wide // LANES):
            at = (c * (wide // LANES) + j) * 2 * SUB
            a, b = recv[at : at + SUB], recv[at + SUB : at + 2 * SUB]
            eights.append(jnp.where(left, a, pltpu.roll(b, half, 1)))
            n = jnp.where(left, pltpu.roll(a, half, 1), b)
            ninths.append(n[0:1])
        fill(table, c, jnp.concatenate(eights, axis=1), jnp.concatenate(ninths, axis=1))
    none = jnp.where(rows_of((32, wide)) == 0, -1000.0, 0.0)
    basis[:, :pixels] = terms(pixels).astype(BF16)
    r = rows_of((32, LANES))
    for ch in range(3):
        spread_it = jnp.logical_and(r < 24, jnp.bitwise_and(r, SUB - 1) == 6 + ch) if ch < 2 else jnp.logical_and(r >= 24, r < 27)
        basis[:, pixels + ch * LANES : pixels + (ch + 1) * LANES] = jnp.where(spread_it, 1.0, 0.0).astype(BF16)
    row = rows_of((SUB, pixels))

    def fetch(t):
        per = wide // LANES
        for q in range(0, groups, per):
            idx = jnp.concatenate([idx_ref[pl.ds(t * groups + q + j, 1), :] for j in range(per)], axis=1)
            x = choose(table, idx, none)
            x_ref[t, :, q * LANES : (q + per) * LANES] = x.astype(BF16)

    def composite(t):
        trans = jnp.ones((SUB, pixels), F32)
        acc = [jnp.zeros((SUB, pixels), F32) for _ in range(3)]
        for q in range(groups):
            out = dot(x_ref[t, :, q * LANES : (q + 1) * LANES], basis[...], TN)
            for i in range(LANES // SUB):
                at = slice(i * SUB, (i + 1) * SUB)
                alpha = jnp.exp2(out[at, :pixels])
                w = alpha * trans
                trans = trans * (1.0 - alpha)
                for ch in range(3):
                    tint = out[at, pixels + ch * LANES : pixels + (ch + 1) * LANES]
                    acc[ch] = acc[ch] + jnp.concatenate([tint] * (pixels // LANES), axis=1) * w
        before = jnp.where(row >= 1, shifted(trans, 1), 1.0)
        for by in (1, 2, 4):
            before = before * jnp.where(row >= by, shifted(before, by), 1.0)
        seg_ref[t, 0:SUB] = before
        seg_ref[t, SUB : 2 * SUB] = trans
        image = []
        for ch in range(3):
            seg_ref[t, (2 + ch) * SUB : (3 + ch) * SUB] = acc[ch]
            image.append(jnp.sum(acc[ch] * before, axis=0, keepdims=True))
        img_ref[t] = jnp.concatenate(image, axis=0)

    def body(i, carry):
        for k in range(par):
            fetch(i * par + k)
        for k in range(par):
            composite(i * par + k)
        return carry

    par = part_of(tiles, 8)
    lax.fori_loop(0, tiles // par, body, 0)


def exact(a, b):
    return sum(dot(a[i], b[j], NN) for i in range(3) for j in range(3 - i))


def blur(images, rows, cols):
    height = rows.shape[0] // 3
    done = []
    for x in images:
        got = dot(rows, jnp.concatenate(pieces(x, 3), axis=0), NN)
        done.append(got[:height] + got[height : 2 * height] + got[2 * height :])
    stacked = jnp.concatenate(done, axis=0)
    parts = pieces(stacked, 3)
    width = stacked.shape[1]
    out = []
    for low in range(0, width, 2 * LANES):
        high = min(low + 2 * LANES, width)
        first = max(low - RIM, 0) // LANES * LANES
        end = min(-(-(high + RIM) // LANES) * LANES, width)
        out.append(exact([p[:, first:end] for p in parts], [cols[k, first:end, low:high] for k in range(3)]))
    out = jnp.concatenate(out, axis=1)
    return [out[i * height : (i + 1) * height] for i in range(len(images))]


def padded(own, before, after, ch):
    fill = jnp.zeros((-HALO % SUB, own.shape[2]), F32)
    return jnp.concatenate([own[ch], before[ch], fill, after[ch], fill], axis=0)


def target_kernel(tar, tar_b, tar_a, rows_back, cols, out_ref):
    rows = rows_back[: 3 * out_ref.shape[1]]
    channels = tar.shape[0]
    images = [padded(tar, tar_b, tar_a, ch) for ch in range(channels)]
    for i, v in enumerate(blur(images + [x * x for x in images], rows, cols)):
        out_ref[i] = v


def ssim_kernel(edge, ren, tar, ren_b, tar_b, ren_a, tar_a, known, rows_back, cols, cot_ref):
    channels, height, width = ren.shape
    tall = known.shape[1]
    rows = rows_back[: 3 * tall]
    back = rows_back[3 * tall :, : 3 * tall]
    r_at = rows_of((tall, width))
    inside = jnp.logical_and(r_at >= edge[0], r_at < edge[1])
    ren_s = [padded(ren, ren_b, ren_a, ch) for ch in range(channels)]
    tar_s = [padded(tar, tar_b, tar_a, ch) for ch in range(channels)]
    found = blur(ren_s + [x * x for x in ren_s] + [x * y for x, y in zip(ren_s, tar_s)], rows, cols)
    fields = []
    for ch in range(channels):
        mr, er, ert = found[ch], found[channels + ch], found[2 * channels + ch]
        mt, et = known[ch], known[channels + ch]
        a1 = 2.0 * mr * mt + 0.0001
        a2 = 2.0 * (ert - mr * mt) + 0.0009
        b1 = mr * mr + mt * mt + 0.0001
        b2 = (er - mr * mr) + (et - mt * mt) + 0.0009
        i1, i2 = 1.0 / b1, 1.0 / b2
        s = a1 * a2 * i1 * i2
        d_mr = 2.0 * mt * (a2 - a1) * i1 * i2 - 2.0 * mr * s * (i1 - i2)
        d_er = -s * i2
        d_ert = 2.0 * a1 * i1 * i2
        fields += [jnp.where(inside, d, 0.0) for d in (d_mr, d_er, d_ert)]
    pulled = blur(fields, back, cols)
    for ch in range(channels):
        g0, g1, g2 = pulled[3 * ch : 3 * ch + 3]
        rc, tc = ren[ch], tar[ch]
        cot_ref[ch] = 1.6 * (rc - tc) - 0.2 * (g0 + 2.0 * rc * g1 + tc * g2)


def parts_of(matrix):
    out = []
    rest = matrix.astype(np.float32)
    for _ in range(3):
        top = rest.astype(jnp.bfloat16)
        out.append(top)
        rest = rest - top.astype(np.float32)
    return jnp.asarray(np.stack(out))


def blur_tables(height, width):
    m = np.arange(-RIM, RIM + 1)
    taps = np.exp(-m * m / 4.5)
    taps = taps / taps.sum()
    side = HALO + (-HALO % SUB)
    place = [height + i for i in range(HALO)] + list(range(height)) + [height + side + i for i in range(HALO)]
    mid = height + HALO
    tall = mid + (-mid % SUB)
    rows = np.zeros((tall, height + 2 * side))
    back = np.zeros((height, tall))
    cols = np.zeros((width, width))
    for k, tap in enumerate(taps):
        for i in range(mid):
            rows[i, place[i + k]] = tap
        for i in range(height):
            back[i, i + k] = tap
        for i in range(width):
            if 0 <= i + k - RIM < width:
                cols[i + k - RIM, i] = tap

    def stack(matrix):
        p = parts_of(matrix)
        none = jnp.zeros_like(p[0])
        sides = [[p[i] if i + j < 3 else none for j in range(3)] for i in range(3)]
        return jnp.concatenate([jnp.concatenate(side, axis=1) for side in sides], axis=0)

    down, up = stack(rows), stack(back)
    up = jnp.pad(up, ((0, 0), (0, down.shape[1] - up.shape[1])))
    return jnp.concatenate([down, up], axis=0), parts_of(cols)


def spread(values, where, total):
    count = where.shape[1]
    wide = total.shape[1]
    p0, p1, p2 = [p.astype(F32) for p in pieces(values, 3)]
    rows = rows_of((SUB, count))
    tail = jnp.where(rows == 0, p0[SUB:], jnp.where(rows == 1, p1[SUB:], jnp.where(rows == 2, p2[SUB:], 0.0)))
    stacked = jnp.concatenate([p0[:SUB], p1[:SUB], p2[:SUB], tail], axis=0)
    low = jnp.bitwise_and(where, wide - 1)
    high = jnp.where(where < 0, -1, jnp.right_shift(where, wide.bit_length() - 1))
    hot = (jnp.broadcast_to(low, (wide, count)) == rows_of((wide, count))).astype(F32).astype(BF16)
    parts = []
    for c in range(total.shape[0] // 32):
        parts.append(jnp.where(jnp.broadcast_to(high == c, stacked.shape), stacked, 0.0).astype(BF16))
    total[...] += dot(jnp.concatenate(parts, axis=0), hot, NT)


def nine(total, c):
    got = total[c * 32 : (c + 1) * 32]
    return (
        got[0:SUB] + got[SUB : 2 * SUB] + got[2 * SUB : 3 * SUB],
        got[24:25] + got[25:26] + got[26:27],
    )


def backward_kernel(x_ref, idx_ref, seg_ref, cot_ref, out_ref, total, phi, *buffers):
    tiles, pixels = cot_ref.shape[0], cot_ref.shape[2]
    count = x_ref.shape[2]
    groups = count // LANES
    steps = LANES // SUB
    wide = 2 * LANES
    total[...] = jnp.zeros_like(total)
    row = rows_of((SUB, pixels))
    each = 3
    columns = total.shape[1] // 2
    field = jnp.bitwise_and(lanes_of((SUB, LANES)), BLOCK - 1)
    basis = jnp.concatenate([terms(pixels), jnp.zeros((32, pixels), F32)], axis=0).astype(BF16)
    kind = jnp.bitwise_and(lanes_of((pixels, LANES)), BLOCK - 1)
    six = six_of(kind, rows_of((pixels, LANES)), int(pixels**0.5))
    phi[:pixels] = six.astype(BF16)
    phi[pixels:] = six.astype(BF16)
    moment = jnp.bitwise_and(lanes_of((count, LANES)), BLOCK - 1) < 6
    block = jnp.right_shift(lanes_of((LANES, LANES)), BLOCK.bit_length() - 1)

    def sweep(t, factors, tints_ref, split):
        cot = [jnp.broadcast_to(cot_ref[t, ch : ch + 1], (SUB, pixels)) for ch in range(3)]
        hi = [c.astype(BF16).astype(F32) for c in cot]
        lo = [c - h for c, h in zip(cot, hi)]

        def place(v):
            body = jnp.where(row == 6, v[0], jnp.where(row == 7, v[1], 0.0))
            return [body, body, body, jnp.where(row < 3, v[2], 0.0)]

        rhs = jnp.concatenate(place(hi) + place(lo), axis=0).astype(BF16)
        rhs = jnp.concatenate([basis, rhs], axis=1)
        trans = seg_ref[t, 0:SUB]
        rest = trans * (cot[0] * seg_ref[t, 2 * SUB : 3 * SUB] + cot[1] * seg_ref[t, 3 * SUB : 4 * SUB] + cot[2] * seg_ref[t, 4 * SUB : 5 * SUB])
        for by in (1, 2, 4):
            rest = rest + jnp.where(row < SUB - by, shifted(rest, -by), 0.0)
        for q in range(groups):
            x = x_ref[t, :, q * LANES : (q + 1) * LANES]
            out = dot(jnp.concatenate([x, x], axis=0), rhs, TN)
            for i in range(0, steps, 2):
                hs = []
                for j in (i, i + 1):
                    at = slice(q * LANES + j * SUB, q * LANES + (j + 1) * SUB)
                    alpha = jnp.exp2(out[j * SUB : (j + 1) * SUB, :pixels])
                    w = alpha * trans
                    clear = 1.0 - alpha
                    trans = trans * clear
                    wg = w * out[j * SUB : (j + 1) * SUB, pixels:]
                    rest = rest - wg
                    hs.append(wg - alpha * pl.reciprocal(clear, approx=True) * rest)
                    tints = [jnp.sum(w * c, axis=1, keepdims=True) for c in cot]
                    tints_ref[at] = jnp.where(field == 6, tints[0], jnp.where(field == 7, tints[1], tints[2]))
                at = slice(q * LANES + i * SUB, q * LANES + (i + 2) * SUB)
                for p, v in enumerate(pieces(jnp.concatenate(hs, axis=0), 2)):
                    factors[at, p * pixels : (p + 1) * pixels] = v

    def sums(t, factors, tints_ref, split):
        got = jnp.where(moment, dot(factors[...], phi[...], NN), tints_ref[...])
        where = [idx_ref[pl.ds(t * groups + q, 1), :] for q in range(groups)]
        words = []
        for q, idx in enumerate(where):
            if q % 4 == 0:
                words.append(jnp.zeros((1, LANES), jnp.int32))
            words[-1] = words[-1] | jnp.left_shift(jnp.where(idx < 0, 255, jnp.right_shift(idx, 8)), 8 * (q % 4))
        words = jnp.transpose(jnp.concatenate(words + [words[0]] * (SUB - len(words)), axis=0))
        for q in range(groups):
            at = slice(q * LANES, (q + 1) * LANES)
            if q % 4 == 0:
                word = jnp.broadcast_to(words[:, q // 4 : q // 4 + 1], (LANES, LANES))
            mine = word & jnp.left_shift(jnp.full((LANES, LANES), 255, jnp.int32), 8 * (q % 4))
            for base in range(0, columns, LANES):
                kept = jnp.where(mine == jnp.left_shift(block + base // BLOCK, 8 * (q % 4)), got[at], 0.0)
                top, rest = pieces(kept, 2)
                split[at, base : base + LANES] = top
                split[at, columns + base : columns + base + LANES] = rest

    def scatter(t, factors, tints_ref, split):
        where = jnp.concatenate([idx_ref[pl.ds(t * groups + q, 1), :] for q in range(groups)], axis=1)
        low = jnp.bitwise_and(where, wide - 1)
        hot = (jnp.broadcast_to(low, (wide, count)) == rows_of((wide, count))).astype(F32).astype(BF16)
        total[...] += dot(hot, split[...], NN)

    par = len(buffers) // each

    def body(i, carry):
        for k in range(par):
            now = buffers[each * k : each * (k + 1)]
            last = buffers[each * ((k - 1) % par) :][:each]
            t = i * par + k
            sums(jnp.maximum(t - 1, 0), *last)
            sweep(t, *now)
            scatter(jnp.maximum(t - 1, 0), *last)
        return carry

    buffers[each * (par - 1)][...] = jnp.zeros((count, 2 * pixels), BF16)
    buffers[each * (par - 1) + 1][...] = jnp.zeros((count, LANES), F32)
    lax.fori_loop(0, tiles // par, body, 0)
    sums(tiles - 1, *buffers[each * (par - 1) :])
    scatter(tiles - 1, *buffers[each * (par - 1) :])
    half = LANES // 2
    left = lanes_of((SUB, LANES)) < half
    for c in range(columns // BLOCK):
        if c % SUB == 0:
            at = c // SUB * LANES
            both = total[:, at : at + LANES] + total[:, columns + at : columns + at + LANES]
            turned = jnp.concatenate([jnp.transpose(both[:LANES]), jnp.transpose(both[LANES:])], axis=1)
        got = turned[c % SUB * BLOCK : (c % SUB + 1) * BLOCK]
        eight, ninth = got[:SUB], got[SUB : SUB + 1]
        for j in range(2):
            e = eight[:, j * LANES : (j + 1) * LANES]
            n = jnp.broadcast_to(ninth[:, j * LANES : (j + 1) * LANES], (SUB, LANES))
            at = (c * 2 + j) * 2 * SUB
            out_ref[at : at + SUB] = jnp.where(left, e, pltpu.roll(n, half, 1))
            out_ref[at + SUB : at + 2 * SUB] = jnp.where(left, pltpu.roll(e, half, 1), n)


def home_kernel(recv, rows_ref, centres, conic, rho, opacity, out_ref, total):
    half = LANES // 2
    left = lanes_of((SUB, LANES)) < half
    total[...] = jnp.zeros_like(total)
    step = 4
    for g in range(0, rows_ref.shape[1] // LANES, step):
        eights, ninths = [], []
        for k in range(g, g + step):
            a = recv[2 * k * SUB : (2 * k + 1) * SUB]
            b = recv[(2 * k + 1) * SUB : (2 * k + 2) * SUB]
            eights.append(jnp.where(left, a, pltpu.roll(b, half, 1)))
            n = jnp.where(left, pltpu.roll(a, half, 1), b)
            ninths.append(jnp.broadcast_to(n[0:1], (SUB, LANES)))
        values = jnp.concatenate([jnp.concatenate(eights, axis=1), jnp.concatenate(ninths, axis=1)], axis=0)
        spread(values, rows_ref[0:1, g * LANES : (g + step) * LANES], total)
    wide = total.shape[1]
    for c in range(total.shape[0] // 32):
        m, col2 = nine(total, c)
        at = slice(c * wide, (c + 1) * wide)
        x, y = centres[0:1, at], centres[1:2, at]
        a, d = conic[0:1, at], conic[1:2, at]
        root = jnp.sqrt(a * d)
        b = rho[0:1, at] * root
        m1, mu, mv, muu, muv, mvv = [m[i : i + 1] for i in range(6)]
        dx, dy = mu - x * m1, mv - y * m1
        dxx = muu - 2.0 * x * mu + x * x * m1
        dxy = muv - x * mv - y * mu + x * y * m1
        dyy = mvv - 2.0 * y * mv + y * y * m1
        rows = [
            a * dx + b * dy,
            b * dx + d * dy,
            -0.5 * (dxx + b / a * dxy),
            -0.5 * (dyy + b / d * dxy),
            -root * dxy,
            m1 / opacity[0:1, at],
            m[6:7],
            m[7:8],
            col2,
        ]
        for i, v in enumerate(rows):
            out_ref[i : i + 1, at] = v


def back_scratch(list_len, pixels, slots, par):
    columns = slots // (2 * LANES) * BLOCK
    one = [
        pltpu.VMEM((list_len, 2 * pixels), BF16),
        pltpu.VMEM((list_len, LANES), F32),
        pltpu.VMEM((list_len, 2 * columns), BF16),
    ]
    return [pltpu.VMEM((2 * LANES, 2 * columns), F32), pltpu.VMEM((2 * pixels, LANES), BF16)] + one * par


def call(kernel, out_shape, scratch=(), smem=0, mib=48):
    n_vmem = pl.BlockSpec()

    def run(*args):
        specs = [pl.BlockSpec(memory_space=pltpu.SMEM) if i < smem else n_vmem for i in range(len(args))]
        return pl.pallas_call(
            kernel,
            out_shape=out_shape,
            in_specs=specs,
            out_specs=jax.tree.map(lambda _: n_vmem, out_shape),
            scratch_shapes=list(scratch),
            compiler_params=pltpu.CompilerParams(vmem_limit_bytes=mib * 1024 * 1024),
        )(*args)

    return run


def swap_edges(value):
    size = lax.axis_size("dev")
    me = lax.axis_index("dev")
    first, last = value[:, :HALO], value[:, -HALO:]
    odd = (me % 2) == 1
    inner = [(i, i ^ 1) for i in range(size)]
    outer = [(i, i + 1) for i in range(1, size - 1, 2)]
    outer = outer + [(j, i) for i, j in outer]
    got_in = lax.ppermute(jnp.where(odd, first, last), "dev", inner)
    got_out = lax.ppermute(jnp.where(odd, last, first), "dev", outer)
    return jnp.where(odd, got_in, got_out), jnp.where(odd, got_out, got_in)


def shards(tile_lists, send_rows, centres, conic, rho, opacity, colors, target):
    slot_count = send_rows.shape[1]
    owned_count = centres.shape[1]
    channels, tile, width = target.shape
    strip_tiles, list_len = tile_lists.shape
    size = lax.axis_size("dev")
    me = lax.axis_index("dev")
    pixels = tile * tile
    wide = 2 * LANES
    sds = jax.ShapeDtypeStruct

    packed = call(
        pack_kernel,
        sds((size * SUB, LANES), F32),
        [pltpu.VMEM((owned_count // wide * 32, wide), BF16)],
        mib=63,
    )(send_rows, centres, conic, rho, opacity, colors)
    received = lax.all_to_all(packed, "dev", split_axis=0, concat_axis=0, tiled=True)

    order = tile_lists.reshape(strip_tiles, SUB, list_len // SUB).transpose(0, 2, 1)
    order = order.reshape(strip_tiles * list_len // LANES, LANES)
    tar_b, tar_a = swap_edges(target)
    rows_back, cols = blur_tables(tile, width)
    tall = rows_back.shape[0] // 3 - tile
    known = call(target_kernel, sds((2 * channels, tall, width), F32))(target, tar_b, tar_a, rows_back, cols)

    colour_tiles, coefs, segments = call(
        forward_kernel,
        (
            sds((strip_tiles, channels, pixels), F32),
            sds((strip_tiles, 32, list_len), BF16),
            sds((strip_tiles, 5 * SUB, pixels), F32),
        ),
        [pltpu.VMEM((slot_count // wide * 32, wide), BF16), pltpu.VMEM((32, pixels + 3 * LANES), BF16)],
    )(received, order)
    image = (
        colour_tiles.reshape(strip_tiles, channels, tile, tile).transpose(1, 2, 0, 3).reshape(channels, tile, width)
    )
    ren_b, ren_a = swap_edges(image)
    edge = jnp.stack([jnp.where(me == 0, RIM, 0), jnp.where(me == size - 1, tile + RIM, tile + HALO)]).astype(jnp.int32)
    cot = call(ssim_kernel, sds((channels, tile, width), F32), smem=1)(
        edge, image, target, ren_b, tar_b, ren_a, tar_a, known, rows_back, cols
    )
    cot_tiles = (
        cot.reshape(channels, tile, strip_tiles, tile).transpose(2, 0, 1, 3).reshape(strip_tiles, channels, pixels)
    )
    slot_sums = call(
        backward_kernel,
        sds((size * SUB, LANES), F32),
        back_scratch(list_len, pixels, slot_count, part_of(strip_tiles, 8)),
    )(coefs, order, segments, cot_tiles)
    returned = lax.all_to_all(slot_sums, "dev", split_axis=0, concat_axis=0, tiled=True)
    grads = call(
        home_kernel,
        sds((9, owned_count), F32),
        [pltpu.VMEM((owned_count // wide * 32, wide), F32)],
    )(returned, send_rows, centres, conic, rho, opacity)
    return (image, grads)


def solution(mesh):
    return jax.shard_map(
        shards,
        mesh=mesh,
        in_specs=(
            P("dev", None),
            P("dev", None),
            P(None, "dev"),
            P(None, "dev"),
            P(None, "dev"),
            P(None, "dev"),
            P(None, "dev"),
            P(None, "dev", None),
        ),
        out_specs=(P(None, "dev", None), P(None, "dev")),
        check_vma=False,
    )
```

```python
import functools

import jax
import jax.numpy as jnp
import numpy as np
from jax import lax
from jax.experimental import pallas as pl
from jax.experimental.pallas import tpu as pltpu
from jax.sharding import PartitionSpec as P

LANES = 128
SUB = 8
RIM = 5
HALO = 2 * RIM
BLOCK = 16
LOG2E = 1.4426950408889634
F32 = jnp.float32
BF16 = jnp.bfloat16
NN = (((1,), (0,)), ((), ()))
NT = (((1,), (1,)), ((), ()))
TN = (((0,), (0,)), ((), ()))


def dot(a, b, dims):
    return lax.dot_general(a, b, dims, preferred_element_type=F32)


def pieces(x, count):
    out = []
    for _ in range(count - 1):
        top = x.astype(BF16)
        out.append(top)
        x = x - top.astype(F32)
    out.append(x.astype(BF16))
    return out


def lanes_of(shape):
    return lax.broadcasted_iota(jnp.int32, shape, len(shape) - 1)


def rows_of(shape):
    return lax.broadcasted_iota(jnp.int32, shape, len(shape) - 2)


def fill(table, c, eight, ninth):
    p = [v.astype(F32) for v in pieces(eight, 3)]
    n = [v.astype(F32) for v in pieces(jnp.broadcast_to(ninth, eight.shape), 3)]
    r = rows_of(eight.shape)
    tail = jnp.where(r == 0, n[0], jnp.where(r == 1, n[1], jnp.where(r == 2, n[2], 0.0)))
    table[c * 32 : (c + 1) * 32] = jnp.concatenate(p + [tail], axis=0).astype(BF16)


def choose(table, idx, none):
    wide = table.shape[1]
    low = jnp.broadcast_to(jnp.bitwise_and(idx, wide - 1), (wide, wide))
    hot = (low == rows_of((wide, wide))).astype(F32).astype(BF16)
    got = dot(table[...], hot, NN)
    chunk = jnp.where(idx < 0, -1, jnp.right_shift(idx, wide.bit_length() - 1))
    chunk = jnp.broadcast_to(chunk, (32, wide))
    x = none
    for c in range(table.shape[0] // 32):
        x = jnp.where(chunk == c, got[c * 32 : (c + 1) * 32], x)
    return x


def pack_kernel(rows_ref, centres, conic, rho, opacity, colors, out_ref, table):
    wide = table.shape[1]
    s = -0.5 * LOG2E
    for c in range(table.shape[0] // 32):
        at = slice(c * wide, (c + 1) * wide)
        x, y = centres[0:1, at], centres[1:2, at]
        a, d = conic[0:1, at], conic[1:2, at]
        b = rho[0:1, at] * jnp.sqrt(a * d)
        rows = [
            jnp.log(opacity[0:1, at]) * LOG2E + s * (a * x * x + 2.0 * b * x * y + d * y * y),
            -2.0 * s * (a * x + b * y),
            -2.0 * s * (d * y + b * x),
            s * a,
            2.0 * s * b,
            s * d,
            colors[0:1, at],
            colors[1:2, at],
        ]
        fill(table, c, jnp.concatenate(rows, axis=0), colors[2:3, at])
    half = LANES // 2
    left = lanes_of((SUB, LANES)) < half
    none = jnp.zeros((32, wide), F32)
    for g in range(rows_ref.shape[1] // wide):
        x = choose(table, rows_ref[0:1, g * wide : (g + 1) * wide], none)
        eight = x[0:SUB] + x[SUB : 2 * SUB] + x[2 * SUB : 3 * SUB]
        ninth = jnp.broadcast_to(x[24:25] + x[25:26] + x[26:27], (SUB, wide))
        for j in range(wide // LANES):
            e, n = [v[:, j * LANES : (j + 1) * LANES] for v in (eight, ninth)]
            at = (g * (wide // LANES) + j) * 2 * SUB
            out_ref[at : at + SUB] = jnp.where(left, e, pltpu.roll(n, half, 1))
            out_ref[at + SUB : at + 2 * SUB] = jnp.where(left, pltpu.roll(e, half, 1), n)


def part_of(count, most):
    return max(d for d in range(1, most + 1) if count % d == 0)


def shifted(x, by):
    return pltpu.roll(x, by % SUB, 0)


def six_of(kind, spot, side):
    down = jnp.right_shift(spot, side.bit_length() - 1)
    u = (spot - down * side).astype(F32) - (side - 1) / 2.0
    v = down.astype(F32) - (side - 1) / 2.0
    six = jnp.zeros(kind.shape, F32)
    for i, f in enumerate((jnp.ones_like(u), u, v, u * u, u * v, v * v)):
        six = jnp.where(kind == i, f, six)
    return six


def terms(pixels):
    r = rows_of((32, pixels))
    kind = jnp.where(r < 24, jnp.bitwise_and(r, SUB - 1), SUB)
    return six_of(kind, lanes_of((32, pixels)), int(pixels**0.5))


def forward_kernel(recv, idx_ref, img_ref, x_ref, seg_ref, table, basis):
    tiles, pixels = img_ref.shape[0], img_ref.shape[2]
    groups = x_ref.shape[2] // LANES
    wide = table.shape[1]
    half = LANES // 2
    left = lanes_of((SUB, LANES)) < half
    for c in range(table.shape[0] // 32):
        eights, ninths = [], []
        for j in range(wide // LANES):
            at = (c * (wide // LANES) + j) * 2 * SUB
            a, b = recv[at : at + SUB], recv[at + SUB : at + 2 * SUB]
            eights.append(jnp.where(left, a, pltpu.roll(b, half, 1)))
            n = jnp.where(left, pltpu.roll(a, half, 1), b)
            ninths.append(n[0:1])
        fill(table, c, jnp.concatenate(eights, axis=1), jnp.concatenate(ninths, axis=1))
    none = jnp.where(rows_of((32, wide)) == 0, -1000.0, 0.0)
    basis[:, :pixels] = terms(pixels).astype(BF16)
    r = rows_of((32, LANES))
    for ch in range(3):
        spread_it = jnp.logical_and(r < 24, jnp.bitwise_and(r, SUB - 1) == 6 + ch) if ch < 2 else jnp.logical_and(r >= 24, r < 27)
        basis[:, pixels + ch * LANES : pixels + (ch + 1) * LANES] = jnp.where(spread_it, 1.0, 0.0).astype(BF16)
    row = rows_of((SUB, pixels))

    def fetch(t):
        per = wide // LANES
        for q in range(0, groups, per):
            idx = jnp.concatenate([idx_ref[pl.ds(t * groups + q + j, 1), :] for j in range(per)], axis=1)
            x = choose(table, idx, none)
            x_ref[t, :, q * LANES : (q + per) * LANES] = x.astype(BF16)

    def composite(t):
        trans = jnp.ones((SUB, pixels), F32)
        acc = [jnp.zeros((SUB, pixels), F32) for _ in range(3)]
        for q in range(groups):
            out = dot(x_ref[t, :, q * LANES : (q + 1) * LANES], basis[...], TN)
            for i in range(LANES // SUB):
                at = slice(i * SUB, (i + 1) * SUB)
                alpha = jnp.exp2(out[at, :pixels])
                w = alpha * trans
                trans = trans * (1.0 - alpha)
                for ch in range(3):
                    tint = out[at, pixels + ch * LANES : pixels + (ch + 1) * LANES]
                    acc[ch] = acc[ch] + jnp.concatenate([tint] * (pixels // LANES), axis=1) * w
        before = jnp.where(row >= 1, shifted(trans, 1), 1.0)
        for by in (1, 2, 4):
            before = before * jnp.where(row >= by, shifted(before, by), 1.0)
        seg_ref[t, 0:SUB] = before
        image = []
        for ch in range(3):
            seg_ref[t, (1 + ch) * SUB : (2 + ch) * SUB] = acc[ch]
            image.append(jnp.sum(acc[ch] * before, axis=0, keepdims=True))
        img_ref[t] = jnp.concatenate(image, axis=0)

    def body(i, carry):
        for k in range(par):
            fetch(i * par + k)
        for k in range(par):
            composite(i * par + k)
        return carry

    par = part_of(tiles, 8)
    lax.fori_loop(0, tiles // par, body, 0)


def exact(a, b):
    return sum(dot(a[i], b[j], NN) for i in range(3) for j in range(3 - i))


def blur(images, rows, cols):
    height = rows.shape[0] // 3
    done = []
    for x in images:
        got = dot(rows, jnp.concatenate(pieces(x, 3), axis=0), NN)
        done.append(got[:height] + got[height : 2 * height] + got[2 * height :])
    stacked = jnp.concatenate(done, axis=0)
    parts = pieces(stacked, 3)
    width = stacked.shape[1]
    out = []
    for low in range(0, width, 2 * LANES):
        high = min(low + 2 * LANES, width)
        first = max(low - RIM, 0) // LANES * LANES
        end = min(-(-(high + RIM) // LANES) * LANES, width)
        out.append(exact([p[:, first:end] for p in parts], [cols[k, first:end, low:high] for k in range(3)]))
    out = jnp.concatenate(out, axis=1)
    return [out[i * height : (i + 1) * height] for i in range(len(images))]


def padded(own, before, after, ch):
    fill = jnp.zeros((-HALO % SUB, own.shape[2]), F32)
    return jnp.concatenate([own[ch], before[ch], fill, after[ch], fill], axis=0)


def target_kernel(tar, tar_b, tar_a, rows_back, cols, out_ref):
    rows = rows_back[: 3 * out_ref.shape[1]]
    channels = tar.shape[0]
    images = [padded(tar, tar_b, tar_a, ch) for ch in range(channels)]
    for i, v in enumerate(blur(images + [x * x for x in images], rows, cols)):
        out_ref[i] = v


def ssim_kernel(edge, ren, tar, ren_b, tar_b, ren_a, tar_a, known, rows_back, cols, cot_ref):
    channels, height, width = ren.shape
    tall = known.shape[1]
    rows = rows_back[: 3 * tall]
    back = rows_back[3 * tall :, : 3 * tall]
    r_at = rows_of((tall, width))
    inside = jnp.logical_and(r_at >= edge[0], r_at < edge[1])
    ren_s = [padded(ren, ren_b, ren_a, ch) for ch in range(channels)]
    tar_s = [padded(tar, tar_b, tar_a, ch) for ch in range(channels)]
    found = blur(ren_s + [x * x for x in ren_s] + [x * y for x, y in zip(ren_s, tar_s)], rows, cols)
    fields = []
    for ch in range(channels):
        mr, er, ert = found[ch], found[channels + ch], found[2 * channels + ch]
        mt, et = known[ch], known[channels + ch]
        a1 = 2.0 * mr * mt + 0.0001
        a2 = 2.0 * (ert - mr * mt) + 0.0009
        b1 = mr * mr + mt * mt + 0.0001
        b2 = (er - mr * mr) + (et - mt * mt) + 0.0009
        i1, i2 = 1.0 / b1, 1.0 / b2
        s = a1 * a2 * i1 * i2
        d_mr = 2.0 * mt * (a2 - a1) * i1 * i2 - 2.0 * mr * s * (i1 - i2)
        d_er = -s * i2
        d_ert = 2.0 * a1 * i1 * i2
        fields += [jnp.where(inside, d, 0.0) for d in (d_mr, d_er, d_ert)]
    pulled = blur(fields, back, cols)
    for ch in range(channels):
        g0, g1, g2 = pulled[3 * ch : 3 * ch + 3]
        rc, tc = ren[ch], tar[ch]
        cot_ref[ch] = 1.6 * (rc - tc) - 0.2 * (g0 + 2.0 * rc * g1 + tc * g2)


def parts_of(matrix):
    out = []
    rest = matrix.astype(np.float32)
    for _ in range(3):
        top = rest.astype(jnp.bfloat16)
        out.append(top)
        rest = rest - top.astype(np.float32)
    return jnp.asarray(np.stack(out))


def blur_tables(height, width):
    m = np.arange(-RIM, RIM + 1)
    taps = np.exp(-m * m / 4.5)
    taps = taps / taps.sum()
    side = HALO + (-HALO % SUB)
    place = [height + i for i in range(HALO)] + list(range(height)) + [height + side + i for i in range(HALO)]
    mid = height + HALO
    tall = mid + (-mid % SUB)
    rows = np.zeros((tall, height + 2 * side))
    back = np.zeros((height, tall))
    cols = np.zeros((width, width))
    for k, tap in enumerate(taps):
        for i in range(mid):
            rows[i, place[i + k]] = tap
        for i in range(height):
            back[i, i + k] = tap
        for i in range(width):
            if 0 <= i + k - RIM < width:
                cols[i + k - RIM, i] = tap

    def stack(matrix):
        p = parts_of(matrix)
        none = jnp.zeros_like(p[0])
        sides = [[p[i] if i + j < 3 else none for j in range(3)] for i in range(3)]
        return jnp.concatenate([jnp.concatenate(side, axis=1) for side in sides], axis=0)

    down, up = stack(rows), stack(back)
    up = jnp.pad(up, ((0, 0), (0, down.shape[1] - up.shape[1])))
    return jnp.concatenate([down, up], axis=0), parts_of(cols)


def spread(values, where, total):
    count = where.shape[1]
    wide = total.shape[1]
    p0, p1, p2 = [p.astype(F32) for p in pieces(values, 3)]
    rows = rows_of((SUB, count))
    tail = jnp.where(rows == 0, p0[SUB:], jnp.where(rows == 1, p1[SUB:], jnp.where(rows == 2, p2[SUB:], 0.0)))
    stacked = jnp.concatenate([p0[:SUB], p1[:SUB], p2[:SUB], tail], axis=0)
    low = jnp.bitwise_and(where, wide - 1)
    high = jnp.where(where < 0, -1, jnp.right_shift(where, wide.bit_length() - 1))
    hot = (jnp.broadcast_to(low, (wide, count)) == rows_of((wide, count))).astype(F32).astype(BF16)
    parts = []
    for c in range(total.shape[0] // 32):
        parts.append(jnp.where(jnp.broadcast_to(high == c, stacked.shape), stacked, 0.0).astype(BF16))
    total[...] += dot(jnp.concatenate(parts, axis=0), hot, NT)


def nine(total, c):
    got = total[c * 32 : (c + 1) * 32]
    return (
        got[0:SUB] + got[SUB : 2 * SUB] + got[2 * SUB : 3 * SUB],
        got[24:25] + got[25:26] + got[26:27],
    )


def backward_kernel(x_ref, idx_ref, seg_ref, cot_ref, out_ref, total, phi, *buffers):
    tiles, pixels = cot_ref.shape[0], cot_ref.shape[2]
    count = x_ref.shape[2]
    groups = count // LANES
    steps = LANES // SUB
    wide = 2 * LANES
    total[...] = jnp.zeros_like(total)
    row = rows_of((SUB, pixels))
    each = 3
    columns = total.shape[1] // 2
    field = jnp.bitwise_and(lanes_of((SUB, LANES)), BLOCK - 1)
    basis = jnp.concatenate([terms(pixels), jnp.zeros((32, pixels), F32)], axis=0).astype(BF16)
    kind = jnp.bitwise_and(lanes_of((pixels, LANES)), BLOCK - 1)
    six = six_of(kind, rows_of((pixels, LANES)), int(pixels**0.5))
    phi[:pixels] = six.astype(BF16)
    phi[pixels:] = six.astype(BF16)
    moment = jnp.bitwise_and(lanes_of((count, LANES)), BLOCK - 1) < 6
    block = jnp.right_shift(lanes_of((LANES, LANES)), BLOCK.bit_length() - 1)

    def sweep(t, factors, tints_ref, split):
        cot = [jnp.broadcast_to(cot_ref[t, ch : ch + 1], (SUB, pixels)) for ch in range(3)]
        hi = [c.astype(BF16).astype(F32) for c in cot]
        lo = [c - h for c, h in zip(cot, hi)]

        def place(v):
            body = jnp.where(row == 6, v[0], jnp.where(row == 7, v[1], 0.0))
            return [body, body, body, jnp.where(row < 3, v[2], 0.0)]

        rhs = jnp.concatenate(place(hi) + place(lo), axis=0).astype(BF16)
        rhs = jnp.concatenate([basis, rhs], axis=1)
        trans = seg_ref[t, 0:SUB]
        rest = trans * (cot[0] * seg_ref[t, SUB : 2 * SUB] + cot[1] * seg_ref[t, 2 * SUB : 3 * SUB] + cot[2] * seg_ref[t, 3 * SUB : 4 * SUB])
        for by in (1, 2, 4):
            rest = rest + jnp.where(row < SUB - by, shifted(rest, -by), 0.0)
        for q in range(groups):
            x = x_ref[t, :, q * LANES : (q + 1) * LANES]
            out = dot(jnp.concatenate([x, x], axis=0), rhs, TN)
            for i in range(0, steps, 2):
                hs = []
                for j in (i, i + 1):
                    at = slice(q * LANES + j * SUB, q * LANES + (j + 1) * SUB)
                    alpha = jnp.exp2(out[j * SUB : (j + 1) * SUB, :pixels])
                    w = alpha * trans
                    clear = 1.0 - alpha
                    trans = trans * clear
                    wg = w * out[j * SUB : (j + 1) * SUB, pixels:]
                    rest = rest - wg
                    hs.append(wg - alpha * pl.reciprocal(clear, approx=True) * rest)
                    tints = [jnp.sum(w * c, axis=1, keepdims=True) for c in cot]
                    tints_ref[at] = jnp.where(field == 6, tints[0], jnp.where(field == 7, tints[1], tints[2]))
                at = slice(q * LANES + i * SUB, q * LANES + (i + 2) * SUB)
                for p, v in enumerate(pieces(jnp.concatenate(hs, axis=0), 2)):
                    factors[at, p * pixels : (p + 1) * pixels] = v

    def sums(t, factors, tints_ref, split):
        got = jnp.where(moment, dot(factors[...], phi[...], NN), tints_ref[...])
        where = [idx_ref[pl.ds(t * groups + q, 1), :] for q in range(groups)]
        words = []
        for q, idx in enumerate(where):
            if q % 4 == 0:
                words.append(jnp.zeros((1, LANES), jnp.int32))
            words[-1] = words[-1] | jnp.left_shift(jnp.where(idx < 0, 255, jnp.right_shift(idx, 8)), 8 * (q % 4))
        words = jnp.transpose(jnp.concatenate(words + [words[0]] * (SUB - len(words)), axis=0))
        for q in range(groups):
            at = slice(q * LANES, (q + 1) * LANES)
            if q % 4 == 0:
                word = jnp.broadcast_to(words[:, q // 4 : q // 4 + 1], (LANES, LANES))
            mine = word & jnp.left_shift(jnp.full((LANES, LANES), 255, jnp.int32), 8 * (q % 4))
            for base in range(0, columns, LANES):
                kept = jnp.where(mine == jnp.left_shift(block + base // BLOCK, 8 * (q % 4)), got[at], 0.0)
                top, rest = pieces(kept, 2)
                split[at, base : base + LANES] = top
                split[at, columns + base : columns + base + LANES] = rest

    def scatter(t, factors, tints_ref, split):
        where = jnp.concatenate([idx_ref[pl.ds(t * groups + q, 1), :] for q in range(groups)], axis=1)
        low = jnp.bitwise_and(where, wide - 1)
        hot = (jnp.broadcast_to(low, (wide, count)) == rows_of((wide, count))).astype(F32).astype(BF16)
        total[...] += dot(hot, split[...], NN)

    par = len(buffers) // each

    def body(i, carry):
        for k in range(par):
            now = buffers[each * k : each * (k + 1)]
            last = buffers[each * ((k - 1) % par) :][:each]
            t = i * par + k
            sums(jnp.maximum(t - 1, 0), *last)
            sweep(t, *now)
            scatter(jnp.maximum(t - 1, 0), *last)
        return carry

    buffers[each * (par - 1)][...] = jnp.zeros((count, 2 * pixels), BF16)
    buffers[each * (par - 1) + 1][...] = jnp.zeros((count, LANES), F32)
    lax.fori_loop(0, tiles // par, body, 0)
    sums(tiles - 1, *buffers[each * (par - 1) :])
    scatter(tiles - 1, *buffers[each * (par - 1) :])
    half = LANES // 2
    left = lanes_of((SUB, LANES)) < half
    for c in range(columns // BLOCK):
        if c % SUB == 0:
            at = c // SUB * LANES
            both = total[:, at : at + LANES] + total[:, columns + at : columns + at + LANES]
            turned = jnp.concatenate([jnp.transpose(both[:LANES]), jnp.transpose(both[LANES:])], axis=1)
        got = turned[c % SUB * BLOCK : (c % SUB + 1) * BLOCK]
        eight, ninth = got[:SUB], got[SUB : SUB + 1]
        for j in range(2):
            e = eight[:, j * LANES : (j + 1) * LANES]
            n = jnp.broadcast_to(ninth[:, j * LANES : (j + 1) * LANES], (SUB, LANES))
            at = (c * 2 + j) * 2 * SUB
            out_ref[at : at + SUB] = jnp.where(left, e, pltpu.roll(n, half, 1))
            out_ref[at + SUB : at + 2 * SUB] = jnp.where(left, pltpu.roll(e, half, 1), n)


def home_kernel(recv, rows_ref, centres, conic, rho, opacity, out_ref, total):
    half = LANES // 2
    left = lanes_of((SUB, LANES)) < half
    total[...] = jnp.zeros_like(total)
    step = 8
    for g in range(0, rows_ref.shape[1] // LANES, step):
        eights, ninths = [], []
        for k in range(g, g + step):
            a = recv[2 * k * SUB : (2 * k + 1) * SUB]
            b = recv[(2 * k + 1) * SUB : (2 * k + 2) * SUB]
            eights.append(jnp.where(left, a, pltpu.roll(b, half, 1)))
            n = jnp.where(left, pltpu.roll(a, half, 1), b)
            ninths.append(jnp.broadcast_to(n[0:1], (SUB, LANES)))
        values = jnp.concatenate([jnp.concatenate(eights, axis=1), jnp.concatenate(ninths, axis=1)], axis=0)
        spread(values, rows_ref[0:1, g * LANES : (g + step) * LANES], total)
    wide = total.shape[1]
    for c in range(total.shape[0] // 32):
        m, col2 = nine(total, c)
        at = slice(c * wide, (c + 1) * wide)
        x, y = centres[0:1, at], centres[1:2, at]
        a, d = conic[0:1, at], conic[1:2, at]
        root = jnp.sqrt(a * d)
        b = rho[0:1, at] * root
        m1, mu, mv, muu, muv, mvv = [m[i : i + 1] for i in range(6)]
        dx, dy = mu - x * m1, mv - y * m1
        dxx = muu - 2.0 * x * mu + x * x * m1
        dxy = muv - x * mv - y * mu + x * y * m1
        dyy = mvv - 2.0 * y * mv + y * y * m1
        rows = [
            a * dx + b * dy,
            b * dx + d * dy,
            -0.5 * (dxx + b / a * dxy),
            -0.5 * (dyy + b / d * dxy),
            -root * dxy,
            m1 / opacity[0:1, at],
            m[6:7],
            m[7:8],
            col2,
        ]
        for i, v in enumerate(rows):
            out_ref[i : i + 1, at] = v


def back_scratch(list_len, pixels, slots, par):
    columns = slots // (2 * LANES) * BLOCK
    one = [
        pltpu.VMEM((list_len, 2 * pixels), BF16),
        pltpu.VMEM((list_len, LANES), F32),
        pltpu.VMEM((list_len, 2 * columns), BF16),
    ]
    return [pltpu.VMEM((2 * LANES, 2 * columns), F32), pltpu.VMEM((2 * pixels, LANES), BF16)] + one * par


def call(kernel, out_shape, scratch=(), smem=0, mib=48):
    n_vmem = pl.BlockSpec()

    def run(*args):
        specs = [pl.BlockSpec(memory_space=pltpu.SMEM) if i < smem else n_vmem for i in range(len(args))]
        return pl.pallas_call(
            kernel,
            out_shape=out_shape,
            in_specs=specs,
            out_specs=jax.tree.map(lambda _: n_vmem, out_shape),
            scratch_shapes=list(scratch),
            compiler_params=pltpu.CompilerParams(vmem_limit_bytes=mib * 1024 * 1024),
        )(*args)

    return run


def swap_edges(value):
    size = lax.axis_size("dev")
    me = lax.axis_index("dev")
    first, last = value[:, :HALO], value[:, -HALO:]
    odd = (me % 2) == 1
    inner = [(i, i ^ 1) for i in range(size)]
    outer = [(i, i + 1) for i in range(1, size - 1, 2)]
    outer = outer + [(j, i) for i, j in outer]
    got_in = lax.ppermute(jnp.where(odd, first, last), "dev", inner)
    got_out = lax.ppermute(jnp.where(odd, last, first), "dev", outer)
    return jnp.where(odd, got_in, got_out), jnp.where(odd, got_out, got_in)


def shards(tile_lists, send_rows, centres, conic, rho, opacity, colors, target):
    slot_count = send_rows.shape[1]
    owned_count = centres.shape[1]
    channels, tile, width = target.shape
    strip_tiles, list_len = tile_lists.shape
    size = lax.axis_size("dev")
    me = lax.axis_index("dev")
    pixels = tile * tile
    wide = 2 * LANES
    sds = jax.ShapeDtypeStruct

    packed = call(
        pack_kernel,
        sds((size * SUB, LANES), F32),
        [pltpu.VMEM((owned_count // wide * 32, wide), BF16)],
        mib=63,
    )(send_rows, centres, conic, rho, opacity, colors)
    received = lax.all_to_all(packed, "dev", split_axis=0, concat_axis=0, tiled=True)

    order = tile_lists.reshape(strip_tiles, SUB, list_len // SUB).transpose(0, 2, 1)
    order = order.reshape(strip_tiles * list_len // LANES, LANES)
    tar_b, tar_a = swap_edges(target)
    rows_back, cols = blur_tables(tile, width)
    tall = rows_back.shape[0] // 3 - tile
    known = call(target_kernel, sds((2 * channels, tall, width), F32))(target, tar_b, tar_a, rows_back, cols)

    colour_tiles, coefs, segments = call(
        forward_kernel,
        (
            sds((strip_tiles, channels, pixels), F32),
            sds((strip_tiles, 32, list_len), BF16),
            sds((strip_tiles, 4 * SUB, pixels), F32),
        ),
        [pltpu.VMEM((slot_count // wide * 32, wide), BF16), pltpu.VMEM((32, pixels + 3 * LANES), BF16)],
    )(received, order)
    image = (
        colour_tiles.reshape(strip_tiles, channels, tile, tile).transpose(1, 2, 0, 3).reshape(channels, tile, width)
    )
    ren_b, ren_a = swap_edges(image)
    edge = jnp.stack([jnp.where(me == 0, RIM, 0), jnp.where(me == size - 1, tile + RIM, tile + HALO)]).astype(jnp.int32)
    cot = call(ssim_kernel, sds((channels, tile, width), F32), smem=1)(
        edge, image, target, ren_b, tar_b, ren_a, tar_a, known, rows_back, cols
    )
    cot_tiles = (
        cot.reshape(channels, tile, strip_tiles, tile).transpose(2, 0, 1, 3).reshape(strip_tiles, channels, pixels)
    )
    slot_sums = call(
        backward_kernel,
        sds((size * SUB, LANES), F32),
        back_scratch(list_len, pixels, slot_count, part_of(strip_tiles, 8)),
    )(coefs, order, segments, cot_tiles)
    returned = lax.all_to_all(slot_sums, "dev", split_axis=0, concat_axis=0, tiled=True)
    grads = call(
        home_kernel,
        sds((9, owned_count), F32),
        [pltpu.VMEM((owned_count // wide * 32, wide), F32)],
    )(returned, send_rows, centres, conic, rho, opacity)
    return (image, grads)


def solution(mesh):
    return jax.shard_map(
        shards,
        mesh=mesh,
        in_specs=(
            P("dev", None),
            P("dev", None),
            P(None, "dev"),
            P(None, "dev"),
            P(None, "dev"),
            P(None, "dev"),
            P(None, "dev"),
            P(None, "dev", None),
        ),
        out_specs=(P(None, "dev", None), P(None, "dev")),
        check_vma=False,
    )
```

```python
import functools

import jax
import jax.numpy as jnp
import numpy as np
from jax import lax
from jax.experimental import pallas as pl
from jax.experimental.pallas import tpu as pltpu
from jax.sharding import PartitionSpec as P

LANES = 128
SUB = 8
RIM = 5
HALO = 2 * RIM
BLOCK = 16
LOG2E = 1.4426950408889634
F32 = jnp.float32
BF16 = jnp.bfloat16
NN = (((1,), (0,)), ((), ()))
NT = (((1,), (1,)), ((), ()))
TN = (((0,), (0,)), ((), ()))


def dot(a, b, dims):
    return lax.dot_general(a, b, dims, preferred_element_type=F32)


def pieces(x, count):
    out = []
    for _ in range(count - 1):
        top = x.astype(BF16)
        out.append(top)
        x = x - top.astype(F32)
    out.append(x.astype(BF16))
    return out


def lanes_of(shape):
    return lax.broadcasted_iota(jnp.int32, shape, len(shape) - 1)


def rows_of(shape):
    return lax.broadcasted_iota(jnp.int32, shape, len(shape) - 2)


def fill(table, c, eight, ninth):
    p = [v.astype(F32) for v in pieces(eight, 3)]
    n = [v.astype(F32) for v in pieces(jnp.broadcast_to(ninth, eight.shape), 3)]
    r = rows_of(eight.shape)
    tail = jnp.where(r == 0, n[0], jnp.where(r == 1, n[1], jnp.where(r == 2, n[2], 0.0)))
    table[c * 32 : (c + 1) * 32] = jnp.concatenate(p + [tail], axis=0).astype(BF16)


def choose(table, idx, none):
    wide = table.shape[1]
    low = jnp.broadcast_to(jnp.bitwise_and(idx, wide - 1), (wide, wide))
    hot = (low == rows_of((wide, wide))).astype(F32).astype(BF16)
    got = dot(table[...], hot, NN)
    chunk = jnp.where(idx < 0, -1, jnp.right_shift(idx, wide.bit_length() - 1))
    chunk = jnp.broadcast_to(chunk, (32, wide))
    x = none
    for c in range(table.shape[0] // 32):
        x = jnp.where(chunk == c, got[c * 32 : (c + 1) * 32], x)
    return x


def pack_kernel(rows_ref, centres, conic, rho, opacity, colors, out_ref, table):
    wide = table.shape[1]
    s = -0.5 * LOG2E
    for c in range(table.shape[0] // 32):
        at = slice(c * wide, (c + 1) * wide)
        x, y = centres[0:1, at], centres[1:2, at]
        a, d = conic[0:1, at], conic[1:2, at]
        b = rho[0:1, at] * jnp.sqrt(a * d)
        rows = [
            jnp.log(opacity[0:1, at]) * LOG2E + s * (a * x * x + 2.0 * b * x * y + d * y * y),
            -2.0 * s * (a * x + b * y),
            -2.0 * s * (d * y + b * x),
            s * a,
            2.0 * s * b,
            s * d,
            colors[0:1, at],
            colors[1:2, at],
        ]
        fill(table, c, jnp.concatenate(rows, axis=0), colors[2:3, at])
    half = LANES // 2
    left = lanes_of((SUB, LANES)) < half
    none = jnp.zeros((32, wide), F32)
    for g in range(rows_ref.shape[1] // wide):
        x = choose(table, rows_ref[0:1, g * wide : (g + 1) * wide], none)
        eight = x[0:SUB] + x[SUB : 2 * SUB] + x[2 * SUB : 3 * SUB]
        ninth = jnp.broadcast_to(x[24:25] + x[25:26] + x[26:27], (SUB, wide))
        for j in range(wide // LANES):
            e, n = [v[:, j * LANES : (j + 1) * LANES] for v in (eight, ninth)]
            at = (g * (wide // LANES) + j) * 2 * SUB
            out_ref[at : at + SUB] = jnp.where(left, e, pltpu.roll(n, half, 1))
            out_ref[at + SUB : at + 2 * SUB] = jnp.where(left, pltpu.roll(e, half, 1), n)


def part_of(count, most):
    return max(d for d in range(1, most + 1) if count % d == 0)


def shifted(x, by):
    return pltpu.roll(x, by % SUB, 0)


def six_of(kind, spot, side):
    down = jnp.right_shift(spot, side.bit_length() - 1)
    u = (spot - down * side).astype(F32) - (side - 1) / 2.0
    v = down.astype(F32) - (side - 1) / 2.0
    six = jnp.zeros(kind.shape, F32)
    for i, f in enumerate((jnp.ones_like(u), u, v, u * u, u * v, v * v)):
        six = jnp.where(kind == i, f, six)
    return six


def terms(pixels):
    r = rows_of((32, pixels))
    kind = jnp.where(r < 24, jnp.bitwise_and(r, SUB - 1), SUB)
    return six_of(kind, lanes_of((32, pixels)), int(pixels**0.5))


def forward_kernel(recv, idx_ref, img_ref, x_ref, seg_ref, table, basis):
    tiles, pixels = img_ref.shape[0], img_ref.shape[2]
    groups = x_ref.shape[2] // LANES
    wide = table.shape[1]
    half = LANES // 2
    left = lanes_of((SUB, LANES)) < half
    for c in range(table.shape[0] // 32):
        eights, ninths = [], []
        for j in range(wide // LANES):
            at = (c * (wide // LANES) + j) * 2 * SUB
            a, b = recv[at : at + SUB], recv[at + SUB : at + 2 * SUB]
            eights.append(jnp.where(left, a, pltpu.roll(b, half, 1)))
            n = jnp.where(left, pltpu.roll(a, half, 1), b)
            ninths.append(n[0:1])
        fill(table, c, jnp.concatenate(eights, axis=1), jnp.concatenate(ninths, axis=1))
    none = jnp.where(rows_of((32, wide)) == 0, -1000.0, 0.0)
    basis[:, :pixels] = terms(pixels).astype(BF16)
    r = rows_of((32, LANES))
    for ch in range(3):
        spread_it = jnp.logical_and(r < 24, jnp.bitwise_and(r, SUB - 1) == 6 + ch) if ch < 2 else jnp.logical_and(r >= 24, r < 27)
        basis[:, pixels + ch * LANES : pixels + (ch + 1) * LANES] = jnp.where(spread_it, 1.0, 0.0).astype(BF16)
    row = rows_of((SUB, pixels))

    def fetch(t):
        per = wide // LANES
        for q in range(0, groups, per):
            idx = jnp.concatenate([idx_ref[pl.ds(t * groups + q + j, 1), :] for j in range(per)], axis=1)
            x = choose(table, idx, none)
            x_ref[t, :, q * LANES : (q + per) * LANES] = x.astype(BF16)

    def composite(t):
        trans = jnp.ones((SUB, pixels), F32)
        acc = [jnp.zeros((SUB, pixels), F32) for _ in range(3)]
        for q in range(groups):
            out = dot(x_ref[t, :, q * LANES : (q + 1) * LANES], basis[...], TN)
            for i in range(LANES // SUB):
                at = slice(i * SUB, (i + 1) * SUB)
                alpha = jnp.exp2(out[at, :pixels])
                w = alpha * trans
                trans = trans * (1.0 - alpha)
                for ch in range(3):
                    tint = out[at, pixels + ch * LANES : pixels + (ch + 1) * LANES]
                    acc[ch] = acc[ch] + jnp.concatenate([tint] * (pixels // LANES), axis=1) * w
        before = jnp.where(row >= 1, shifted(trans, 1), 1.0)
        for by in (1, 2, 4):
            before = before * jnp.where(row >= by, shifted(before, by), 1.0)
        seg_ref[t, 0:SUB] = before
        image = []
        for ch in range(3):
            seg_ref[t, (1 + ch) * SUB : (2 + ch) * SUB] = acc[ch]
            image.append(jnp.sum(acc[ch] * before, axis=0, keepdims=True))
        img_ref[t] = jnp.concatenate(image, axis=0)

    def body(i, carry):
        for k in range(par):
            fetch(i * par + k)
        for k in range(par):
            composite(i * par + k)
        return carry

    par = part_of(tiles, 8)
    lax.fori_loop(0, tiles // par, body, 0)


def exact(a, b):
    return sum(dot(a[i], b[j], NN) for i in range(3) for j in range(3 - i))


def blur(images, rows, cols):
    height = rows.shape[0] // 3
    done = []
    for x in images:
        got = dot(rows, jnp.concatenate(pieces(x, 3), axis=0), NN)
        done.append(got[:height] + got[height : 2 * height] + got[2 * height :])
    stacked = jnp.concatenate(done, axis=0)
    parts = pieces(stacked, 3)
    width = stacked.shape[1]
    out = []
    for low in range(0, width, 2 * LANES):
        high = min(low + 2 * LANES, width)
        first = max(low - RIM, 0) // LANES * LANES
        end = min(-(-(high + RIM) // LANES) * LANES, width)
        out.append(exact([p[:, first:end] for p in parts], [cols[k, first:end, low:high] for k in range(3)]))
    out = jnp.concatenate(out, axis=1)
    return [out[i * height : (i + 1) * height] for i in range(len(images))]


def padded(own, before, after, ch):
    fill = jnp.zeros((-HALO % SUB, own.shape[2]), F32)
    return jnp.concatenate([own[ch], before[ch], fill, after[ch], fill], axis=0)


def target_kernel(tar, tar_b, tar_a, rows_back, cols, out_ref):
    rows = rows_back[: 3 * out_ref.shape[1]]
    channels = tar.shape[0]
    images = [padded(tar, tar_b, tar_a, ch) for ch in range(channels)]
    for i, v in enumerate(blur(images + [x * x for x in images], rows, cols)):
        out_ref[i] = v


def ssim_kernel(edge, ren, tar, ren_b, tar_b, ren_a, tar_a, known, rows_back, cols, cot_ref):
    channels, height, width = ren.shape
    tall = known.shape[1]
    rows = rows_back[: 3 * tall]
    back = rows_back[3 * tall :, : 3 * tall]
    r_at = rows_of((tall, width))
    inside = jnp.logical_and(r_at >= edge[0], r_at < edge[1])
    ren_s = [padded(ren, ren_b, ren_a, ch) for ch in range(channels)]
    tar_s = [padded(tar, tar_b, tar_a, ch) for ch in range(channels)]
    found = blur(ren_s + [x * x for x in ren_s] + [x * y for x, y in zip(ren_s, tar_s)], rows, cols)
    fields = []
    for ch in range(channels):
        mr, er, ert = found[ch], found[channels + ch], found[2 * channels + ch]
        mt, et = known[ch], known[channels + ch]
        a1 = 2.0 * mr * mt + 0.0001
        a2 = 2.0 * (ert - mr * mt) + 0.0009
        b1 = mr * mr + mt * mt + 0.0001
        b2 = (er - mr * mr) + (et - mt * mt) + 0.0009
        i1, i2 = 1.0 / b1, 1.0 / b2
        s = a1 * a2 * i1 * i2
        d_mr = 2.0 * mt * (a2 - a1) * i1 * i2 - 2.0 * mr * s * (i1 - i2)
        d_er = -s * i2
        d_ert = 2.0 * a1 * i1 * i2
        fields += [jnp.where(inside, d, 0.0) for d in (d_mr, d_er, d_ert)]
    pulled = blur(fields, back, cols)
    for ch in range(channels):
        g0, g1, g2 = pulled[3 * ch : 3 * ch + 3]
        rc, tc = ren[ch], tar[ch]
        cot_ref[ch] = 1.6 * (rc - tc) - 0.2 * (g0 + 2.0 * rc * g1 + tc * g2)


def parts_of(matrix):
    out = []
    rest = matrix.astype(np.float32)
    for _ in range(3):
        top = rest.astype(jnp.bfloat16)
        out.append(top)
        rest = rest - top.astype(np.float32)
    return jnp.asarray(np.stack(out))


def blur_tables(height, width):
    m = np.arange(-RIM, RIM + 1)
    taps = np.exp(-m * m / 4.5)
    taps = taps / taps.sum()
    side = HALO + (-HALO % SUB)
    place = [height + i for i in range(HALO)] + list(range(height)) + [height + side + i for i in range(HALO)]
    mid = height + HALO
    tall = mid + (-mid % SUB)
    rows = np.zeros((tall, height + 2 * side))
    back = np.zeros((height, tall))
    cols = np.zeros((width, width))
    for k, tap in enumerate(taps):
        for i in range(mid):
            rows[i, place[i + k]] = tap
        for i in range(height):
            back[i, i + k] = tap
        for i in range(width):
            if 0 <= i + k - RIM < width:
                cols[i + k - RIM, i] = tap

    def stack(matrix):
        p = parts_of(matrix)
        none = jnp.zeros_like(p[0])
        sides = [[p[i] if i + j < 3 else none for j in range(3)] for i in range(3)]
        return jnp.concatenate([jnp.concatenate(side, axis=1) for side in sides], axis=0)

    down, up = stack(rows), stack(back)
    up = jnp.pad(up, ((0, 0), (0, down.shape[1] - up.shape[1])))
    return jnp.concatenate([down, up], axis=0), parts_of(cols)


def spread(values, where, total):
    count = where.shape[1]
    wide = total.shape[1]
    p0, p1, p2 = [p.astype(F32) for p in pieces(values, 3)]
    rows = rows_of((SUB, count))
    tail = jnp.where(rows == 0, p0[SUB:], jnp.where(rows == 1, p1[SUB:], jnp.where(rows == 2, p2[SUB:], 0.0)))
    stacked = jnp.concatenate([p0[:SUB], p1[:SUB], p2[:SUB], tail], axis=0)
    low = jnp.bitwise_and(where, wide - 1)
    high = jnp.where(where < 0, -1, jnp.right_shift(where, wide.bit_length() - 1))
    hot = (jnp.broadcast_to(low, (wide, count)) == rows_of((wide, count))).astype(F32).astype(BF16)
    parts = []
    for c in range(total.shape[0] // 32):
        parts.append(jnp.where(jnp.broadcast_to(high == c, stacked.shape), stacked, 0.0).astype(BF16))
    total[...] += dot(jnp.concatenate(parts, axis=0), hot, NT)


def nine(total, c):
    got = total[c * 32 : (c + 1) * 32]
    return (
        got[0:SUB] + got[SUB : 2 * SUB] + got[2 * SUB : 3 * SUB],
        got[24:25] + got[25:26] + got[26:27],
    )


def backward_kernel(x_ref, idx_ref, seg_ref, cot_ref, out_ref, total, phi, *buffers):
    tiles, pixels = cot_ref.shape[0], cot_ref.shape[2]
    count = x_ref.shape[2]
    groups = count // LANES
    steps = LANES // SUB
    wide = 2 * LANES
    total[...] = jnp.zeros_like(total)
    row = rows_of((SUB, pixels))
    each = 3
    columns = total.shape[1] // 2
    field = jnp.bitwise_and(lanes_of((SUB, LANES)), BLOCK - 1)
    basis = jnp.concatenate([terms(pixels), jnp.zeros((32, pixels), F32)], axis=0).astype(BF16)
    kind = jnp.bitwise_and(lanes_of((pixels, LANES)), BLOCK - 1)
    six = six_of(kind, rows_of((pixels, LANES)), int(pixels**0.5))
    phi[:pixels] = six.astype(BF16)
    phi[pixels:] = six.astype(BF16)
    moment = jnp.bitwise_and(lanes_of((count, LANES)), BLOCK - 1) < 6
    block = jnp.right_shift(lanes_of((LANES, LANES)), BLOCK.bit_length() - 1)

    def sweep(t, factors, tints_ref, split):
        cot = [jnp.broadcast_to(cot_ref[t, ch : ch + 1], (SUB, pixels)) for ch in range(3)]
        hi = [c.astype(BF16).astype(F32) for c in cot]
        lo = [c - h for c, h in zip(cot, hi)]

        def place(v):
            body = jnp.where(row == 6, v[0], jnp.where(row == 7, v[1], 0.0))
            return [body, body, body, jnp.where(row < 3, v[2], 0.0)]

        rhs = jnp.concatenate(place(hi) + place(lo), axis=0).astype(BF16)
        rhs = jnp.concatenate([basis, rhs], axis=1)
        trans = seg_ref[t, 0:SUB]
        rest = trans * (cot[0] * seg_ref[t, SUB : 2 * SUB] + cot[1] * seg_ref[t, 2 * SUB : 3 * SUB] + cot[2] * seg_ref[t, 3 * SUB : 4 * SUB])
        for by in (1, 2, 4):
            rest = rest + jnp.where(row < SUB - by, shifted(rest, -by), 0.0)
        for q in range(groups):
            x = x_ref[t, :, q * LANES : (q + 1) * LANES]
            out = dot(jnp.concatenate([x, x], axis=0), rhs, TN)
            for i in range(0, steps, 2):
                hs = []
                for j in (i, i + 1):
                    at = slice(q * LANES + j * SUB, q * LANES + (j + 1) * SUB)
                    alpha = jnp.exp2(out[j * SUB : (j + 1) * SUB, :pixels])
                    w = alpha * trans
                    clear = 1.0 - alpha
                    trans = trans * clear
                    wg = w * out[j * SUB : (j + 1) * SUB, pixels:]
                    rest = rest - wg
                    hs.append(wg - alpha * pl.reciprocal(clear, approx=True) * rest)
                    tints = [jnp.sum(w * c, axis=1, keepdims=True) for c in cot]
                    tints_ref[at] = jnp.where(field == 6, tints[0], jnp.where(field == 7, tints[1], tints[2]))
                at = slice(q * LANES + i * SUB, q * LANES + (i + 2) * SUB)
                for p, v in enumerate(pieces(jnp.concatenate(hs, axis=0), 2)):
                    factors[at, p * pixels : (p + 1) * pixels] = v

    def sums(t, factors, tints_ref, split):
        got = jnp.where(moment, dot(factors[...], phi[...], NN), tints_ref[...])
        where = [idx_ref[pl.ds(t * groups + q, 1), :] for q in range(groups)]
        words = []
        for q, idx in enumerate(where):
            if q % 4 == 0:
                words.append(jnp.zeros((1, LANES), jnp.int32))
            words[-1] = words[-1] | jnp.left_shift(jnp.where(idx < 0, 255, jnp.right_shift(idx, 8)), 8 * (q % 4))
        words = jnp.transpose(jnp.concatenate(words + [words[0]] * (SUB - len(words)), axis=0))
        for q in range(groups):
            at = slice(q * LANES, (q + 1) * LANES)
            if q % 4 == 0:
                word = jnp.broadcast_to(words[:, q // 4 : q // 4 + 1], (LANES, LANES))
            mine = word & jnp.left_shift(jnp.full((LANES, LANES), 255, jnp.int32), 8 * (q % 4))
            for base in range(0, columns, LANES):
                kept = jnp.where(mine == jnp.left_shift(block + base // BLOCK, 8 * (q % 4)), got[at], 0.0)
                top, rest = pieces(kept, 2)
                split[at, base : base + LANES] = top
                split[at, columns + base : columns + base + LANES] = rest

    def scatter(t, factors, tints_ref, split):
        where = jnp.concatenate([idx_ref[pl.ds(t * groups + q, 1), :] for q in range(groups)], axis=1)
        low = jnp.bitwise_and(where, wide - 1)
        hot = (jnp.broadcast_to(low, (wide, count)) == rows_of((wide, count))).astype(F32).astype(BF16)
        total[...] += dot(hot, split[...], NN)

    par = len(buffers) // each

    def body(i, carry):
        for k in range(par):
            now = buffers[each * k : each * (k + 1)]
            last = buffers[each * ((k - 1) % par) :][:each]
            t = i * par + k
            sums(jnp.maximum(t - 1, 0), *last)
            sweep(t, *now)
            scatter(jnp.maximum(t - 1, 0), *last)
        return carry

    buffers[each * (par - 1)][...] = jnp.zeros((count, 2 * pixels), BF16)
    buffers[each * (par - 1) + 1][...] = jnp.zeros((count, LANES), F32)
    lax.fori_loop(0, tiles // par, body, 0)
    sums(tiles - 1, *buffers[each * (par - 1) :])
    scatter(tiles - 1, *buffers[each * (par - 1) :])
    half = LANES // 2
    left = lanes_of((SUB, LANES)) < half
    for c in range(columns // BLOCK):
        if c % SUB == 0:
            at = c // SUB * LANES
            both = total[:, at : at + LANES] + total[:, columns + at : columns + at + LANES]
            turned = jnp.concatenate([jnp.transpose(both[:LANES]), jnp.transpose(both[LANES:])], axis=1)
        got = turned[c % SUB * BLOCK : (c % SUB + 1) * BLOCK]
        eight, ninth = got[:SUB], got[SUB : SUB + 1]
        for j in range(2):
            e = eight[:, j * LANES : (j + 1) * LANES]
            n = jnp.broadcast_to(ninth[:, j * LANES : (j + 1) * LANES], (SUB, LANES))
            at = (c * 2 + j) * 2 * SUB
            out_ref[at : at + SUB] = jnp.where(left, e, pltpu.roll(n, half, 1))
            out_ref[at + SUB : at + 2 * SUB] = jnp.where(left, pltpu.roll(e, half, 1), n)


def home_kernel(recv, rows_ref, centres, conic, rho, opacity, out_ref, total):
    half = LANES // 2
    left = lanes_of((SUB, LANES)) < half
    total[...] = jnp.zeros_like(total)
    step = 8
    for g in range(0, rows_ref.shape[1] // LANES, step):
        eights, ninths = [], []
        for k in range(g, g + step):
            a = recv[2 * k * SUB : (2 * k + 1) * SUB]
            b = recv[(2 * k + 1) * SUB : (2 * k + 2) * SUB]
            eights.append(jnp.where(left, a, pltpu.roll(b, half, 1)))
            n = jnp.where(left, pltpu.roll(a, half, 1), b)
            ninths.append(jnp.broadcast_to(n[0:1], (SUB, LANES)))
        values = jnp.concatenate([jnp.concatenate(eights, axis=1), jnp.concatenate(ninths, axis=1)], axis=0)
        spread(values, rows_ref[0:1, g * LANES : (g + step) * LANES], total)
    wide = total.shape[1]
    for c in range(total.shape[0] // 32):
        m, col2 = nine(total, c)
        at = slice(c * wide, (c + 1) * wide)
        x, y = centres[0:1, at], centres[1:2, at]
        a, d = conic[0:1, at], conic[1:2, at]
        root = jnp.sqrt(a * d)
        b = rho[0:1, at] * root
        m1, mu, mv, muu, muv, mvv = [m[i : i + 1] for i in range(6)]
        dx, dy = mu - x * m1, mv - y * m1
        dxx = muu - 2.0 * x * mu + x * x * m1
        dxy = muv - x * mv - y * mu + x * y * m1
        dyy = mvv - 2.0 * y * mv + y * y * m1
        rows = [
            a * dx + b * dy,
            b * dx + d * dy,
            -0.5 * (dxx + b / a * dxy),
            -0.5 * (dyy + b / d * dxy),
            -root * dxy,
            m1 / opacity[0:1, at],
            m[6:7],
            m[7:8],
            col2,
        ]
        for i, v in enumerate(rows):
            out_ref[i : i + 1, at] = v


def back_scratch(list_len, pixels, slots, par):
    columns = slots // (2 * LANES) * BLOCK
    one = [
        pltpu.VMEM((list_len, 2 * pixels), BF16),
        pltpu.VMEM((list_len, LANES), F32),
        pltpu.VMEM((list_len, 2 * columns), BF16),
    ]
    return [pltpu.VMEM((2 * LANES, 2 * columns), F32), pltpu.VMEM((2 * pixels, LANES), BF16)] + one * par


def call(kernel, out_shape, scratch=(), smem=0, mib=48):
    n_vmem = pl.BlockSpec()

    def run(*args):
        specs = [pl.BlockSpec(memory_space=pltpu.SMEM) if i < smem else n_vmem for i in range(len(args))]
        return pl.pallas_call(
            kernel,
            out_shape=out_shape,
            in_specs=specs,
            out_specs=jax.tree.map(lambda _: n_vmem, out_shape),
            scratch_shapes=list(scratch),
            compiler_params=pltpu.CompilerParams(vmem_limit_bytes=mib * 1024 * 1024),
        )(*args)

    return run


def swap_edges(value):
    size = lax.axis_size("dev")
    me = lax.axis_index("dev")
    first, last = value[:, :HALO], value[:, -HALO:]
    odd = (me % 2) == 1
    inner = [(i, i ^ 1) for i in range(size)]
    outer = [(i, i + 1) for i in range(1, size - 1, 2)]
    outer = outer + [(j, i) for i, j in outer]
    got_in = lax.ppermute(jnp.where(odd, first, last), "dev", inner)
    got_out = lax.ppermute(jnp.where(odd, last, first), "dev", outer)
    return jnp.where(odd, got_in, got_out), jnp.where(odd, got_out, got_in)


def shards(tile_lists, send_rows, centres, conic, rho, opacity, colors, target):
    slot_count = send_rows.shape[1]
    owned_count = centres.shape[1]
    channels, tile, width = target.shape
    strip_tiles, list_len = tile_lists.shape
    size = lax.axis_size("dev")
    me = lax.axis_index("dev")
    pixels = tile * tile
    wide = 2 * LANES
    sds = jax.ShapeDtypeStruct

    packed = call(
        pack_kernel,
        sds((size * SUB, LANES), F32),
        [pltpu.VMEM((owned_count // wide * 32, wide), BF16)],
        mib=63,
    )(send_rows, centres, conic, rho, opacity, colors)
    received = lax.all_to_all(packed, "dev", split_axis=0, concat_axis=0, tiled=True)

    order = tile_lists.reshape(strip_tiles, SUB, list_len // SUB).transpose(0, 2, 1)
    order = order.reshape(strip_tiles * list_len // LANES, LANES)
    tar_b, tar_a = swap_edges(target)
    rows_back, cols = blur_tables(tile, width)
    tall = rows_back.shape[0] // 3 - tile
    known = call(target_kernel, sds((2 * channels, tall, width), F32))(target, tar_b, tar_a, rows_back, cols)

    colour_tiles, coefs, segments = call(
        forward_kernel,
        (
            sds((strip_tiles, channels, pixels), F32),
            sds((strip_tiles, 32, list_len), BF16),
            sds((strip_tiles, 4 * SUB, pixels), F32),
        ),
        [pltpu.VMEM((slot_count // wide * 32, wide), BF16), pltpu.VMEM((32, pixels + 3 * LANES), BF16)],
    )(received, order)
    image = (
        colour_tiles.reshape(strip_tiles, channels, tile, tile).transpose(1, 2, 0, 3).reshape(channels, tile, width)
    )
    ren_b, ren_a = swap_edges(image)
    edge = jnp.stack([jnp.where(me == 0, RIM, 0), jnp.where(me == size - 1, tile + RIM, tile + HALO)]).astype(jnp.int32)
    cot = call(ssim_kernel, sds((channels, tile, width), F32), smem=1)(
        edge, image, target, ren_b, tar_b, ren_a, tar_a, known, rows_back, cols
    )
    cot_tiles = (
        cot.reshape(channels, tile, strip_tiles, tile).transpose(2, 0, 1, 3).reshape(strip_tiles, channels, pixels)
    )
    slot_sums = call(
        backward_kernel,
        sds((size * SUB, LANES), F32),
        back_scratch(list_len, pixels, slot_count, part_of(strip_tiles, 12)),
    )(coefs, order, segments, cot_tiles)
    returned = lax.all_to_all(slot_sums, "dev", split_axis=0, concat_axis=0, tiled=True)
    grads = call(
        home_kernel,
        sds((9, owned_count), F32),
        [pltpu.VMEM((owned_count // wide * 32, wide), F32)],
    )(returned, send_rows, centres, conic, rho, opacity)
    return (image, grads)


def solution(mesh):
    return jax.shard_map(
        shards,
        mesh=mesh,
        in_specs=(
            P("dev", None),
            P("dev", None),
            P(None, "dev"),
            P(None, "dev"),
            P(None, "dev"),
            P(None, "dev"),
            P(None, "dev"),
            P(None, "dev", None),
        ),
        out_specs=(P(None, "dev", None), P(None, "dev")),
        check_vma=False,
    )
```
